32 devices in a mesh: groups: 2 (over x), expert: 16 (over z, y, core).
Axes of the slice: x: 2, y: 2, z: 4, core: 2. Of those that a mesh axis runs over, the one named last changes fastest.
Arguments:
- tokens: bfloat16 [4096, 4096], P(('groups', 'expert')), parts along dimension 0, may hold values from -6 to 6
- routes: int32 [4096, 4], P(('groups', 'expert')), parts along dimension 0, may hold values from 0 to 7, all different within a row; in each aligned block of 128 rows (0 to 127, 128 to 255, ...) at most 64 rows name the same one
- route_weights: float32 [4096, 4], P(('groups', 'expert')), parts along dimension 0, may hold values from 0.1 to 1
- gate_weight: bfloat16 [4096, 7168], P(None, 'expert'), may hold values from -0.09375 to 0.09375
- up_weight: bfloat16 [4096, 7168], P(None, 'expert'), may hold values from -0.09375 to 0.09375
- down_weight: bfloat16 [896, 32768], P(None, 'expert'), may hold values from -0.1875 to 0.1875
Outputs:
- mixed: bfloat16 [4096, 4096], P(('groups', 'expert')), parts along dimension 0
The draws below stay inside these ranges and needn't reach their ends.
There are 2 independent parts, one for each index of `groups`. The reference program is written for one: setup_inputs(seed, part) draws one part's arguments, and reference() takes and returns one part's arrays. A program takes and returns all parts, laid end to end along the dimension named above; an argument that names none is the same for every part. Nothing has to cross between parts.
Inputs may be any that keep to these rules, and one draw needn't show every extreme that they name: `routes`: each row names 4 different experts; in each aligned block of 128 rows (the rows of one device) every expert is named by exactly 64 rows.
All inputs are finite; a program needn't handle non-finite values.
Results may differ from the reference program's by a relative error of at most 0.008.
Values may be sent and summed in bfloat16 or wider, within the bound.
No kernel may reach another device: no remote copies, remote signals or barrier semaphores. Data moves between devices by JAX's collectives and lax.ppermute only.
A program may use at most 128 MiB of HBM per device.

```python
import math
import jax
import jax.numpy as jnp
import numpy as np
from jax import lax

D = 4096
FF = 896
TOP = 4
TOK_DEV = 128
EXPERTS = 8
CAP = 64
TOKENS = 2048


def block_scale(own_key, shape, pieces, least, high):
    def one(position, shards_of):
        draws = jax.random.uniform(jax.random.fold_in(jax.random.fold_in(own_key, 6), position), (shards_of,), jnp.float32, least / len(pieces), high / len(pieces))
        return jnp.repeat(jnp.exp(draws), shape[position] // shards_of).reshape((-1,) + (1,) * (len(shape) - position - 1))

    level = one(*pieces[0])
    for cut in pieces[1:]:
        level = level * one(*cut)
    return level


def shared_out(key, own, number, rows, count, top, limit, slope):
    ranking = jax.random.permutation(key, count)
    crowded, usual = portions_of(count, rows * top, limit, slope, True), portions_of(count, rows * top, limit, slope, False)
    places = jnp.arange(count)

    def named(lengths, turn):
        used = int((lengths > 0).sum())
        fixed = max(1, used // 4)
        passed = fixed + (places - fixed + turn * (used - fixed)) % max(1, count - fixed)
        return jnp.zeros((count,), jnp.int32).at[ranking[jnp.where(places < fixed, places, passed)]].set(jnp.asarray(lengths, jnp.int32))

    lengths = jnp.where(number % 4 == 0, named(crowded, number // 4), named(usual, number - number // 4 - 1))
    mixed = jax.random.permutation(jax.random.fold_in(own, 3), count)
    giver, receiver = mixed[0:count // 2 * 2:2], mixed[1:count // 2 * 2:2]
    room = jnp.minimum(lengths[giver] - 1, limit - lengths[receiver]) // 2
    room = jnp.where((giver == ranking[0]) | (receiver == ranking[0]) | (lengths[receiver] == 0), 0, jnp.maximum(room, 0))
    passed = jax.random.randint(jax.random.fold_in(own, 4), (count // 2,), 0, 1 << 20) % (room + 1)
    lengths = lengths.at[giver].add(-passed).at[receiver].add(passed)
    members = jnp.searchsorted(jnp.cumsum(lengths), jnp.arange(rows * top), side="right").astype(jnp.int32)
    grid = members.reshape(top, rows).T
    grid = grid[jax.random.permutation(jax.random.fold_in(own, 1), rows)]
    turn = jax.random.randint(jax.random.fold_in(own, 2), (rows, 1), 0, top)
    return jnp.take_along_axis(grid, (jnp.arange(top)[None, :] + turn) % top, axis=1)


def portions_of(count, total, most, lean, full):
    weights = [(1 << 20) // math.isqrt(standing ** lean) + 1 for standing in range(1, count + 1)]
    largest = most if full else min(most, max(-(-total // count), total * weights[0] // sum(weights)))
    least = 1 if total - largest >= count - 1 else 0
    counts, rest = [largest] + [least] * (count - 1), total - largest - least * (count - 1)
    while rest > 0:
        candidates = [i for i in range(1, count) if counts[i] < largest] or [i for i in range(1, count) if counts[i] < most]
        pool, left = sum([weights[i] for i in candidates]), rest
        for i in candidates:
            more = min(most - counts[i], max(1, left * weights[i] // pool), rest)
            counts[i] = counts[i] + more
            rest = rest - more
    return np.array(counts)


def gaussian(own_key, extent, deviation, limit, cuts=(), kind=jnp.bfloat16):
    drawn = deviation * jax.random.normal(own_key, extent, jnp.float32)
    if cuts:
        drawn = drawn * block_scale(own_key, extent, cuts, -0.22, 0.18)
    return jnp.clip(drawn, -limit, limit).astype(kind)


def setup_inputs(seed: int = 0, part: int = 0) -> dict:
    seeds = jax.random.split(jax.random.key(seed), 7)
    part_keys = jax.random.split(jax.random.fold_in(seeds[6], part), 7)
    tokens = gaussian(part_keys[0], (TOKENS, D), 1.0, 6.0, ((0, 16),))
    routes_keys = jax.random.split(jax.random.fold_in(part_keys[1], 1), TOKENS // TOK_DEV)
    routes_turns = jax.random.permutation(jax.random.fold_in(part_keys[1], 3), TOKENS // TOK_DEV)
    routes = jax.vmap(lambda own, number: shared_out(jax.random.fold_in(part_keys[1], 2), own, number, TOK_DEV, EXPERTS, TOP, CAP, 0))(routes_keys, routes_turns).reshape((TOKENS, TOP))
    route_weights = jnp.clip(0.1 + 0.9 * jax.random.uniform(part_keys[2], (TOKENS, TOP), jnp.float32) ** block_scale(part_keys[2], (TOKENS, TOP), ((0, 16),), -0.2, 0.2), 0.1, 1.0)
    gate_weight = gaussian(seeds[3], (D, EXPERTS * FF), D ** -0.5, 0.09375, ((1, 16),))
    up_weight = gaussian(seeds[4], (D, EXPERTS * FF), D ** -0.5, 0.09375, ((1, 16),))
    down_weight = gaussian(seeds[5], (FF, EXPERTS * D), FF ** -0.5, 0.1875, ((1, 16),))
    return dict(tokens=tokens, routes=routes, route_weights=route_weights, gate_weight=gate_weight, up_weight=up_weight, down_weight=down_weight)


def reference(tokens, routes, route_weights, gate_weight, up_weight, down_weight):
    flat = routes.reshape(-1)
    total = flat.shape[0]
    order = jnp.argsort(flat, stable=True).astype(jnp.int32)
    owner = order // TOP
    per_expert = total // EXPERTS
    rows = tokens[owner].reshape(EXPERTS, per_expert, D)

    def one_expert(args):
        block, index = args
        g_cols = lax.dynamic_slice_in_dim(gate_weight, index * FF, FF, 1)
        u_cols = lax.dynamic_slice_in_dim(up_weight, index * FF, FF, 1)
        d_cols = lax.dynamic_slice_in_dim(down_weight, index * D, D, 1)
        gate = jnp.dot(block, g_cols, preferred_element_type=jnp.float32)
        upval = jnp.dot(block, u_cols, preferred_element_type=jnp.float32)
        hidden = (jax.nn.silu(gate) * upval).astype(jnp.bfloat16)
        return jnp.dot(hidden, d_cols, preferred_element_type=jnp.float32).astype(jnp.bfloat16)

    outputs = lax.map(one_expert, (rows, jnp.arange(EXPERTS, dtype=jnp.int32)))
    placed = jnp.zeros((total, D), jnp.bfloat16).at[order].set(outputs.reshape(total, D))
    placed = placed.reshape(TOKENS, TOP, D).astype(jnp.float32)
    mixed = jnp.sum(route_weights[:, :, None] * placed, axis=1)
    return mixed.astype(jnp.bfloat16)
```

```python
import jax
import jax.numpy as jnp
from jax import lax
from jax.sharding import PartitionSpec as P

CHUNKS = 1


def swapped(x, axis, apart):
    return lax.ppermute(x, axis, [(i, i ^ 1 << apart) for i in range(lax.axis_size(axis))])


def dot32(a, b):
    return jnp.dot(a, b, preferred_element_type=jnp.float32)


def expert_hidden(rows, gate_part, up_part, parity):
    gate = dot32(rows, gate_part)
    upval = dot32(rows, up_part)
    hidden = (jax.nn.silu(gate) * upval).astype(jnp.bfloat16)
    partner = swapped(hidden, "expert", 0)
    return jnp.where(
        parity == 0, jnp.concatenate([hidden, partner], 1), jnp.concatenate([partner, hidden], 1)
    )


def dispatched(tokens, routes, route_weights, gate_weight, up_weight, down_weight):
    tok_rows, top_count = routes.shape
    width = tokens.shape[1]
    half_width = down_weight.shape[1]
    devices = lax.axis_size("expert")
    experts = devices // 2
    capacity = tok_rows * top_count // experts
    parity = lax.axis_index("expert") % 2
    flat = routes.reshape(-1)
    onehot = (flat[:, None] == jnp.arange(experts, dtype=jnp.int32)[None, :]).astype(jnp.int32)
    before = jnp.cumsum(onehot, axis=0) - onehot
    slot_of = jnp.sum(before * onehot, axis=1)
    position = flat * capacity + slot_of
    assign_ids = jnp.arange(flat.shape[0], dtype=jnp.int32) // top_count
    owner = jnp.zeros((experts * capacity,), jnp.int32).at[position].set(assign_ids)
    gathered = tokens[owner]
    outgoing = jnp.broadcast_to(
        gathered.reshape(experts, 1, capacity, width), (experts, 2, capacity, width)
    )
    outgoing = outgoing.reshape(devices, capacity, width)
    received = lax.all_to_all(outgoing, "expert", split_axis=0, concat_axis=0, tiled=True)
    count, items, _ = received.shape
    hidden = expert_hidden(received.reshape(count * items, width), gate_weight, up_weight, parity)
    produced = dot32(hidden, down_weight).astype(jnp.bfloat16)
    returned = lax.all_to_all(
        produced.reshape(count, items, half_width),
        "expert",
        split_axis=0,
        concat_axis=0,
        tiled=True,
    )
    returned = returned.reshape(experts, 2, capacity, half_width).transpose(0, 2, 1, 3)
    expert_rows = returned.reshape(experts * capacity, width)
    picked = expert_rows[position].reshape(tok_rows, top_count, width)
    mixed = jnp.einsum("tk,tkd->td", route_weights, picked.astype(jnp.float32))
    return mixed.astype(jnp.bfloat16)


def along_line(x, pairs):
    moves = [((a * 2 + s) * 2 + c, (b * 2 + s) * 2 + c) for a, b in pairs for s in (0, 1) for c in (0, 1)]
    return lax.ppermute(x, "expert", moves)


def exchange_outer(x):
    return along_line(x, [(0, 1), (1, 0), (2, 3), (3, 2)])


def exchange_middle(x):
    return along_line(x, [(1, 2), (2, 1)])


def move_out(x):
    return along_line(x, [(1, 0), (2, 3)])


def move_in(x):
    return along_line(x, [(0, 1), (3, 2)])


def lined(tokens, routes, route_weights, gate_weight, up_weight, down_weight):
    tok_rows, top_count = routes.shape
    devices = lax.axis_size("expert")
    experts = devices // 2
    capacity = tok_rows * top_count // experts
    index = lax.axis_index("expert")
    core, side, line = index % 2, index // 2 % 2, index // 4
    inner = (line == 1) | (line == 2)
    bf16, f32 = jnp.bfloat16, jnp.float32
    rows = tok_rows // CHUNKS
    slots = capacity

    gate_other = swapped(gate_weight, "expert", 0)
    up_other = swapped(up_weight, "expert", 0)
    down_full = jnp.concatenate([down_weight, swapped(down_weight, "expert", 0)], 1)

    def hidden_of(x, scale):
        def half(g, u):
            return (jax.nn.silu(dot32(x, g)) * dot32(x, u) * scale[:, None]).astype(bf16)

        own, other = half(gate_weight, up_weight), half(gate_other, up_other)
        return jnp.where(core == 0, jnp.concatenate([own, other], 1), jnp.concatenate([other, own], 1))

    def ffn(x, scale):
        return dot32(hidden_of(x, scale), down_full)

    named = routes[:, :, None] == jnp.arange(experts, dtype=jnp.int32)[None, None, :]
    dense = jnp.sum(jnp.where(named, route_weights[:, :, None], 0.0), axis=1)
    table = lax.all_gather(dense, "expert", tiled=False)
    table = table.reshape(4, 2, 2, tok_rows, 4, 2)
    table = lax.dynamic_index_in_dim(table, core, 2, keepdims=False)
    table = lax.dynamic_index_in_dim(table, line, 3, keepdims=False)
    sources = [line, line ^ 1, jnp.where(line < 2, 2, 1), jnp.where(line < 2, 3, 0)]
    table = jnp.stack([lax.dynamic_index_in_dim(table, s, 0, keepdims=False) for s in sources])
    table = jnp.where(side == 0, table, table[:, ::-1, :, ::-1])
    table = table.reshape(4, 2, CHUNKS, rows, 2)
    own_scale = table[:, 0, :, :, 0]

    def picks(weights):
        mask = weights > 0
        lower = (jnp.arange(rows)[:, None] <= jnp.arange(rows)[None, :]).astype(bf16)
        place = dot32(mask.astype(bf16), lower).astype(jnp.int32) - 1
        return mask[..., None, :] & (place[..., None, :] == jnp.arange(slots, dtype=jnp.int32)[:, None])

    sent_pick = picks(table[:, 0, :, :, 1]).astype(bf16)
    got_pick = picks(table[:, 1, :, :, 0])
    got_scale = jnp.sum(jnp.where(got_pick, table[:, 1, :, None, :, 0], 0.0), axis=-1)

    outs = []
    for q in range(CHUNKS):
        x0 = tokens[q * rows : (q + 1) * rows]
        x1 = exchange_outer(x0)
        m1 = exchange_middle(x0)
        o1 = move_out(m1)
        m2 = exchange_middle(x1)
        o2 = move_out(m2)
        blocks = [x0, x1, jnp.where(inner, m1, o1), jnp.where(inner, m2, o2)]
        partial = []
        for k, x in enumerate(blocks):
            chosen = dot32(sent_pick[k, q], x).astype(bf16)
            arrived = swapped(chosen, "expert", 1)
            made = ffn(arrived, got_scale[k, q]).astype(bf16)
            back = swapped(made, "expert", 1)
            partial.append(ffn(x, own_scale[k, q]) + dot32(sent_pick[k, q].T, back))
        p0, p1, p2, p3 = partial
        i2 = move_in(p2.astype(bf16))
        m2 = exchange_middle((p2 + i2).astype(bf16))
        i3 = move_in(p3.astype(bf16))
        m3 = exchange_middle((p3 + i3).astype(bf16))
        e1 = exchange_outer((p1 + m3).astype(bf16))
        outs.append((p0 + e1 + m2).astype(bf16))
    out = jnp.concatenate(outs, 0)
    own, other = jnp.split(out, 2, axis=1)
    return jnp.where(core == 0, out, jnp.concatenate([other, own], 1))


def solution(mesh):
    body = lined if mesh.shape["expert"] == 16 else dispatched
    return jax.shard_map(
        body,
        mesh=mesh,
        in_specs=(
            P(("groups", "expert"), None),
            P(("groups", "expert"), None),
            P(("groups", "expert"), None),
            P(None, "expert"),
            P(None, "expert"),
            P(None, "expert"),
        ),
        out_specs=P(("groups", "expert"), None),
        check_vma=False,
    )
```

```python
import functools

import jax
import jax.experimental.pallas as pl
import jax.experimental.pallas.tpu as pltpu
import jax.numpy as jnp
from jax import lax
from jax.sharding import PartitionSpec as P

CHUNKS = 1
CROSS_ROWS = 40
LANES = 128


def swapped(x, axis, apart):
    return lax.ppermute(x, axis, [(i, i ^ 1 << apart) for i in range(lax.axis_size(axis))])


def dot32(a, b):
    return jnp.dot(a, b, preferred_element_type=jnp.float32)


def expert_hidden(rows, gate_part, up_part, parity):
    gate = dot32(rows, gate_part)
    upval = dot32(rows, up_part)
    hidden = (jax.nn.silu(gate) * upval).astype(jnp.bfloat16)
    partner = swapped(hidden, "expert", 0)
    return jnp.where(
        parity == 0, jnp.concatenate([hidden, partner], 1), jnp.concatenate([partner, hidden], 1)
    )


def dispatched(tokens, routes, route_weights, gate_weight, up_weight, down_weight):
    tok_rows, top_count = routes.shape
    width = tokens.shape[1]
    half_width = down_weight.shape[1]
    devices = lax.axis_size("expert")
    experts = devices // 2
    capacity = tok_rows * top_count // experts
    parity = lax.axis_index("expert") % 2
    flat = routes.reshape(-1)
    onehot = (flat[:, None] == jnp.arange(experts, dtype=jnp.int32)[None, :]).astype(jnp.int32)
    before = jnp.cumsum(onehot, axis=0) - onehot
    slot_of = jnp.sum(before * onehot, axis=1)
    position = flat * capacity + slot_of
    assign_ids = jnp.arange(flat.shape[0], dtype=jnp.int32) // top_count
    owner = jnp.zeros((experts * capacity,), jnp.int32).at[position].set(assign_ids)
    gathered = tokens[owner]
    outgoing = jnp.broadcast_to(
        gathered.reshape(experts, 1, capacity, width), (experts, 2, capacity, width)
    )
    outgoing = outgoing.reshape(devices, capacity, width)
    received = lax.all_to_all(outgoing, "expert", split_axis=0, concat_axis=0, tiled=True)
    count, items, _ = received.shape
    hidden = expert_hidden(received.reshape(count * items, width), gate_weight, up_weight, parity)
    produced = dot32(hidden, down_weight).astype(jnp.bfloat16)
    returned = lax.all_to_all(
        produced.reshape(count, items, half_width),
        "expert",
        split_axis=0,
        concat_axis=0,
        tiled=True,
    )
    returned = returned.reshape(experts, 2, capacity, half_width).transpose(0, 2, 1, 3)
    expert_rows = returned.reshape(experts * capacity, width)
    picked = expert_rows[position].reshape(tok_rows, top_count, width)
    mixed = jnp.einsum("tk,tkd->td", route_weights, picked.astype(jnp.float32))
    return mixed.astype(jnp.bfloat16)


def along_line(x, pairs):
    moves = [((a * 2 + s) * 2 + c, (b * 2 + s) * 2 + c) for a, b in pairs for s in (0, 1) for c in (0, 1)]
    return lax.ppermute(x, "expert", moves)


def exchange_outer(x):
    return along_line(x, [(0, 1), (1, 0), (2, 3), (3, 2)])


def exchange_middle(x):
    return along_line(x, [(1, 2), (2, 1)])


def move_out(x):
    return along_line(x, [(1, 0), (2, 3)])


def move_in(x):
    return along_line(x, [(0, 1), (3, 2)])


def contract(a, b, da, db):
    return lax.dot_general(a, b, (((da,), (db,)), ((), ())), preferred_element_type=jnp.float32)


def iota(shape, dim):
    return lax.broadcasted_iota(jnp.int32, shape, dim)


def eye(n):
    return (iota((n, n), 0) == iota((n, n), 1)).astype(jnp.bfloat16)


def scale_of(ext, expert, experts):
    lane = iota(ext.shape, 1)
    mine = (lane % experts == expert) & (lane < 3 * experts)
    return jnp.sum(jnp.where(mine, ext.astype(jnp.float32), 0.0), axis=1, keepdims=True)


def prepare_kernel(experts, idx, tokens, routes, weights, *outs):
    rows, width = tokens.shape
    chunks = len(outs) - 1 if len(outs) > 1 else 1
    lane = iota((rows, LANES), 1)
    part = lane // experts
    full = jnp.zeros((rows, LANES), jnp.float32)
    for k in range(routes.shape[1]):
        full += jnp.where(lane % experts == routes[:, k : k + 1], weights[:, k : k + 1], 0.0)
    high = full.astype(jnp.bfloat16).astype(jnp.float32)
    mid = (full - high).astype(jnp.bfloat16).astype(jnp.float32)
    low = full - high - mid
    ext = jnp.where(part == 0, high, jnp.where(part == 1, mid, jnp.where(part == 2, low, 0.0)))
    ext = ext.astype(jnp.bfloat16)
    if chunks == 1:
        outs[0][:, :width] = tokens[...]
        outs[0][:, width:] = ext
        return
    gray = jnp.zeros((rows, 1), jnp.int32)
    bit = jnp.zeros((rows, 1), jnp.int32)
    for z in range(experts // 2):
        named = jnp.zeros((rows, 1), jnp.int32)
        for k in range(routes.shape[1]):
            named += (routes[:, k : k + 1] == idx[5] + 2 * z).astype(jnp.int32)
        bit = bit ^ named
        gray = gray * 2 + bit
    down = jnp.broadcast_to(gray.astype(jnp.float32), (rows, rows))
    across = contract(down.astype(jnp.bfloat16), eye(rows), 0, 0)
    first, second = iota((rows, rows), 0), iota((rows, rows), 1)
    ahead = (down < across) | ((down == across) & (first < second))
    rank = jnp.sum(ahead.astype(jnp.float32), axis=0, keepdims=True).astype(jnp.int32)
    size = rows // chunks
    target = rank % chunks * size + rank // chunks
    order = (first == target).astype(jnp.bfloat16)
    outs[-1][...] = order
    ext = dot32(order, ext).astype(jnp.bfloat16)
    for q in range(chunks):
        outs[q][:, width:] = ext[q * size : (q + 1) * size]
    step = 1024
    for n in range(0, width, step):
        moved = dot32(order, tokens[:, n : n + step]).astype(jnp.bfloat16)
        for q in range(chunks):
            outs[q][:, n : n + step] = moved[q * size : (q + 1) * size]


def pick_kernel(experts, dense, idx, *refs):
    *blocks, own_out, cross_out, pick_out = refs
    rows, total = blocks[0].shape
    own_rows, cross_rows = own_out.shape[0], cross_out.shape[0]
    inner = idx[3] == 1

    def load(cols):
        x = blocks[0][:, cols]
        return jnp.where(inner, x, blocks[1][:, cols]) if len(blocks) > 1 else x

    ext = load(slice(total - LANES, total))

    def picks(expert, count):
        mask = jnp.broadcast_to(scale_of(ext, expert, experts) > 0, (rows, LANES)).astype(jnp.bfloat16)
        upto = (iota((rows, rows), 0) <= iota((rows, rows), 1)).astype(jnp.bfloat16)
        place = contract(mask, upto, 0, 0)[:count]
        named = contract(mask, eye(rows), 0, 0)[:count]
        slot = iota((count, rows), 0).astype(jnp.float32)
        return ((named > 0.5) & (place - 1.0 == slot)).astype(jnp.float32)

    own = eye(rows).astype(jnp.float32) if dense else picks(idx[1], own_rows)
    pick = jnp.concatenate([own, picks(idx[2], cross_rows)], 0).astype(jnp.bfloat16)
    pick_out[...] = pick
    step = total // 3
    for n in range(0, total, step):
        got = dot32(pick, load(slice(n, n + step)))
        own_out[:, n : n + step] = got[:own_rows].astype(jnp.bfloat16)
        cross_out[:, n : n + step] = got[own_rows:].astype(jnp.bfloat16)


def expert_kernel(experts, idx, own, cross, ga, gb, ua, ub, da, db, own_out, cross_out, hidden):
    own_rows, total = own.shape
    width = total - LANES
    core, expert = idx[0], idx[1]
    half = ga.shape[0]
    x = jnp.concatenate([own[:, :width], cross[:, :width]], 0)
    ext = jnp.concatenate([own[:, width:], cross[:, width:]], 0)
    scale = scale_of(ext, expert, experts)
    for place, g, u in ((core, ga, ua), (1 - core, gb, ub)):
        gate = contract(x, g[...], 1, 1)
        upval = contract(x, u[...], 1, 1)
        hidden[place] = (gate / (1.0 + jnp.exp(-gate)) * upval * scale).astype(jnp.bfloat16)
    step = 512
    cols = da.shape[1]
    for n in range(0, 2 * cols, step):
        d, m = (da, n) if n < cols else (db, n - cols)
        made = dot32(hidden[0], d[:half, m : m + step]) + dot32(hidden[1], d[half:, m : m + step])
        own_out[:, n : n + step] = made[:own_rows].astype(jnp.bfloat16)
        cross_out[:, n : n + step] = made[own_rows:].astype(jnp.bfloat16)


def combine_kernel(placed, idx, pick, own, cross, *refs):
    *more, out = refs
    width = own.shape[1]
    step = 1024
    for n in range(0, width, step):
        cols = slice(n, n + step)
        got = contract(pick[...], jnp.concatenate([own[:, cols], cross[:, cols]], 0), 0, 0)
        for ref in more:
            got += ref[:, cols].astype(jnp.float32)
        start = pl.multiple_of((idx[4] + n) % width, step) if placed else n
        out[:, pl.ds(start, step)] = got.astype(jnp.bfloat16)


def place_kernel(idx, order, *refs):
    *chunks, out = refs
    width = out.shape[1]
    step = 1024
    for n in range(0, width, step):
        cols = slice(n, n + step)
        got = contract(order[...], jnp.concatenate([c[:, cols] for c in chunks], 0), 0, 0)
        out[:, pl.ds(pl.multiple_of((idx[4] + n) % width, step), step)] = got.astype(jnp.bfloat16)


def call(kernel, outs, idx, *args, scratch=(), flops=0, limit=24):
    vmem = pl.BlockSpec(memory_space=pltpu.VMEM)
    size = sum(a.size * a.dtype.itemsize for a in list(args) + list(outs))
    return pl.pallas_call(
        kernel,
        out_shape=outs,
        in_specs=[pl.BlockSpec(memory_space=pltpu.SMEM)] + [vmem] * len(args),
        out_specs=[vmem] * len(outs),
        scratch_shapes=list(scratch),
        compiler_params=pltpu.CompilerParams(vmem_limit_bytes=limit << 20),
        cost_estimate=pl.CostEstimate(flops=flops, bytes_accessed=size, transcendentals=0),
    )(idx, *args)


def lined(tokens, routes, route_weights, gate_weight, up_weight, down_weight):
    tok_rows, top_count = routes.shape
    width = tokens.shape[1]
    devices = lax.axis_size("expert")
    experts = devices // 2
    capacity = tok_rows * top_count // experts
    half = gate_weight.shape[1]
    index = lax.axis_index("expert")
    core, side, line = index % 2, index // 2 % 2, index // 4
    inner = ((line == 1) | (line == 2)).astype(jnp.int32)
    idx = jnp.stack(
        [core, 2 * line + side, 2 * line + 1 - side, inner, core * down_weight.shape[1], 1 - side]
    ).astype(jnp.int32)
    rows = tok_rows // CHUNKS
    dense = CHUNKS > 1
    own_rows = rows if dense else capacity
    cross_rows = CROSS_ROWS if dense else capacity
    bf16 = jnp.bfloat16

    def like(*shape):
        return jax.ShapeDtypeStruct(shape, bf16)

    def in_vmem(x):
        return pltpu.with_memory_space_constraint(x, pltpu.VMEM)

    gate, up = gate_weight.T, up_weight.T
    both = [gate, swapped(gate, "expert", 0), up, swapped(up, "expert", 0)]
    both += [down_weight, swapped(down_weight, "expert", 0)]
    both = [in_vmem(w) for w in both]

    total = width + LANES
    payload = [like(rows, total)] * CHUNKS + ([like(tok_rows, tok_rows)] if dense else [])
    payload = call(functools.partial(prepare_kernel, experts), payload, idx, tokens, routes, route_weights)

    def pick(*blocks):
        return call(
            functools.partial(pick_kernel, experts, dense),
            [like(own_rows, total), like(cross_rows, total), like(own_rows + cross_rows, rows)],
            idx,
            *blocks,
            flops=2 * (own_rows + cross_rows) * rows * total,
        )

    def expert(own, cross):
        count = own_rows + cross_rows
        return call(
            functools.partial(expert_kernel, experts),
            [like(own_rows, width), like(cross_rows, width)],
            idx,
            own,
            cross,
            *both,
            scratch=[pltpu.VMEM((2, count, half), bf16)],
            flops=2 * 256 * half * 2 * width * 3,
        )

    def combine(made, *more, placed=False):
        return call(
            functools.partial(combine_kernel, placed),
            [like(rows, width)],
            idx,
            *made,
            *more,
            flops=2 * (own_rows + cross_rows) * rows * width,
        )[0]

    outs = []
    for q in range(CHUNKS):
        x0 = payload[q]
        x1 = exchange_outer(x0)
        m1 = exchange_middle(x0)
        o1 = move_out(m1)
        m2 = exchange_middle(x1)
        o2 = move_out(m2)
        made = []
        for blocks in ([x0], [x1], [m1, o1], [m2, o2]):
            own, cross, chosen = pick(*blocks)
            own, cross = expert(own, swapped(cross, "expert", 1))
            made.append((chosen, own, swapped(cross, "expert", 1)))
        p2 = combine(made[2])
        s2 = exchange_middle(combine(made[2], move_in(p2)))
        p3 = combine(made[3])
        s3 = exchange_middle(combine(made[3], move_in(p3)))
        s1 = exchange_outer(combine(made[1], s3))
        outs.append(combine(made[0], s1, s2, placed=not dense))
    if not dense:
        return outs[0]
    return call(place_kernel, [like(tok_rows, width)], idx, payload[-1], *outs)[0]


def solution(mesh):
    body = lined if mesh.shape["expert"] == 16 else dispatched
    return jax.shard_map(
        body,
        mesh=mesh,
        in_specs=(
            P(("groups", "expert"), None),
            P(("groups", "expert"), None),
            P(("groups", "expert"), None),
            P(None, "expert"),
            P(None, "expert"),
            P(None, "expert"),
        ),
        out_specs=P(("groups", "expert"), None),
        check_vma=False,
    )
```

```python
import functools

import jax
import jax.experimental.pallas as pl
import jax.experimental.pallas.tpu as pltpu
import jax.numpy as jnp
from jax import lax
from jax.sharding import PartitionSpec as P

CROSS_ROWS = 40
LANES = 128


def swapped(x, axis, apart):
    return lax.ppermute(x, axis, [(i, i ^ 1 << apart) for i in range(lax.axis_size(axis))])


def dot32(a, b):
    return jnp.dot(a, b, preferred_element_type=jnp.float32)


def expert_hidden(rows, gate_part, up_part, parity):
    gate = dot32(rows, gate_part)
    upval = dot32(rows, up_part)
    hidden = (jax.nn.silu(gate) * upval).astype(jnp.bfloat16)
    partner = swapped(hidden, "expert", 0)
    return jnp.where(
        parity == 0, jnp.concatenate([hidden, partner], 1), jnp.concatenate([partner, hidden], 1)
    )


def dispatched(tokens, routes, route_weights, gate_weight, up_weight, down_weight):
    tok_rows, top_count = routes.shape
    width = tokens.shape[1]
    half_width = down_weight.shape[1]
    devices = lax.axis_size("expert")
    experts = devices // 2
    capacity = tok_rows * top_count // experts
    parity = lax.axis_index("expert") % 2
    flat = routes.reshape(-1)
    onehot = (flat[:, None] == jnp.arange(experts, dtype=jnp.int32)[None, :]).astype(jnp.int32)
    before = jnp.cumsum(onehot, axis=0) - onehot
    slot_of = jnp.sum(before * onehot, axis=1)
    position = flat * capacity + slot_of
    assign_ids = jnp.arange(flat.shape[0], dtype=jnp.int32) // top_count
    owner = jnp.zeros((experts * capacity,), jnp.int32).at[position].set(assign_ids)
    gathered = tokens[owner]
    outgoing = jnp.broadcast_to(
        gathered.reshape(experts, 1, capacity, width), (experts, 2, capacity, width)
    )
    outgoing = outgoing.reshape(devices, capacity, width)
    received = lax.all_to_all(outgoing, "expert", split_axis=0, concat_axis=0, tiled=True)
    count, items, _ = received.shape
    hidden = expert_hidden(received.reshape(count * items, width), gate_weight, up_weight, parity)
    produced = dot32(hidden, down_weight).astype(jnp.bfloat16)
    returned = lax.all_to_all(
        produced.reshape(count, items, half_width),
        "expert",
        split_axis=0,
        concat_axis=0,
        tiled=True,
    )
    returned = returned.reshape(experts, 2, capacity, half_width).transpose(0, 2, 1, 3)
    expert_rows = returned.reshape(experts * capacity, width)
    picked = expert_rows[position].reshape(tok_rows, top_count, width)
    mixed = jnp.einsum("tk,tkd->td", route_weights, picked.astype(jnp.float32))
    return mixed.astype(jnp.bfloat16)


def along_line(x, pairs):
    moves = [((a * 2 + s) * 2 + c, (b * 2 + s) * 2 + c) for a, b in pairs for s in (0, 1) for c in (0, 1)]
    return lax.ppermute(x, "expert", moves)


OUTER = [(0, 1), (1, 0), (2, 3), (3, 2)]
MIDDLE = [(1, 2), (2, 1)]
OUT = [(1, 0), (2, 3)]
IN = [(0, 1), (3, 2)]
ENDS = [(0, 3), (3, 0)]


def contract(a, b, da, db):
    return lax.dot_general(a, b, (((da,), (db,)), ((), ())), preferred_element_type=jnp.float32)


def iota(shape, dim):
    return lax.broadcasted_iota(jnp.int32, shape, dim)


def eye(n):
    return (iota((n, n), 0) == iota((n, n), 1)).astype(jnp.bfloat16)


def scale_of(ext, expert, experts):
    lane = iota(ext.shape, 1)
    mine = (lane % experts == expert) & (lane < 3 * experts)
    return jnp.sum(jnp.where(mine, ext.astype(jnp.float32), 0.0), axis=1, keepdims=True)


def prepare_kernel(experts, idx, tokens, routes, weights, *outs):
    rows, width = tokens.shape
    *chunks, order_out = outs
    size = rows // len(chunks)
    lane = iota((rows, LANES), 1)
    part = lane // experts
    full = jnp.zeros((rows, LANES), jnp.float32)
    for k in range(routes.shape[1]):
        full += jnp.where(lane % experts == routes[:, k : k + 1], weights[:, k : k + 1], 0.0)
    high = full.astype(jnp.bfloat16).astype(jnp.float32)
    mid = (full - high).astype(jnp.bfloat16).astype(jnp.float32)
    low = full - high - mid
    ext = jnp.where(part == 0, high, jnp.where(part == 1, mid, jnp.where(part == 2, low, 0.0)))
    ext = ext.astype(jnp.bfloat16)
    gray = jnp.zeros((rows, 1), jnp.int32)
    bit = jnp.zeros((rows, 1), jnp.int32)
    for z in range(experts // 2):
        named = jnp.zeros((rows, 1), jnp.int32)
        for k in range(routes.shape[1]):
            named += (routes[:, k : k + 1] == idx[5] + 2 * z).astype(jnp.int32)
        bit = bit ^ named
        gray = gray * 2 + bit
    down = jnp.broadcast_to(gray.astype(jnp.float32), (rows, rows))
    across = contract(down.astype(jnp.bfloat16), eye(rows), 0, 0)
    first, second = iota((rows, rows), 0), iota((rows, rows), 1)
    ahead = (down < across) | ((down == across) & (first < second))
    rank = jnp.sum(ahead.astype(jnp.float32), axis=0, keepdims=True).astype(jnp.int32)
    target = rank % len(chunks) * size + rank // len(chunks)
    order = (first == target).astype(jnp.bfloat16)
    order_out[...] = order
    ext = dot32(order, ext).astype(jnp.bfloat16)
    for q, chunk in enumerate(chunks):
        chunk[:, width:] = ext[q * size : (q + 1) * size]
    step = 1024
    for n in range(0, width, step):
        moved = dot32(order, tokens[:, n : n + step]).astype(jnp.bfloat16)
        for q, chunk in enumerate(chunks):
            chunk[:, n : n + step] = moved[q * size : (q + 1) * size]


def pick_kernel(experts, mode, idx, *refs):
    *blocks, own_out, cross_out, pick_out = refs
    total = blocks[0].shape[1]
    rows = blocks[0].shape[0] * (len(blocks) if mode == "both" else 1)
    own_rows, cross_rows = own_out.shape[0], cross_out.shape[0]
    inner = idx[3] == 1

    def load(cols):
        if mode == "both":
            return jnp.concatenate([b[:, cols] for b in blocks], 0)
        if mode == "either":
            return jnp.where(inner, blocks[0][:, cols], blocks[1][:, cols])
        return blocks[0][:, cols]

    ext = load(slice(total - LANES, total))

    def picks(expert, count):
        mask = jnp.broadcast_to(scale_of(ext, expert, experts) > 0, (rows, LANES)).astype(jnp.bfloat16)
        upto = (iota((rows, rows), 0) <= iota((rows, rows), 1)).astype(jnp.bfloat16)
        place = contract(mask, upto, 0, 0)[:count]
        named = contract(mask, eye(rows), 0, 0)[:count]
        slot = iota((count, rows), 0).astype(jnp.float32)
        return ((named > 0.5) & (place - 1.0 == slot)).astype(jnp.float32)

    own = picks(idx[1], own_rows) if mode == "both" else eye(rows).astype(jnp.float32)
    pick = jnp.concatenate([own, picks(idx[2], cross_rows)], 0).astype(jnp.bfloat16)
    pick_out[...] = pick
    step = total // 3
    for n in range(0, total, step):
        got = dot32(pick, load(slice(n, n + step)))
        own_out[:, n : n + step] = got[:own_rows].astype(jnp.bfloat16)
        cross_out[:, n : n + step] = got[own_rows:].astype(jnp.bfloat16)


def expert_kernel(experts, idx, own, cross, ga, gb, ua, ub, da, db, own_out, cross_out, hidden):
    own_rows, total = own.shape
    width = total - LANES
    core, expert = idx[0], idx[1]
    half = ga.shape[0]
    x = jnp.concatenate([own[:, :width], cross[:, :width]], 0)
    ext = jnp.concatenate([own[:, width:], cross[:, width:]], 0)
    scale = scale_of(ext, expert, experts)
    for place, g, u in ((core, ga, ua), (1 - core, gb, ub)):
        gate = contract(x, g[...], 1, 1)
        upval = contract(x, u[...], 1, 1)
        hidden[place] = (gate / (1.0 + jnp.exp(-gate)) * upval * scale).astype(jnp.bfloat16)
    step = 512
    cols = da.shape[1]
    for n in range(0, 2 * cols, step):
        d, m = (da, n) if n < cols else (db, n - cols)
        made = dot32(hidden[0], d[:half, m : m + step]) + dot32(hidden[1], d[half:, m : m + step])
        own_out[:, n : n + step] = made[:own_rows].astype(jnp.bfloat16)
        cross_out[:, n : n + step] = made[own_rows:].astype(jnp.bfloat16)


def combine_kernel(idx, pick, own, cross, *refs):
    *more, out = refs
    width = own.shape[1]
    step = 1024
    for n in range(0, width, step):
        cols = slice(n, n + step)
        got = contract(pick[...], jnp.concatenate([own[:, cols], cross[:, cols]], 0), 0, 0)
        for ref in more:
            got += ref[:, cols].astype(jnp.float32)
        out[:, cols] = got.astype(jnp.bfloat16)


def finish_kernel(idx, order, pick, own, cross, *refs):
    *more, out = refs
    half = len(more) // 2
    width = own.shape[1]
    step = 1024
    for n in range(0, width, step):
        cols = slice(n, n + step)
        got = contract(pick[...], jnp.concatenate([own[:, cols], cross[:, cols]], 0), 0, 0)
        sums = [sum(r[:, cols].astype(jnp.float32) for r in part) for part in (more[:half], more[half:])]
        got = (got + jnp.concatenate(sums, 0)).astype(jnp.bfloat16)
        got = contract(order[...], got, 0, 0).astype(jnp.bfloat16)
        out[:, pl.ds(pl.multiple_of((idx[4] + n) % width, step), step)] = got


def fence_kernel(idx):
    pass


def call(kernel, outs, idx, token, args, passes=(), scratch=()):
    vmem, anywhere = pl.BlockSpec(memory_space=pltpu.VMEM), pl.BlockSpec(memory_space=pl.ANY)
    through = [token, *passes]
    first = 1 + len(args)

    def body(*refs):
        ins, rest = refs[:first], refs[first + len(through) :]
        kernel(*ins, *rest[: len(outs)], *rest[len(outs) + len(through) :])

    got = pl.pallas_call(
        body,
        out_shape=[*outs, *(jax.ShapeDtypeStruct(x.shape, x.dtype) for x in through)],
        in_specs=[pl.BlockSpec(memory_space=pltpu.SMEM)] + [vmem] * len(args) + [anywhere] * len(through),
        out_specs=[vmem] * len(outs) + [anywhere] * len(through),
        input_output_aliases={first + i: len(outs) + i for i in range(len(through))},
        scratch_shapes=list(scratch),
        compiler_params=pltpu.CompilerParams(vmem_limit_bytes=24 << 20),
        cost_estimate=pl.CostEstimate(flops=1, bytes_accessed=1, transcendentals=0),
    )(idx, *args, *through)
    return got[: len(outs)], got[len(outs)], got[len(outs) + 1 :]


ORDER = [
    ["prep", "EA", "MB"],
    ["P0", "Y0"],
    ["f", "EB"],
    ["f", "OB"],
    ["P1A"],
    ["f", "NA", "Y1A"],
    ["P1B"],
    ["f", "NB", "Y1B"],
    ["f", "QA"],
    ["P2B", "Y2B"],
    ["F0"],
    ["f", "MA", "QB"],
    ["P3A", "Y3A"],
    ["F2B", "R2B"],
    ["F3A", "R3A"],
    ["f", "OA"],
    ["C2B", "I2B"],
    ["P3B", "Y3B"],
    ["C3A", "S3A"],
    ["P2A", "Y2A", "X3A"],
    ["F3B", "R3B"],
    ["F2A"],
    ["C3B", "X3B", "R2A"],
    ["F1A"],
    ["C2A", "I2A", "S3B", "R1A"],
    ["F1B", "R1B", "R0"],
    ["D2B"],
    ["D1A", "S2B", "S1A"],
    ["D2A", "S2A"],
    ["D1B", "S1B"],
    ["fin"],
]


def lined(tokens, routes, route_weights, gate_weight, up_weight, down_weight):
    tok_rows, top_count = routes.shape
    width = tokens.shape[1]
    devices = lax.axis_size("expert")
    experts = devices // 2
    capacity = tok_rows * top_count // experts
    half = gate_weight.shape[1]
    index = lax.axis_index("expert")
    core, side, line = index % 2, index // 2 % 2, index // 4
    inner = ((line == 1) | (line == 2)).astype(jnp.int32)
    idx = jnp.stack(
        [core, 2 * line + side, 2 * line + 1 - side, inner, core * down_weight.shape[1], 1 - side]
    ).astype(jnp.int32)
    rows = tok_rows // 2
    total = width + LANES
    bf16 = jnp.bfloat16

    def like(*shape):
        return jax.ShapeDtypeStruct(shape, bf16)

    gate, up = gate_weight.T, up_weight.T
    both = [gate, swapped(gate, "expert", 0), up, swapped(up, "expert", 0)]
    both += [down_weight, swapped(down_weight, "expert", 0)]
    both = [pltpu.with_memory_space_constraint(w, pltpu.VMEM) for w in both]

    val = {}

    def kernel_of(name):
        kind, q = name[:-1], name[-1]
        if name == "prep":
            return (
                functools.partial(prepare_kernel, experts),
                [like(rows, total), like(rows, total), like(tok_rows, tok_rows)],
                [tokens, routes, route_weights],
                [],
            )
        if name[0] == "P":
            slot = name[1:]
            blocks, mode = {
                "0": (["payA", "payB"], "both"),
                "1": (["E" + q], "one"),
                "2": (["M" + q, "O" + q], "either"),
                "3": (["N" + q, "Q" + q], "either"),
            }[slot[0]]
            own, cross, size = (capacity, capacity, tok_rows) if mode == "both" else (rows, CROSS_ROWS, rows)
            return (
                functools.partial(pick_kernel, experts, mode),
                [like(own, total), like(cross, total), like(own + cross, size)],
                [val[b] for b in blocks],
                [],
            )
        if name[0] == "F":
            own, cross = val["own" + name[1:]], val["Y" + name[1:]]
            return (
                functools.partial(expert_kernel, experts),
                [like(own.shape[0], width), like(cross.shape[0], width)],
                [own, cross, *both],
                [pltpu.VMEM((2, own.shape[0] + cross.shape[0], half), bf16)],
            )
        if name == "fin":
            made = [val["order"], val["pick0"], val["made0"], val["R0"]]
            made += [val[s + q] for q in "AB" for s in ("S1", "S2", "X3")]
            return finish_kernel, [like(tok_rows, width)], made, []
        made = [val[s + name[1:]] for s in ("pick", "made", "R")]
        made += [val[x] for x in {"D2": ["I2" + q], "D1": ["S3" + q]}.get(kind, [])]
        return combine_kernel, [like(rows, width)], made, []

    def keep(name, got):
        slot = name[1:]
        if name == "prep":
            val["payA"], val["payB"], val["order"] = got
        elif name[0] == "P":
            val["own" + slot], val["cross" + slot], val["pick" + slot] = got
        elif name[0] == "F":
            val["made" + slot], val["back" + slot] = got
        else:
            val[name] = got[0]

    def move_of(name):
        kind, slot, q = name[0], name[1:], name[-1]
        if kind == "Y":
            return "cross" + slot, lambda x: swapped(x, "expert", 1)
        if kind == "R":
            return "back" + slot, lambda x: swapped(x, "expert", 1)
        source, pairs = {
            "E": ("pay" + q, OUTER),
            "M": ("pay" + q, MIDDLE),
            "O": ("M" + q, OUT),
            "N": ("E" + q, MIDDLE),
            "Q": ("N" + q, OUT),
            "I2": ("C2" + q, IN),
            "S2": ("D2" + q, MIDDLE),
            "X3": ("C3" + q, ENDS),
            "S3": ("C3" + q, MIDDLE),
            "S1": ("D1" + q, OUTER),
        }[name[:-1]]
        return source, lambda x: along_line(x, pairs)

    token = jnp.zeros((8, LANES), jnp.float32)
    for name, *moves in ORDER:
        sources = {m: move_of(m)[0] for m in moves}
        passed = sorted({s for s in sources.values() if s in val})
        if name == "f":
            _, token, through = call(fence_kernel, [], idx, token, [], [val[s] for s in passed])
        else:
            kernel, outs, args, scratch = kernel_of(name)
            got, token, through = call(kernel, outs, idx, token, args, [val[s] for s in passed], scratch)
            keep(name, got)
        val.update(zip(passed, through))
        for m in moves:
            val[m] = move_of(m)[1](val[sources[m]])
    return val["fin"]


def solution(mesh):
    body = lined if mesh.shape["expert"] == 16 else dispatched
    return jax.shard_map(
        body,
        mesh=mesh,
        in_specs=(
            P(("groups", "expert"), None),
            P(("groups", "expert"), None),
            P(("groups", "expert"), None),
            P(None, "expert"),
            P(None, "expert"),
            P(None, "expert"),
        ),
        out_specs=P(("groups", "expert"), None),
        check_vma=False,
    )
```

```python
import functools

import jax
import jax.experimental.pallas as pl
import jax.experimental.pallas.tpu as pltpu
import jax.numpy as jnp
from jax import lax
from jax.sharding import PartitionSpec as P

CROSS_ROWS = 40
LANES = 128
LIMIT = 36 << 20


def swapped(x, axis, apart):
    return lax.ppermute(x, axis, [(i, i ^ 1 << apart) for i in range(lax.axis_size(axis))])


def dot32(a, b):
    return jnp.dot(a, b, preferred_element_type=jnp.float32)


def expert_hidden(rows, gate_part, up_part, parity):
    gate = dot32(rows, gate_part)
    upval = dot32(rows, up_part)
    hidden = (jax.nn.silu(gate) * upval).astype(jnp.bfloat16)
    partner = swapped(hidden, "expert", 0)
    return jnp.where(
        parity == 0, jnp.concatenate([hidden, partner], 1), jnp.concatenate([partner, hidden], 1)
    )


def dispatched(tokens, routes, route_weights, gate_weight, up_weight, down_weight):
    tok_rows, top_count = routes.shape
    width = tokens.shape[1]
    half_width = down_weight.shape[1]
    devices = lax.axis_size("expert")
    experts = devices // 2
    capacity = tok_rows * top_count // experts
    parity = lax.axis_index("expert") % 2
    flat = routes.reshape(-1)
    onehot = (flat[:, None] == jnp.arange(experts, dtype=jnp.int32)[None, :]).astype(jnp.int32)
    before = jnp.cumsum(onehot, axis=0) - onehot
    slot_of = jnp.sum(before * onehot, axis=1)
    position = flat * capacity + slot_of
    assign_ids = jnp.arange(flat.shape[0], dtype=jnp.int32) // top_count
    owner = jnp.zeros((experts * capacity,), jnp.int32).at[position].set(assign_ids)
    gathered = tokens[owner]
    outgoing = jnp.broadcast_to(
        gathered.reshape(experts, 1, capacity, width), (experts, 2, capacity, width)
    )
    outgoing = outgoing.reshape(devices, capacity, width)
    received = lax.all_to_all(outgoing, "expert", split_axis=0, concat_axis=0, tiled=True)
    count, items, _ = received.shape
    hidden = expert_hidden(received.reshape(count * items, width), gate_weight, up_weight, parity)
    produced = dot32(hidden, down_weight).astype(jnp.bfloat16)
    returned = lax.all_to_all(
        produced.reshape(count, items, half_width),
        "expert",
        split_axis=0,
        concat_axis=0,
        tiled=True,
    )
    returned = returned.reshape(experts, 2, capacity, half_width).transpose(0, 2, 1, 3)
    expert_rows = returned.reshape(experts * capacity, width)
    picked = expert_rows[position].reshape(tok_rows, top_count, width)
    mixed = jnp.einsum("tk,tkd->td", route_weights, picked.astype(jnp.float32))
    return mixed.astype(jnp.bfloat16)


def along_line(x, pairs):
    moves = [((a * 2 + s) * 2 + c, (b * 2 + s) * 2 + c) for a, b in pairs for s in (0, 1) for c in (0, 1)]
    return lax.ppermute(x, "expert", moves)


OUTER = [(0, 1), (1, 0), (2, 3), (3, 2)]
MIDDLE = [(1, 2), (2, 1)]
OUT = [(1, 0), (2, 3)]
IN = [(0, 1), (3, 2)]
ENDS = [(0, 3), (3, 0)]


def contract(a, b, da, db):
    return lax.dot_general(a, b, (((da,), (db,)), ((), ())), preferred_element_type=jnp.float32)


def iota(shape, dim):
    return lax.broadcasted_iota(jnp.int32, shape, dim)


def eye(n):
    return (iota((n, n), 0) == iota((n, n), 1)).astype(jnp.bfloat16)


def scale_of(ext, expert, experts):
    lane = iota(ext.shape, 1)
    mine = (lane % experts == expert) & (lane < 3 * experts)
    return jnp.sum(jnp.where(mine, ext.astype(jnp.float32), 0.0), axis=1, keepdims=True)


def prepare_kernel(experts, idx, tokens, routes, weights, *outs):
    rows, width = tokens.shape
    *chunks, order_out = outs
    size = rows // len(chunks)
    lane = iota((rows, LANES), 1)
    part = lane // experts
    full = jnp.zeros((rows, LANES), jnp.float32)
    for k in range(routes.shape[1]):
        full += jnp.where(lane % experts == routes[:, k : k + 1], weights[:, k : k + 1], 0.0)
    high = full.astype(jnp.bfloat16).astype(jnp.float32)
    mid = (full - high).astype(jnp.bfloat16).astype(jnp.float32)
    low = full - high - mid
    ext = jnp.where(part == 0, high, jnp.where(part == 1, mid, jnp.where(part == 2, low, 0.0)))
    ext = ext.astype(jnp.bfloat16)
    gray = jnp.zeros((rows, 1), jnp.int32)
    bit = jnp.zeros((rows, 1), jnp.int32)
    for z in range(experts // 2):
        named = jnp.zeros((rows, 1), jnp.int32)
        for k in range(routes.shape[1]):
            named += (routes[:, k : k + 1] == idx[5] + 2 * z).astype(jnp.int32)
        bit = bit ^ named
        gray = gray * 2 + bit
    down = jnp.broadcast_to(gray.astype(jnp.float32), (rows, rows))
    across = contract(down.astype(jnp.bfloat16), eye(rows), 0, 0)
    first, second = iota((rows, rows), 0), iota((rows, rows), 1)
    ahead = (down < across) | ((down == across) & (first < second))
    rank = jnp.sum(ahead.astype(jnp.float32), axis=0, keepdims=True).astype(jnp.int32)
    target = rank % len(chunks) * size + rank // len(chunks)
    order = (first == target).astype(jnp.bfloat16)
    order_out[...] = order
    ext = dot32(order, ext).astype(jnp.bfloat16)
    for q, chunk in enumerate(chunks):
        chunk[:, width:] = ext[q * size : (q + 1) * size]
    step = 1024
    for n in range(0, width, step):
        moved = dot32(order, tokens[:, n : n + step]).astype(jnp.bfloat16)
        for q, chunk in enumerate(chunks):
            chunk[:, n : n + step] = moved[q * size : (q + 1) * size]


def pick_kernel(experts, mode, idx, *refs):
    *blocks, own_out, cross_out, pick_out = refs
    total = blocks[0].shape[1]
    rows = blocks[0].shape[0] * (len(blocks) if mode == "both" else 1)
    own_rows, cross_rows = own_out.shape[0], cross_out.shape[0]
    inner = idx[3] == 1

    def load(cols):
        if mode == "both":
            return jnp.concatenate([b[:, cols] for b in blocks], 0)
        if mode == "either":
            return jnp.where(inner, blocks[0][:, cols], blocks[1][:, cols])
        return blocks[0][:, cols]

    ext = load(slice(total - LANES, total))

    def picks(expert, count):
        mask = jnp.broadcast_to(scale_of(ext, expert, experts) > 0, (rows, LANES)).astype(jnp.bfloat16)
        upto = (iota((rows, rows), 0) <= iota((rows, rows), 1)).astype(jnp.bfloat16)
        place = contract(mask, upto, 0, 0)[:count]
        named = contract(mask, eye(rows), 0, 0)[:count]
        slot = iota((count, rows), 0).astype(jnp.float32)
        return ((named > 0.5) & (place - 1.0 == slot)).astype(jnp.float32)

    own = picks(idx[1], own_rows) if mode == "both" else eye(rows).astype(jnp.float32)
    pick = jnp.concatenate([own, picks(idx[2], cross_rows)], 0).astype(jnp.bfloat16)
    pick_out[...] = pick
    step = total // 3
    for n in range(0, total, step):
        got = dot32(pick, load(slice(n, n + step)))
        own_out[:, n : n + step] = got[:own_rows].astype(jnp.bfloat16)
        cross_out[:, n : n + step] = got[own_rows:].astype(jnp.bfloat16)


def expert_kernel(experts, idx, own, cross, *refs):
    *weights, own_out, cross_out, hidden, wide, deep, sems = refs
    gates, ups, downs = weights[:2], weights[2:4], weights[4:]
    own_rows, total = own.shape
    width = total - LANES
    core, expert = idx[0], idx[1]
    part, step = wide.shape[3], deep.shape[2]
    pieces = wide.shape[1]
    spans = downs[0].shape[1] // step
    copies = []
    for h in range(2):
        for p in range(pieces):
            rows = pl.ds(p * part, part)
            for s, ref in enumerate((gates[h], ups[h])):
                copies.append((ref.at[rows], wide.at[h, p, s]))
    for h in range(2):
        for n in range(spans):
            copies.append((downs[h].at[:, pl.ds(n * step, step)], deep.at[h * spans + n]))
    copies = [pltpu.make_async_copy(s, d, sems.at[i]) for i, (s, d) in enumerate(copies)]
    for c in copies:
        c.start()
    x = jnp.concatenate([own[:, :width], cross[:, :width]], 0)
    ext = jnp.concatenate([own[:, width:], cross[:, width:]], 0)
    scale = scale_of(ext, expert, experts)
    due = iter(copies)
    for h in range(2):
        place = core if h == 0 else 1 - core
        for p in range(pieces):
            next(due).wait()
            gate = contract(x, wide[h, p, 0], 1, 1)
            next(due).wait()
            upval = contract(x, wide[h, p, 1], 1, 1)
            hidden[place, p] = (gate / (1.0 + jnp.exp(-gate)) * upval * scale).astype(jnp.bfloat16)
    for n in range(2 * spans):
        next(due).wait()
        made = jnp.zeros((x.shape[0], step), jnp.float32)
        for k in range(2 * pieces):
            made += dot32(hidden[k // pieces, k % pieces], deep[n, k * part : (k + 1) * part])
        cols = slice(n * step, (n + 1) * step)
        own_out[:, cols] = made[:own_rows].astype(jnp.bfloat16)
        cross_out[:, cols] = made[own_rows:].astype(jnp.bfloat16)


def combine_kernel(first, idx, pick, own, cross, *refs):
    *more, out = refs
    width = own.shape[1]
    rows = slice(first, first + out.shape[0])
    step = 1024
    for n in range(0, width, step):
        cols = slice(n, n + step)
        got = contract(pick[...], jnp.concatenate([own[:, cols], cross[:, cols]], 0), 0, 0)[rows]
        for ref in more:
            got += ref[:, cols].astype(jnp.float32)
        out[:, cols] = got.astype(jnp.bfloat16)


def finish_kernel(half, idx, order, pick, own, cross, *refs):
    *more, out = refs
    width = own.shape[1]
    step = 1024
    for n in range(0, width, step):
        cols = slice(n, n + step)
        got = contract(pick[...], jnp.concatenate([own[:, cols], cross[:, cols]], 0), 0, 0)
        sums = [sum(r[:, cols].astype(jnp.float32) for r in part) for part in (more[:half], more[half:])]
        got = (got + jnp.concatenate(sums, 0)).astype(jnp.bfloat16)
        got = contract(order[...], got, 0, 0).astype(jnp.bfloat16)
        out[:, pl.ds(pl.multiple_of((idx[4] + n) % width, step), step)] = got


def fence_kernel(idx):
    pass


def call(kernel, outs, idx, token, args, left=(), passes=(), scratch=()):
    vmem, anywhere = pl.BlockSpec(memory_space=pltpu.VMEM), pl.BlockSpec(memory_space=pl.ANY)
    through = [token, *passes]
    first = 1 + len(args) + len(left)

    def body(*refs):
        ins, rest = refs[:first], refs[first + len(through) :]
        kernel(*ins, *rest[: len(outs)], *rest[len(outs) + len(through) :])

    got = pl.pallas_call(
        body,
        out_shape=[*outs, *(jax.ShapeDtypeStruct(x.shape, x.dtype) for x in through)],
        in_specs=[pl.BlockSpec(memory_space=pltpu.SMEM)] + [vmem] * len(args) + [anywhere] * (len(left) + len(through)),
        out_specs=[vmem] * len(outs) + [anywhere] * len(through),
        input_output_aliases={first + i: len(outs) + i for i in range(len(through))},
        scratch_shapes=list(scratch),
        compiler_params=pltpu.CompilerParams(vmem_limit_bytes=LIMIT),
        cost_estimate=pl.CostEstimate(flops=1, bytes_accessed=1, transcendentals=0),
    )(idx, *args, *left, *through)
    return got[: len(outs)], got[len(outs)], got[len(outs) + 1 :]


ORDER = [
    ["prep", "EB", "MA", "EA", "+EB"],
    ["P1B", "Y1B", "+MA", "+wg"],
    ["f", "NB"],
    ["f", "OA", "+wd"],
    ["P0"],
    ["f", "Y0", "+wu"],
    ["F1B"],
    ["P1A", "Y1A", "QB"],
    ["f", "NA"],
    ["P2A", "Y2A"],
    ["F0"],
    ["f", "MB", "QA"],
    ["P3B", "Y3B"],
    ["F2A", "R2A"],
    ["P3A", "OB", "Y3A"],
    ["F3B"],
    ["C2A", "I2A", "R3B"],
    ["F3A"],
    ["C3B", "R3A", "X3B"],
    ["P2B", "Y2B"],
    ["D2A"],
    ["F1A", "S3B"],
    ["C3A", "I3A", "R1B"],
    ["F2B", "R2B"],
    ["D1B", "S1B", "R1A"],
    ["D3A", "S3A"],
    ["C2B", "I2B", "S2A", "+R1A", "R0", "+S3A"],
    ["D1A"],
    ["D2B", "S2B", "S1A", "+X3B"],
    ["fin"],
]


def lined(tokens, routes, route_weights, gate_weight, up_weight, down_weight):
    tok_rows, top_count = routes.shape
    width = tokens.shape[1]
    devices = lax.axis_size("expert")
    experts = devices // 2
    capacity = tok_rows * top_count // experts
    half = gate_weight.shape[1]
    index = lax.axis_index("expert")
    core, side, line = index % 2, index // 2 % 2, index // 4
    inner = ((line == 1) | (line == 2)).astype(jnp.int32)
    idx = jnp.stack(
        [core, 2 * line + side, 2 * line + 1 - side, inner, core * down_weight.shape[1], 1 - side]
    ).astype(jnp.int32)
    rows = tok_rows // 2
    total = width + LANES
    bf16 = jnp.bfloat16

    def like(*shape):
        return jax.ShapeDtypeStruct(shape, bf16)

    gate, up = gate_weight.T, up_weight.T

    val = {"wg": swapped(gate, "expert", 0), "wu": swapped(up, "expert", 0)}
    val["wd"] = swapped(down_weight, "expert", 0)
    steps = {name for name, *_ in ORDER}
    slots = {name[1:] for name in steps if name[0] == "P"}

    def kernel_of(name):
        kind, q = name[:-1], name[-1]
        if name == "prep":
            return (
                functools.partial(prepare_kernel, experts),
                [like(rows, total), like(rows, total), like(tok_rows, tok_rows)],
                [tokens, routes, route_weights],
                [],
                [],
            )
        if name[0] == "P":
            slot = name[1:]
            if slot in ("0", "1"):
                blocks, mode = [["payA", "payB"], ["EA", "EB"]][int(slot)], "both"
                own, cross, size = capacity, capacity, tok_rows
            else:
                blocks = {"1": ["E" + q], "2": ["M" + q, "O" + q], "3": ["N" + q, "Q" + q]}[slot[0]]
                mode = "one" if len(blocks) == 1 else "either"
                own, cross, size = rows, CROSS_ROWS, rows
            return (
                functools.partial(pick_kernel, experts, mode),
                [like(own, total), like(cross, total), like(own + cross, size)],
                [val[b] for b in blocks],
                [],
                [],
            )
        if name[0] == "F":
            own, cross = val["own" + name[1:]], val["Y" + name[1:]]
            pieces, step = 2, 512
            part, spans = half // pieces, width // step
            scratch = [
                pltpu.VMEM((2, pieces, own.shape[0] + cross.shape[0], part), bf16),
                pltpu.VMEM((2, pieces, 2, part, width), bf16),
                pltpu.VMEM((spans, 2 * half, step), bf16),
                pltpu.SemaphoreType.DMA((4 * pieces + spans,)),
            ]
            return (
                functools.partial(expert_kernel, experts),
                [like(own.shape[0], width), like(cross.shape[0], width)],
                [own, cross],
                [gate, val["wg"], up, val["wu"], down_weight, val["wd"]],
                scratch,
            )
        if name == "fin":
            made = [val["order"], val["pick0"], val["made0"], val["R0"]]
            made += [val[s + q] for q in "AB" for s in ("S1", "S2", "X3") if s + q in val]
            counts = [sum(s + q in val for s in ("S1", "S2", "X3")) for q in "AB"]
            return functools.partial(finish_kernel, counts[0]), [like(tok_rows, width)], made, [], []
        slot = name[1:] if name[1:] in slots else name[1]
        made = [val[s + slot] for s in ("pick", "made", "R")]
        made += [val[x] for x in {"D2": ["I2" + q], "D3": ["I3" + q], "D1": ["S3" + q]}.get(kind, [])]
        first = rows if slot == name[1] and q == "B" else 0
        return functools.partial(combine_kernel, first), [like(rows, width)], made, [], []

    def keep(name, got):
        slot = name[1:]
        if name == "prep":
            val["payA"], val["payB"], val["order"] = got
        elif name[0] == "P":
            val["own" + slot], val["cross" + slot], val["pick" + slot] = got
        elif name[0] == "F":
            val["made" + slot], val["back" + slot] = got
        else:
            val[name] = got[0]

    def move_of(name):
        kind, slot, q = name[0], name[1:], name[-1]
        if kind == "Y":
            return "cross" + slot, lambda x: swapped(x, "expert", 1)
        if kind == "R":
            return "back" + slot, lambda x: swapped(x, "expert", 1)
        source, pairs = {
            "E": ("pay" + q, OUTER),
            "M": ("pay" + q, MIDDLE),
            "O": ("M" + q, OUT),
            "N": ("E" + q, MIDDLE),
            "Q": ("N" + q, OUT),
            "I2": ("C2" + q, IN),
            "S2": ("D2" + q, MIDDLE),
            "X3": ("C3" + q, ENDS),
            "I3": ("C3" + q, IN),
            "S3": (("D3" if "D3" + q in steps else "C3") + q, MIDDLE),
            "S1": ("D1" + q, OUTER),
        }[name[:-1]]
        return source, lambda x: along_line(x, pairs)

    token = jnp.zeros((8, LANES), jnp.float32)
    for name, *moves in ORDER:
        done = [m[1:] for m in moves if m[0] == "+"]
        moves = [m for m in moves if m[0] != "+"]
        sources = {m: move_of(m)[0] for m in moves}
        passed = sorted({s for s in [*sources.values(), *done] if s in val})
        if name == "f":
            _, token, through = call(fence_kernel, [], idx, token, [], passes=[val[s] for s in passed])
        else:
            kernel, outs, args, left, scratch = kernel_of(name)
            passes = [val[s] for s in passed]
            got, token, through = call(kernel, outs, idx, token, args, left, passes, scratch)
            keep(name, got)
        val.update(zip(passed, through))
        for m in moves:
            val[m] = move_of(m)[1](val[sources[m]])
    return val["fin"]


def solution(mesh):
    body = lined if mesh.shape["expert"] == 16 else dispatched
    return jax.shard_map(
        body,
        mesh=mesh,
        in_specs=(
            P(("groups", "expert"), None),
            P(("groups", "expert"), None),
            P(("groups", "expert"), None),
            P(None, "expert"),
            P(None, "expert"),
            P(None, "expert"),
        ),
        out_specs=P(("groups", "expert"), None),
        check_vma=False,
    )
```

```python
import functools

import jax
import jax.experimental.pallas as pl
import jax.experimental.pallas.tpu as pltpu
import jax.numpy as jnp
from jax import lax
from jax.sharding import PartitionSpec as P

CROSS_ROWS = 40
LANES = 128
LIMIT = 12 << 20


def swapped(x, axis, apart):
    return lax.ppermute(x, axis, [(i, i ^ 1 << apart) for i in range(lax.axis_size(axis))])


def dot32(a, b):
    return jnp.dot(a, b, preferred_element_type=jnp.float32)


def expert_hidden(rows, gate_part, up_part, parity):
    gate = dot32(rows, gate_part)
    upval = dot32(rows, up_part)
    hidden = (jax.nn.silu(gate) * upval).astype(jnp.bfloat16)
    partner = swapped(hidden, "expert", 0)
    return jnp.where(
        parity == 0, jnp.concatenate([hidden, partner], 1), jnp.concatenate([partner, hidden], 1)
    )


def dispatched(tokens, routes, route_weights, gate_weight, up_weight, down_weight):
    tok_rows, top_count = routes.shape
    width = tokens.shape[1]
    half_width = down_weight.shape[1]
    devices = lax.axis_size("expert")
    experts = devices // 2
    capacity = tok_rows * top_count // experts
    parity = lax.axis_index("expert") % 2
    flat = routes.reshape(-1)
    onehot = (flat[:, None] == jnp.arange(experts, dtype=jnp.int32)[None, :]).astype(jnp.int32)
    before = jnp.cumsum(onehot, axis=0) - onehot
    slot_of = jnp.sum(before * onehot, axis=1)
    position = flat * capacity + slot_of
    assign_ids = jnp.arange(flat.shape[0], dtype=jnp.int32) // top_count
    owner = jnp.zeros((experts * capacity,), jnp.int32).at[position].set(assign_ids)
    gathered = tokens[owner]
    outgoing = jnp.broadcast_to(
        gathered.reshape(experts, 1, capacity, width), (experts, 2, capacity, width)
    )
    outgoing = outgoing.reshape(devices, capacity, width)
    received = lax.all_to_all(outgoing, "expert", split_axis=0, concat_axis=0, tiled=True)
    count, items, _ = received.shape
    hidden = expert_hidden(received.reshape(count * items, width), gate_weight, up_weight, parity)
    produced = dot32(hidden, down_weight).astype(jnp.bfloat16)
    returned = lax.all_to_all(
        produced.reshape(count, items, half_width),
        "expert",
        split_axis=0,
        concat_axis=0,
        tiled=True,
    )
    returned = returned.reshape(experts, 2, capacity, half_width).transpose(0, 2, 1, 3)
    expert_rows = returned.reshape(experts * capacity, width)
    picked = expert_rows[position].reshape(tok_rows, top_count, width)
    mixed = jnp.einsum("tk,tkd->td", route_weights, picked.astype(jnp.float32))
    return mixed.astype(jnp.bfloat16)


def along_line(x, pairs):
    moves = [((a * 2 + s) * 2 + c, (b * 2 + s) * 2 + c) for a, b in pairs for s in (0, 1) for c in (0, 1)]
    return lax.ppermute(x, "expert", moves)


OUTER = [(0, 1), (1, 0), (2, 3), (3, 2)]
MIDDLE = [(1, 2), (2, 1)]
OUT = [(1, 0), (2, 3)]
IN = [(0, 1), (3, 2)]
ENDS = [(0, 3), (3, 0)]


def contract(a, b, da, db):
    return lax.dot_general(a, b, (((da,), (db,)), ((), ())), preferred_element_type=jnp.float32)


def iota(shape, dim):
    return lax.broadcasted_iota(jnp.int32, shape, dim)


def eye(n):
    return (iota((n, n), 0) == iota((n, n), 1)).astype(jnp.bfloat16)


def scale_of(ext, expert, experts):
    lane = iota(ext.shape, 1)
    mine = (lane % experts == expert) & (lane < 3 * experts)
    return jnp.sum(jnp.where(mine, ext.astype(jnp.float32), 0.0), axis=1, keepdims=True)


def prepare_kernel(experts, idx, tokens, routes, weights, *outs):
    rows, width = tokens.shape
    *chunks, order_out = outs
    size = rows // len(chunks)
    lane = iota((rows, LANES), 1)
    part = lane // experts
    full = jnp.zeros((rows, LANES), jnp.float32)
    for k in range(routes.shape[1]):
        full += jnp.where(lane % experts == routes[:, k : k + 1], weights[:, k : k + 1], 0.0)
    high = full.astype(jnp.bfloat16).astype(jnp.float32)
    mid = (full - high).astype(jnp.bfloat16).astype(jnp.float32)
    low = full - high - mid
    ext = jnp.where(part == 0, high, jnp.where(part == 1, mid, jnp.where(part == 2, low, 0.0)))
    ext = ext.astype(jnp.bfloat16)
    gray = jnp.zeros((rows, 1), jnp.int32)
    bit = jnp.zeros((rows, 1), jnp.int32)
    for z in range(experts // 2):
        named = jnp.zeros((rows, 1), jnp.int32)
        for k in range(routes.shape[1]):
            named += (routes[:, k : k + 1] == idx[5] + 2 * z).astype(jnp.int32)
        bit = bit ^ named
        gray = gray * 2 + bit
    down = jnp.broadcast_to(gray.astype(jnp.float32), (rows, rows))
    across = contract(down.astype(jnp.bfloat16), eye(rows), 0, 0)
    first, second = iota((rows, rows), 0), iota((rows, rows), 1)
    ahead = (down < across) | ((down == across) & (first < second))
    rank = jnp.sum(ahead.astype(jnp.float32), axis=0, keepdims=True).astype(jnp.int32)
    target = rank % len(chunks) * size + rank // len(chunks)
    order = (first == target).astype(jnp.bfloat16)
    order_out[...] = order
    ext = dot32(order, ext).astype(jnp.bfloat16)
    for q, chunk in enumerate(chunks):
        chunk[:, width:] = ext[q * size : (q + 1) * size]
    step = 1024
    for n in range(0, width, step):
        moved = dot32(order, tokens[:, n : n + step]).astype(jnp.bfloat16)
        for q, chunk in enumerate(chunks):
            chunk[:, n : n + step] = moved[q * size : (q + 1) * size]


def pick_kernel(experts, mode, idx, *refs):
    *blocks, own_out, cross_out, pick_out = refs
    total = blocks[0].shape[1]
    rows = blocks[0].shape[0] * (len(blocks) if mode == "both" else 1)
    own_rows, cross_rows = own_out.shape[0], cross_out.shape[0]
    inner = idx[3] == 1

    def load(cols):
        if mode == "both":
            return jnp.concatenate([b[:, cols] for b in blocks], 0)
        if mode == "either":
            return jnp.where(inner, blocks[0][:, cols], blocks[1][:, cols])
        return blocks[0][:, cols]

    ext = load(slice(total - LANES, total))

    def picks(expert, count):
        mask = jnp.broadcast_to(scale_of(ext, expert, experts) > 0, (rows, LANES)).astype(jnp.bfloat16)
        upto = (iota((rows, rows), 0) <= iota((rows, rows), 1)).astype(jnp.bfloat16)
        place = contract(mask, upto, 0, 0)[:count]
        named = contract(mask, eye(rows), 0, 0)[:count]
        slot = iota((count, rows), 0).astype(jnp.float32)
        return ((named > 0.5) & (place - 1.0 == slot)).astype(jnp.float32)

    own = picks(idx[1], own_rows) if mode == "both" else eye(rows).astype(jnp.float32)
    pick = jnp.concatenate([own, picks(idx[2], cross_rows)], 0).astype(jnp.bfloat16)
    pick_out[...] = pick
    step = total // 3
    for n in range(0, total, step):
        got = dot32(pick, load(slice(n, n + step)))
        own_out[:, n : n + step] = got[:own_rows].astype(jnp.bfloat16)
        cross_out[:, n : n + step] = got[own_rows:].astype(jnp.bfloat16)


def expert_kernel(experts, idx, own, cross, ga, gb, ua, ub, da, db, own_out, cross_out, hidden):
    own_rows, total = own.shape
    width = total - LANES
    core, expert = idx[0], idx[1]
    half = ga.shape[0]
    x = jnp.concatenate([own[:, :width], cross[:, :width]], 0)
    ext = jnp.concatenate([own[:, width:], cross[:, width:]], 0)
    scale = scale_of(ext, expert, experts)
    for place, g, u in ((core, ga, ua), (1 - core, gb, ub)):
        gate = contract(x, g[...], 1, 1)
        upval = contract(x, u[...], 1, 1)
        hidden[place] = (gate / (1.0 + jnp.exp(-gate)) * upval * scale).astype(jnp.bfloat16)
    step = 512
    cols = da.shape[1]
    for n in range(0, 2 * cols, step):
        d, m = (da, n) if n < cols else (db, n - cols)
        made = dot32(hidden[0], d[:half, m : m + step]) + dot32(hidden[1], d[half:, m : m + step])
        own_out[:, n : n + step] = made[:own_rows].astype(jnp.bfloat16)
        cross_out[:, n : n + step] = made[own_rows:].astype(jnp.bfloat16)


def combine_kernel(first, idx, pick, own, cross, *refs):
    *more, out = refs
    width = own.shape[1]
    rows = slice(first, first + out.shape[0])
    step = 1024
    for n in range(0, width, step):
        cols = slice(n, n + step)
        got = contract(pick[...], jnp.concatenate([own[:, cols], cross[:, cols]], 0), 0, 0)[rows]
        for ref in more:
            got += ref[:, cols].astype(jnp.float32)
        out[:, cols] = got.astype(jnp.bfloat16)


def finish_kernel(half, idx, order, pick, own, cross, *refs):
    *more, out = refs
    width = own.shape[1]
    step = 1024
    for n in range(0, width, step):
        cols = slice(n, n + step)
        got = contract(pick[...], jnp.concatenate([own[:, cols], cross[:, cols]], 0), 0, 0)
        sums = [sum(r[:, cols].astype(jnp.float32) for r in part) for part in (more[:half], more[half:])]
        got = (got + jnp.concatenate(sums, 0)).astype(jnp.bfloat16)
        got = contract(order[...], got, 0, 0).astype(jnp.bfloat16)
        out[:, pl.ds(pl.multiple_of((idx[4] + n) % width, step), step)] = got


def fence_kernel(idx):
    pass


def call(kernel, outs, idx, token, args, passes=(), scratch=(), cost=1):
    vmem, anywhere = pl.BlockSpec(memory_space=pltpu.VMEM), pl.BlockSpec(memory_space=pl.ANY)
    through = [token, *passes]
    first = 1 + len(args)

    def body(*refs):
        ins, rest = refs[:first], refs[first + len(through) :]
        kernel(*ins, *rest[: len(outs)], *rest[len(outs) + len(through) :])

    got = pl.pallas_call(
        body,
        out_shape=[*outs, *(jax.ShapeDtypeStruct(x.shape, x.dtype) for x in through)],
        in_specs=[pl.BlockSpec(memory_space=pltpu.SMEM)] + [vmem] * len(args) + [anywhere] * len(through),
        out_specs=[vmem] * len(outs) + [anywhere] * len(through),
        input_output_aliases={first + i: len(outs) + i for i in range(len(through))},
        scratch_shapes=list(scratch),
        compiler_params=pltpu.CompilerParams(vmem_limit_bytes=LIMIT),
        cost_estimate=pl.CostEstimate(flops=1, bytes_accessed=cost, transcendentals=0),
    )(idx, *args, *through)
    return got[: len(outs)], got[len(outs)], got[len(outs) + 1 :]


ORDER = [
    ["prep", "EB", "MA", "EA", "+EB"],
    ["P1B", "Y1B", "+MA", "+wg"],
    ["f", "NB"],
    ["f", "OA", "+wd"],
    ["P0"],
    ["f", "Y0", "+wu"],
    ["F1B"],
    ["P1A", "Y1A", "QB"],
    ["f", "NA"],
    ["P2A", "Y2A"],
    ["F0"],
    ["f", "MB", "QA"],
    ["P3B", "Y3B"],
    ["F2A", "R2A"],
    ["P3A", "OB", "Y3A"],
    ["F3B"],
    ["C2A", "I2A", "R3B"],
    ["F3A"],
    ["C3B", "R3A", "X3B"],
    ["P2B", "Y2B"],
    ["D2A"],
    ["F1A", "S3B"],
    ["C3A", "I3A", "R1B"],
    ["F2B", "R2B"],
    ["D1B", "S1B", "R1A"],
    ["D3A", "S3A"],
    ["C2B", "I2B", "S2A", "+R1A", "R0", "+S3A"],
    ["D1A"],
    ["D2B", "S2B", "S1A", "+X3B"],
    ["fin"],
]


def lined(tokens, routes, route_weights, gate_weight, up_weight, down_weight):
    tok_rows, top_count = routes.shape
    width = tokens.shape[1]
    devices = lax.axis_size("expert")
    experts = devices // 2
    capacity = tok_rows * top_count // experts
    half = gate_weight.shape[1]
    index = lax.axis_index("expert")
    core, side, line = index % 2, index // 2 % 2, index // 4
    inner = ((line == 1) | (line == 2)).astype(jnp.int32)
    idx = jnp.stack(
        [core, 2 * line + side, 2 * line + 1 - side, inner, core * down_weight.shape[1], 1 - side]
    ).astype(jnp.int32)
    rows = tok_rows // 2
    total = width + LANES
    bf16 = jnp.bfloat16

    def like(*shape):
        return jax.ShapeDtypeStruct(shape, bf16)

    gate, up = gate_weight.T, up_weight.T

    val = {"wg": swapped(gate, "expert", 0), "wu": swapped(up, "expert", 0)}
    val["wd"] = swapped(down_weight, "expert", 0)
    steps = {name for name, *_ in ORDER}
    slots = {name[1:] for name in steps if name[0] == "P"}

    def kernel_of(name):
        kind, q = name[:-1], name[-1]
        if name == "prep":
            return (
                functools.partial(prepare_kernel, experts),
                [like(rows, total), like(rows, total), like(tok_rows, tok_rows)],
                [tokens, routes, route_weights],
                [],
            )
        if name[0] == "P":
            slot = name[1:]
            if slot in ("0", "1"):
                blocks, mode = [["payA", "payB"], ["EA", "EB"]][int(slot)], "both"
                own, cross, size = capacity, capacity, tok_rows
            else:
                blocks = {"1": ["E" + q], "2": ["M" + q, "O" + q], "3": ["N" + q, "Q" + q]}[slot[0]]
                mode = "one" if len(blocks) == 1 else "either"
                own, cross, size = rows, CROSS_ROWS, rows
            return (
                functools.partial(pick_kernel, experts, mode),
                [like(own, total), like(cross, total), like(own + cross, size)],
                [val[b] for b in blocks],
                [],
            )
        if name[0] == "F":
            own, cross = val["own" + name[1:]], val["Y" + name[1:]]
            weights = [gate, val["wg"], up, val["wu"], down_weight, val["wd"]]
            weights = [pltpu.with_memory_space_constraint(w, pltpu.VMEM) for w in weights]
            args = [own, cross, *weights]
            return (
                functools.partial(expert_kernel, experts),
                [like(own.shape[0], width), like(cross.shape[0], width)],
                args,
                [pltpu.VMEM((2, own.shape[0] + cross.shape[0], half), bf16)],
            )
        if name == "fin":
            made = [val["order"], val["pick0"], val["made0"], val["R0"]]
            made += [val[s + q] for q in "AB" for s in ("S1", "S2", "X3") if s + q in val]
            counts = [sum(s + q in val for s in ("S1", "S2", "X3")) for q in "AB"]
            return functools.partial(finish_kernel, counts[0]), [like(tok_rows, width)], made, []
        slot = name[1:] if name[1:] in slots else name[1]
        made = [val[s + slot] for s in ("pick", "made", "R")]
        made += [val[x] for x in {"D2": ["I2" + q], "D3": ["I3" + q], "D1": ["S3" + q]}.get(kind, [])]
        first = rows if slot == name[1] and q == "B" else 0
        return functools.partial(combine_kernel, first), [like(rows, width)], made, []

    def keep(name, got):
        slot = name[1:]
        if name == "prep":
            val["payA"], val["payB"], val["order"] = got
        elif name[0] == "P":
            val["own" + slot], val["cross" + slot], val["pick" + slot] = got
        elif name[0] == "F":
            val["made" + slot], val["back" + slot] = got
        else:
            val[name] = got[0]

    def move_of(name):
        kind, slot, q = name[0], name[1:], name[-1]
        if kind == "Y":
            return "cross" + slot, lambda x: swapped(x, "expert", 1)
        if kind == "R":
            return "back" + slot, lambda x: swapped(x, "expert", 1)
        source, pairs = {
            "E": ("pay" + q, OUTER),
            "M": ("pay" + q, MIDDLE),
            "O": ("M" + q, OUT),
            "N": ("E" + q, MIDDLE),
            "Q": ("N" + q, OUT),
            "I2": ("C2" + q, IN),
            "S2": ("D2" + q, MIDDLE),
            "X3": ("C3" + q, ENDS),
            "I3": ("C3" + q, IN),
            "S3": (("D3" if "D3" + q in steps else "C3") + q, MIDDLE),
            "S1": ("D1" + q, OUTER),
        }[name[:-1]]
        return source, lambda x: along_line(x, pairs)

    token = jnp.zeros((8, LANES), jnp.float32)
    for name, *moves in ORDER:
        done = [m[1:] for m in moves if m[0] == "+"]
        moves = [m for m in moves if m[0] != "+"]
        sources = {m: move_of(m)[0] for m in moves}
        passed = sorted({s for s in [*sources.values(), *done] if s in val})
        if name == "f":
            _, token, through = call(fence_kernel, [], idx, token, [], passes=[val[s] for s in passed])
        else:
            kernel, outs, args, scratch = kernel_of(name)
            cost = sum(x.size * x.dtype.itemsize for x in [*args, *outs]) if name[0] == "F" else 1
            through = [val[s] for s in passed]
            got, token, through = call(kernel, outs, idx, token, args, through, scratch, cost)
            keep(name, got)
        val.update(zip(passed, through))
        for m in moves:
            val[m] = move_of(m)[1](val[sources[m]])
    return val["fin"]


def solution(mesh):
    body = lined if mesh.shape["expert"] == 16 else dispatched
    return jax.shard_map(
        body,
        mesh=mesh,
        in_specs=(
            P(("groups", "expert"), None),
            P(("groups", "expert"), None),
            P(("groups", "expert"), None),
            P(None, "expert"),
            P(None, "expert"),
            P(None, "expert"),
        ),
        out_specs=P(("groups", "expert"), None),
        check_vma=False,
    )
```

```python
import functools

import jax
import jax.experimental.pallas as pl
import jax.experimental.pallas.tpu as pltpu
import jax.numpy as jnp
from jax import lax
from jax.sharding import PartitionSpec as P

CROSS_ROWS = 40
LANES = 128
LIMIT = 12 << 20


def swapped(x, axis, apart):
    return lax.ppermute(x, axis, [(i, i ^ 1 << apart) for i in range(lax.axis_size(axis))])


def dot32(a, b):
    return jnp.dot(a, b, preferred_element_type=jnp.float32)


def expert_hidden(rows, gate_part, up_part, parity):
    gate = dot32(rows, gate_part)
    upval = dot32(rows, up_part)
    hidden = (jax.nn.silu(gate) * upval).astype(jnp.bfloat16)
    partner = swapped(hidden, "expert", 0)
    return jnp.where(
        parity == 0, jnp.concatenate([hidden, partner], 1), jnp.concatenate([partner, hidden], 1)
    )


def dispatched(tokens, routes, route_weights, gate_weight, up_weight, down_weight):
    tok_rows, top_count = routes.shape
    width = tokens.shape[1]
    half_width = down_weight.shape[1]
    devices = lax.axis_size("expert")
    experts = devices // 2
    capacity = tok_rows * top_count // experts
    parity = lax.axis_index("expert") % 2
    flat = routes.reshape(-1)
    onehot = (flat[:, None] == jnp.arange(experts, dtype=jnp.int32)[None, :]).astype(jnp.int32)
    before = jnp.cumsum(onehot, axis=0) - onehot
    slot_of = jnp.sum(before * onehot, axis=1)
    position = flat * capacity + slot_of
    assign_ids = jnp.arange(flat.shape[0], dtype=jnp.int32) // top_count
    owner = jnp.zeros((experts * capacity,), jnp.int32).at[position].set(assign_ids)
    gathered = tokens[owner]
    outgoing = jnp.broadcast_to(
        gathered.reshape(experts, 1, capacity, width), (experts, 2, capacity, width)
    )
    outgoing = outgoing.reshape(devices, capacity, width)
    received = lax.all_to_all(outgoing, "expert", split_axis=0, concat_axis=0, tiled=True)
    count, items, _ = received.shape
    hidden = expert_hidden(received.reshape(count * items, width), gate_weight, up_weight, parity)
    produced = dot32(hidden, down_weight).astype(jnp.bfloat16)
    returned = lax.all_to_all(
        produced.reshape(count, items, half_width),
        "expert",
        split_axis=0,
        concat_axis=0,
        tiled=True,
    )
    returned = returned.reshape(experts, 2, capacity, half_width).transpose(0, 2, 1, 3)
    expert_rows = returned.reshape(experts * capacity, width)
    picked = expert_rows[position].reshape(tok_rows, top_count, width)
    mixed = jnp.einsum("tk,tkd->td", route_weights, picked.astype(jnp.float32))
    return mixed.astype(jnp.bfloat16)


def along_line(x, pairs):
    moves = [((a * 2 + s) * 2 + c, (b * 2 + s) * 2 + c) for a, b in pairs for s in (0, 1) for c in (0, 1)]
    return lax.ppermute(x, "expert", moves)


OUTER = [(0, 1), (1, 0), (2, 3), (3, 2)]
MIDDLE = [(1, 2), (2, 1)]
OUT = [(1, 0), (2, 3)]
IN = [(0, 1), (3, 2)]
ENDS = [(0, 3), (3, 0)]


def contract(a, b, da, db):
    return lax.dot_general(a, b, (((da,), (db,)), ((), ())), preferred_element_type=jnp.float32)


def iota(shape, dim):
    return lax.broadcasted_iota(jnp.int32, shape, dim)


def eye(n):
    return (iota((n, n), 0) == iota((n, n), 1)).astype(jnp.bfloat16)


def scale_of(ext, expert, experts):
    lane = iota(ext.shape, 1)
    mine = (lane % experts == expert) & (lane < 3 * experts)
    return jnp.sum(jnp.where(mine, ext.astype(jnp.float32), 0.0), axis=1, keepdims=True)


def prepare_kernel(experts, idx, tokens, routes, weights, *outs):
    rows, width = tokens.shape
    *chunks, order_out = outs
    size = rows // len(chunks)
    lane = iota((rows, LANES), 1)
    part = lane // experts
    full = jnp.zeros((rows, LANES), jnp.float32)
    for k in range(routes.shape[1]):
        full += jnp.where(lane % experts == routes[:, k : k + 1], weights[:, k : k + 1], 0.0)
    high = full.astype(jnp.bfloat16).astype(jnp.float32)
    mid = (full - high).astype(jnp.bfloat16).astype(jnp.float32)
    low = full - high - mid
    ext = jnp.where(part == 0, high, jnp.where(part == 1, mid, jnp.where(part == 2, low, 0.0)))
    ext = ext.astype(jnp.bfloat16)
    gray = jnp.zeros((rows, 1), jnp.int32)
    bit = jnp.zeros((rows, 1), jnp.int32)
    for z in range(experts // 2):
        named = jnp.zeros((rows, 1), jnp.int32)
        for k in range(routes.shape[1]):
            named += (routes[:, k : k + 1] == idx[5] + 2 * z).astype(jnp.int32)
        bit = bit ^ named
        gray = gray * 2 + bit
    down = jnp.broadcast_to(gray.astype(jnp.float32), (rows, rows))
    across = contract(down.astype(jnp.bfloat16), eye(rows), 0, 0)
    first, second = iota((rows, rows), 0), iota((rows, rows), 1)
    ahead = (down < across) | ((down == across) & (first < second))
    rank = jnp.sum(ahead.astype(jnp.float32), axis=0, keepdims=True).astype(jnp.int32)
    target = rank % len(chunks) * size + rank // len(chunks)
    order = (first == target).astype(jnp.bfloat16)
    order_out[...] = order
    ext = dot32(order, ext).astype(jnp.bfloat16)
    for q, chunk in enumerate(chunks):
        chunk[:, width:] = ext[q * size : (q + 1) * size]
    step = 1024
    for n in range(0, width, step):
        moved = dot32(order, tokens[:, n : n + step]).astype(jnp.bfloat16)
        for q, chunk in enumerate(chunks):
            chunk[:, n : n + step] = moved[q * size : (q + 1) * size]


def pick_kernel(experts, mode, idx, *refs):
    *blocks, own_out, cross_out, pick_out = refs
    total = blocks[0].shape[1]
    rows = blocks[0].shape[0] * (len(blocks) if mode == "both" else 1)
    own_rows, cross_rows = own_out.shape[0], cross_out.shape[0]
    inner = idx[3] == 1

    def load(cols):
        if mode == "both":
            return jnp.concatenate([b[:, cols] for b in blocks], 0)
        if mode == "either":
            return jnp.where(inner, blocks[0][:, cols], blocks[1][:, cols])
        return blocks[0][:, cols]

    ext = load(slice(total - LANES, total))

    def picks(expert, count):
        mask = jnp.broadcast_to(scale_of(ext, expert, experts) > 0, (rows, LANES)).astype(jnp.bfloat16)
        upto = (iota((rows, rows), 0) <= iota((rows, rows), 1)).astype(jnp.bfloat16)
        place = contract(mask, upto, 0, 0)[:count]
        named = contract(mask, eye(rows), 0, 0)[:count]
        slot = iota((count, rows), 0).astype(jnp.float32)
        return ((named > 0.5) & (place - 1.0 == slot)).astype(jnp.float32)

    own = picks(idx[1], own_rows) if mode == "both" else eye(rows).astype(jnp.float32)
    pick = jnp.concatenate([own, picks(idx[2], cross_rows)], 0).astype(jnp.bfloat16)
    pick_out[...] = pick
    step = total // 3
    for n in range(0, total, step):
        got = dot32(pick, load(slice(n, n + step)))
        own_out[:, n : n + step] = got[:own_rows].astype(jnp.bfloat16)
        cross_out[:, n : n + step] = got[own_rows:].astype(jnp.bfloat16)


def expert_kernel(experts, idx, own, cross, ga, gb, ua, ub, da, db, own_out, cross_out, hidden):
    own_rows, total = own.shape
    width = total - LANES
    core, expert = idx[0], idx[1]
    half = ga.shape[0]
    x = jnp.concatenate([own[:, :width], cross[:, :width]], 0)
    ext = jnp.concatenate([own[:, width:], cross[:, width:]], 0)
    scale = scale_of(ext, expert, experts)
    for place, g, u in ((core, ga, ua), (1 - core, gb, ub)):
        gate = contract(x, g[...], 1, 1)
        upval = contract(x, u[...], 1, 1)
        hidden[place] = (gate / (1.0 + jnp.exp(-gate)) * upval * scale).astype(jnp.bfloat16)
    step = 512
    cols = da.shape[1]
    for n in range(0, 2 * cols, step):
        d, m = (da, n) if n < cols else (db, n - cols)
        made = dot32(hidden[0], d[:half, m : m + step]) + dot32(hidden[1], d[half:, m : m + step])
        own_out[:, n : n + step] = made[:own_rows].astype(jnp.bfloat16)
        cross_out[:, n : n + step] = made[own_rows:].astype(jnp.bfloat16)


def combine_kernel(first, idx, pick, own, cross, *refs):
    *more, out = refs
    width = own.shape[1]
    rows = slice(first, first + out.shape[0])
    step = 1024
    for n in range(0, width, step):
        cols = slice(n, n + step)
        got = contract(pick[...], jnp.concatenate([own[:, cols], cross[:, cols]], 0), 0, 0)[rows]
        for ref in more:
            got += ref[:, cols].astype(jnp.float32)
        out[:, cols] = got.astype(jnp.bfloat16)


def finish_kernel(half, idx, order, pick, own, cross, *refs):
    *more, out = refs
    width = own.shape[1]
    step = 1024
    for n in range(0, width, step):
        cols = slice(n, n + step)
        got = contract(pick[...], jnp.concatenate([own[:, cols], cross[:, cols]], 0), 0, 0)
        sums = [sum(r[:, cols].astype(jnp.float32) for r in part) for part in (more[:half], more[half:])]
        got = (got + jnp.concatenate(sums, 0)).astype(jnp.bfloat16)
        got = contract(order[...], got, 0, 0).astype(jnp.bfloat16)
        out[:, pl.ds(pl.multiple_of((idx[4] + n) % width, step), step)] = got


def fence_kernel(idx):
    pass


def fetch_kernel(count, idx, *refs):
    sems = refs[-1]
    copies = [pltpu.make_async_copy(refs[i], refs[count + i], sems.at[i]) for i in range(count)]
    for c in copies:
        c.start()
    for c in copies:
        c.wait()


def call(kernel, outs, idx, token, args, passes=(), scratch=(), cost=1, left=False):
    vmem, anywhere = pl.BlockSpec(memory_space=pltpu.VMEM), pl.BlockSpec(memory_space=pl.ANY)
    through = [token, *passes]
    first = 1 + len(args)

    def body(*refs):
        ins, rest = refs[:first], refs[first + len(through) :]
        kernel(*ins, *rest[: len(outs)], *rest[len(outs) + len(through) :])

    got = pl.pallas_call(
        body,
        out_shape=[*outs, *(jax.ShapeDtypeStruct(x.shape, x.dtype) for x in through)],
        in_specs=[pl.BlockSpec(memory_space=pltpu.SMEM)]
        + [anywhere if left else vmem] * len(args)
        + [anywhere] * len(through),
        out_specs=[vmem] * len(outs) + [anywhere] * len(through),
        input_output_aliases={first + i: len(outs) + i for i in range(len(through))},
        scratch_shapes=list(scratch),
        compiler_params=pltpu.CompilerParams(vmem_limit_bytes=LIMIT),
        cost_estimate=pl.CostEstimate(flops=1, bytes_accessed=cost, transcendentals=0),
    )(idx, *args, *through)
    return got[: len(outs)], got[len(outs)], got[len(outs) + 1 :]


ORDER = [
    ["prep", "EA", "MB", "EB", "+EA"],
    ["P0", "+EA", "+MB"],
    ["f", "NA", "Y0"],
    ["W", "OB"],
    ["P1", "Y1", "QA"],
    ["f", "NB"],
    ["F0", "MA"],
    ["P2B", "Y2B"],
    ["f", "QB", "+Y1"],
    ["P3A", "Y3A"],
    ["F2B", "R2B"],
    ["F3A", "R3A", "OA", "+QB"],
    ["C2B"],
    ["P3B", "I2B", "Y3B"],
    ["C3A", "S3A"],
    ["P2A", "Y2A", "X3A", "+Y3B"],
    ["F3B", "R3B", "+I2B", "+Y2A"],
    ["F2A"],
    ["C3B", "X3B", "R2A", "+S3A", "+Y1"],
    ["F1", "+X3A"],
    ["D2B", "R1"],
    ["C2A", "S3B", "I2A", "+S3A"],
    ["D1A", "S1A", "S2B", "+S3B", "+X3B"],
    ["D1B", "S1B", "+I2A"],
    ["D2A"],
    ["f", "S2A", "R0", "+X3A", "+X3B"],
    ["fin"],
]


def lined(tokens, routes, route_weights, gate_weight, up_weight, down_weight):
    tok_rows, top_count = routes.shape
    width = tokens.shape[1]
    devices = lax.axis_size("expert")
    experts = devices // 2
    capacity = tok_rows * top_count // experts
    half = gate_weight.shape[1]
    index = lax.axis_index("expert")
    core, side, line = index % 2, index // 2 % 2, index // 4
    inner = ((line == 1) | (line == 2)).astype(jnp.int32)
    idx = jnp.stack(
        [core, 2 * line + side, 2 * line + 1 - side, inner, core * down_weight.shape[1], 1 - side]
    ).astype(jnp.int32)
    rows = tok_rows // 2
    total = width + LANES
    bf16 = jnp.bfloat16

    def like(*shape):
        return jax.ShapeDtypeStruct(shape, bf16)

    gate, up = gate_weight.T, up_weight.T

    val = {"wg": swapped(gate, "expert", 0), "wu": swapped(up, "expert", 0)}
    val["wd"] = swapped(down_weight, "expert", 0)
    steps = {name for name, *_ in ORDER}
    slots = {name[1:] for name in steps if name[0] == "P"}

    def kernel_of(name):
        kind, q = name[:-1], name[-1]
        if name == "prep":
            return (
                functools.partial(prepare_kernel, experts),
                [like(rows, total), like(rows, total), like(tok_rows, tok_rows)],
                [tokens, routes, route_weights],
                [],
            )
        if name[0] == "P":
            slot = name[1:]
            if slot in ("0", "1"):
                blocks, mode = [["payA", "payB"], ["EA", "EB"]][int(slot)], "both"
                own, cross, size = capacity, capacity, tok_rows
            else:
                blocks = {"1": ["E" + q], "2": ["M" + q, "O" + q], "3": ["N" + q, "Q" + q]}[slot[0]]
                mode = "one" if len(blocks) == 1 else "either"
                own, cross, size = rows, CROSS_ROWS, rows
            return (
                functools.partial(pick_kernel, experts, mode),
                [like(own, total), like(cross, total), like(own + cross, size)],
                [val[b] for b in blocks],
                [],
            )
        if name[0] == "F":
            own, cross = val["own" + name[1:]], val["Y" + name[1:]]
            weights = [gate, val["vg"], up, val["vu"], down_weight, val["vd"]]
            weights = [pltpu.with_memory_space_constraint(w, pltpu.VMEM) for w in weights]
            args = [own, cross, *weights]
            return (
                functools.partial(expert_kernel, experts),
                [like(own.shape[0], width), like(cross.shape[0], width)],
                args,
                [pltpu.VMEM((2, own.shape[0] + cross.shape[0], half), bf16)],
            )
        if name == "W":
            args = [val["wg"], val["wu"], val["wd"]]
            outs = [pltpu.VMEM(w.shape, w.dtype) for w in args]
            return functools.partial(fetch_kernel, 3), outs, args, [pltpu.SemaphoreType.DMA((3,))]
        if name == "fin":
            made = [val["order"], val["pick0"], val["made0"], val["R0"]]
            made += [val[s + q] for q in "AB" for s in ("S1", "S2", "X3") if s + q in val]
            counts = [sum(s + q in val for s in ("S1", "S2", "X3")) for q in "AB"]
            return functools.partial(finish_kernel, counts[0]), [like(tok_rows, width)], made, []
        slot = name[1:] if name[1:] in slots else name[1]
        made = [val[s + slot] for s in ("pick", "made", "R")]
        made += [val[x] for x in {"D2": ["I2" + q], "D3": ["I3" + q], "D1": ["S3" + q]}.get(kind, [])]
        first = rows if slot == name[1] and q == "B" else 0
        return functools.partial(combine_kernel, first), [like(rows, width)], made, []

    def keep(name, got):
        slot = name[1:]
        if name == "prep":
            val["payA"], val["payB"], val["order"] = got
        elif name[0] == "P":
            val["own" + slot], val["cross" + slot], val["pick" + slot] = got
        elif name == "W":
            val["vg"], val["vu"], val["vd"] = got
        elif name[0] == "F":
            val["made" + slot], val["back" + slot] = got
        else:
            val[name] = got[0]

    def move_of(name):
        kind, slot, q = name[0], name[1:], name[-1]
        if kind == "Y":
            return "cross" + slot, lambda x: swapped(x, "expert", 1)
        if kind == "R":
            return "back" + slot, lambda x: swapped(x, "expert", 1)
        source, pairs = {
            "E": ("pay" + q, OUTER),
            "M": ("pay" + q, MIDDLE),
            "O": ("M" + q, OUT),
            "N": ("E" + q, MIDDLE),
            "Q": ("N" + q, OUT),
            "I2": ("C2" + q, IN),
            "S2": ("D2" + q, MIDDLE),
            "X3": ("C3" + q, ENDS),
            "I3": ("C3" + q, IN),
            "S3": (("D3" if "D3" + q in steps else "C3") + q, MIDDLE),
            "S1": ("D1" + q, OUTER),
        }[name[:-1]]
        return source, lambda x: along_line(x, pairs)

    token = jnp.zeros((8, LANES), jnp.float32)
    for name, *moves in ORDER:
        done = [m[1:] for m in moves if m[0] == "+"]
        moves = [m for m in moves if m[0] != "+"]
        sources = {m: move_of(m)[0] for m in moves}
        passed = sorted({s for s in [*sources.values(), *done] if s in val})
        if name == "f":
            _, token, through = call(fence_kernel, [], idx, token, [], passes=[val[s] for s in passed])
        else:
            kernel, outs, args, scratch = kernel_of(name)
            cost = sum(x.size * x.dtype.itemsize for x in [*args, *outs]) if name[0] == "F" else 1
            through = [val[s] for s in passed]
            got, token, through = call(kernel, outs, idx, token, args, through, scratch, cost, name == "W")
            keep(name, got)
        val.update(zip(passed, through))
        for m in moves:
            val[m] = move_of(m)[1](val[sources[m]])
    return val["fin"]


def solution(mesh):
    body = lined if mesh.shape["expert"] == 16 else dispatched
    return jax.shard_map(
        body,
        mesh=mesh,
        in_specs=(
            P(("groups", "expert"), None),
            P(("groups", "expert"), None),
            P(("groups", "expert"), None),
            P(None, "expert"),
            P(None, "expert"),
            P(None, "expert"),
        ),
        out_specs=P(("groups", "expert"), None),
        check_vma=False,
    )
```

```python
import functools

import jax
import jax.experimental.pallas as pl
import jax.experimental.pallas.tpu as pltpu
import jax.numpy as jnp
from jax import lax
from jax.sharding import PartitionSpec as P

CROSS_ROWS = 40
LANES = 128
LIMIT = 12 << 20


def swapped(x, axis, apart):
    return lax.ppermute(x, axis, [(i, i ^ 1 << apart) for i in range(lax.axis_size(axis))])


def dot32(a, b):
    return jnp.dot(a, b, preferred_element_type=jnp.float32)


def expert_hidden(rows, gate_part, up_part, parity):
    gate = dot32(rows, gate_part)
    upval = dot32(rows, up_part)
    hidden = (jax.nn.silu(gate) * upval).astype(jnp.bfloat16)
    partner = swapped(hidden, "expert", 0)
    return jnp.where(
        parity == 0, jnp.concatenate([hidden, partner], 1), jnp.concatenate([partner, hidden], 1)
    )


def dispatched(tokens, routes, route_weights, gate_weight, up_weight, down_weight):
    tok_rows, top_count = routes.shape
    width = tokens.shape[1]
    half_width = down_weight.shape[1]
    devices = lax.axis_size("expert")
    experts = devices // 2
    capacity = tok_rows * top_count // experts
    parity = lax.axis_index("expert") % 2
    flat = routes.reshape(-1)
    onehot = (flat[:, None] == jnp.arange(experts, dtype=jnp.int32)[None, :]).astype(jnp.int32)
    before = jnp.cumsum(onehot, axis=0) - onehot
    slot_of = jnp.sum(before * onehot, axis=1)
    position = flat * capacity + slot_of
    assign_ids = jnp.arange(flat.shape[0], dtype=jnp.int32) // top_count
    owner = jnp.zeros((experts * capacity,), jnp.int32).at[position].set(assign_ids)
    gathered = tokens[owner]
    outgoing = jnp.broadcast_to(
        gathered.reshape(experts, 1, capacity, width), (experts, 2, capacity, width)
    )
    outgoing = outgoing.reshape(devices, capacity, width)
    received = lax.all_to_all(outgoing, "expert", split_axis=0, concat_axis=0, tiled=True)
    count, items, _ = received.shape
    hidden = expert_hidden(received.reshape(count * items, width), gate_weight, up_weight, parity)
    produced = dot32(hidden, down_weight).astype(jnp.bfloat16)
    returned = lax.all_to_all(
        produced.reshape(count, items, half_width),
        "expert",
        split_axis=0,
        concat_axis=0,
        tiled=True,
    )
    returned = returned.reshape(experts, 2, capacity, half_width).transpose(0, 2, 1, 3)
    expert_rows = returned.reshape(experts * capacity, width)
    picked = expert_rows[position].reshape(tok_rows, top_count, width)
    mixed = jnp.einsum("tk,tkd->td", route_weights, picked.astype(jnp.float32))
    return mixed.astype(jnp.bfloat16)


def along_line(x, pairs):
    moves = [((a * 2 + s) * 2 + c, (b * 2 + s) * 2 + c) for a, b in pairs for s in (0, 1) for c in (0, 1)]
    return lax.ppermute(x, "expert", moves)


OUTER = [(0, 1), (1, 0), (2, 3), (3, 2)]
MIDDLE = [(1, 2), (2, 1)]
OUT = [(1, 0), (2, 3)]
IN = [(0, 1), (3, 2)]
ENDS = [(0, 3), (3, 0)]


def contract(a, b, da, db):
    return lax.dot_general(a, b, (((da,), (db,)), ((), ())), preferred_element_type=jnp.float32)


def iota(shape, dim):
    return lax.broadcasted_iota(jnp.int32, shape, dim)


def eye(n):
    return (iota((n, n), 0) == iota((n, n), 1)).astype(jnp.bfloat16)


def scale_of(ext, expert, experts):
    lane = iota(ext.shape, 1)
    mine = (lane % experts == expert) & (lane < 3 * experts)
    return jnp.sum(jnp.where(mine, ext.astype(jnp.float32), 0.0), axis=1, keepdims=True)


def prepare_kernel(experts, idx, routes, weights, tokens, *refs):
    *chunks, order_out, held, sem = refs
    fetch = pltpu.make_async_copy(tokens, held, sem)
    fetch.start()
    rows, width = tokens.shape
    size = rows // len(chunks)
    f32, bf16 = jnp.float32, jnp.bfloat16
    full = jnp.zeros((experts, rows), f32)
    for k in range(routes.shape[0]):
        full += jnp.where(iota((experts, rows), 0) == routes[k : k + 1], weights[k : k + 1], 0.0)
    high = full.astype(bf16).astype(f32)
    mid = (full - high).astype(bf16).astype(f32)
    parts = jnp.concatenate([high, mid, full - high - mid], 0).astype(bf16)
    spread = (iota((3 * experts, LANES), 0) == iota((3 * experts, LANES), 1)).astype(bf16)
    ext = contract(parts, spread, 0, 0).astype(bf16)
    gray = jnp.zeros((1, rows), jnp.int32)
    bit = jnp.zeros((1, rows), jnp.int32)
    for z in range(experts // 2):
        named = jnp.zeros((1, rows), jnp.int32)
        for k in range(routes.shape[0]):
            named += (routes[k : k + 1] == idx[5] + 2 * z).astype(jnp.int32)
        bit = bit ^ named
        gray = gray * 2 + bit
    across = jnp.broadcast_to(gray.astype(f32), (rows, rows))
    first, second = iota((rows, rows), 0), iota((rows, rows), 1)
    top = jnp.where(first[:8] == 0, across[:8], 0.0).astype(bf16)
    down = contract(top, jnp.ones((8, rows), bf16), 0, 0)
    ahead = (down < across) | ((down == across) & (first < second))
    rank = jnp.sum(ahead.astype(f32), axis=0, keepdims=True).astype(jnp.int32)
    target = rank % len(chunks) * size + rank // len(chunks)
    order = (first == target).astype(bf16)
    order_out[...] = order
    ext = dot32(order, ext).astype(bf16)
    for q, chunk in enumerate(chunks):
        chunk[:, width:] = ext[q * size : (q + 1) * size]
    fetch.wait()
    step = 1024
    for n in range(0, width, step):
        moved = dot32(order, held[:, n : n + step]).astype(bf16)
        for q, chunk in enumerate(chunks):
            chunk[:, n : n + step] = moved[q * size : (q + 1) * size]


def pick_kernel(experts, mode, idx, *refs):
    *blocks, own_out, cross_out, pick_out = refs
    total = blocks[0].shape[1]
    rows = blocks[0].shape[0] * (len(blocks) if mode == "both" else 1)
    own_rows, cross_rows = own_out.shape[0], cross_out.shape[0]
    inner = idx[3] == 1

    def load(cols):
        if mode == "both":
            return jnp.concatenate([b[:, cols] for b in blocks], 0)
        if mode == "either":
            return jnp.where(inner, blocks[0][:, cols], blocks[1][:, cols])
        return blocks[0][:, cols]

    ext = load(slice(total - LANES, total))

    def picks(expert, count):
        mask = jnp.broadcast_to(scale_of(ext, expert, experts) > 0, (rows, LANES)).astype(jnp.bfloat16)
        upto = (iota((rows, rows), 0) <= iota((rows, rows), 1)).astype(jnp.bfloat16)
        place = contract(mask, upto, 0, 0)[:count]
        named = contract(mask, eye(rows), 0, 0)[:count]
        slot = iota((count, rows), 0).astype(jnp.float32)
        return ((named > 0.5) & (place - 1.0 == slot)).astype(jnp.float32)

    own = picks(idx[1], own_rows) if mode == "both" else eye(rows).astype(jnp.float32)
    pick = jnp.concatenate([own, picks(idx[2], cross_rows)], 0).astype(jnp.bfloat16)
    pick_out[...] = pick
    step = total // 3
    for n in range(0, total, step):
        got = dot32(pick, load(slice(n, n + step)))
        own_out[:, n : n + step] = got[:own_rows].astype(jnp.bfloat16)
        cross_out[:, n : n + step] = got[own_rows:].astype(jnp.bfloat16)


def expert_kernel(experts, idx, own, cross, ga, gb, ua, ub, da, db, own_out, cross_out, hidden):
    own_rows, total = own.shape
    width = total - LANES
    core, expert = idx[0], idx[1]
    half = ga.shape[0]
    x = jnp.concatenate([own[:, :width], cross[:, :width]], 0)
    ext = jnp.concatenate([own[:, width:], cross[:, width:]], 0)
    scale = scale_of(ext, expert, experts)
    for place, g, u in ((core, ga, ua), (1 - core, gb, ub)):
        gate = contract(x, g[...], 1, 1)
        upval = contract(x, u[...], 1, 1)
        hidden[place] = (gate / (1.0 + jnp.exp(-gate)) * upval * scale).astype(jnp.bfloat16)
    step = 512
    cols = da.shape[1]
    for n in range(0, 2 * cols, step):
        d, m = (da, n) if n < cols else (db, n - cols)
        made = dot32(hidden[0], d[:half, m : m + step]) + dot32(hidden[1], d[half:, m : m + step])
        own_out[:, n : n + step] = made[:own_rows].astype(jnp.bfloat16)
        cross_out[:, n : n + step] = made[own_rows:].astype(jnp.bfloat16)


def combine_kernel(first, idx, pick, own, cross, *refs):
    *more, out = refs
    width = own.shape[1]
    rows = slice(first, first + out.shape[0])
    step = 1024
    for n in range(0, width, step):
        cols = slice(n, n + step)
        got = contract(pick[...], jnp.concatenate([own[:, cols], cross[:, cols]], 0), 0, 0)[rows]
        for ref in more:
            got += ref[:, cols].astype(jnp.float32)
        out[:, cols] = got.astype(jnp.bfloat16)


def finish_kernel(half, idx, order, pick, own, cross, *refs):
    *more, out = refs
    width = own.shape[1]
    step = 1024
    for n in range(0, width, step):
        cols = slice(n, n + step)
        got = contract(pick[...], jnp.concatenate([own[:, cols], cross[:, cols]], 0), 0, 0)
        sums = [sum(r[:, cols].astype(jnp.float32) for r in part) for part in (more[:half], more[half:])]
        got = (got + jnp.concatenate(sums, 0)).astype(jnp.bfloat16)
        got = contract(order[...], got, 0, 0).astype(jnp.bfloat16)
        out[:, pl.ds(pl.multiple_of((idx[4] + n) % width, step), step)] = got


def fence_kernel(idx):
    pass


def run_copies(sems, pairs):
    copies = [pltpu.make_async_copy(s, d, sems.at[i]) for i, (s, d) in enumerate(pairs)]
    for c in copies:
        c.start()
    for c in copies:
        c.wait()


def fetch_kernel(idx, *refs):
    count = len(refs) // 2
    run_copies(refs[-1], zip(refs[:count], refs[count:-1]))


def call(name, kernel, outs, idx, token, args, passes=(), scratch=(), cost=1, left=()):
    vmem, anywhere = pl.BlockSpec(memory_space=pltpu.VMEM), pl.BlockSpec(memory_space=pl.ANY)
    through = [token, *passes]
    first = 1 + len(args) + len(left)

    def body(*refs):
        ins, rest = refs[:first], refs[first + len(through) :]
        kernel(*ins, *rest[: len(outs)], *rest[len(outs) + len(through) :])

    got = pl.pallas_call(
        body,
        out_shape=[*outs, *(jax.ShapeDtypeStruct(x.shape, x.dtype) for x in through)],
        in_specs=[pl.BlockSpec(memory_space=pltpu.SMEM)]
        + [vmem] * len(args)
        + [anywhere] * len(left)
        + [anywhere] * len(through),
        out_specs=[vmem] * len(outs) + [anywhere] * len(through),
        input_output_aliases={first + i: len(outs) + i for i in range(len(through))},
        scratch_shapes=list(scratch),
        name=name,
        compiler_params=pltpu.CompilerParams(vmem_limit_bytes=LIMIT),
        cost_estimate=pl.CostEstimate(flops=1, bytes_accessed=cost, transcendentals=0),
    )(idx, *args, *left, *through)
    return got[: len(outs)], got[len(outs)], got[len(outs) + 1 :]


ORDER = [
    ["prep", "EB", "EA", "MA"],
    ["P0", "NA", "+MA"],
    ["P1A", "Y1A", "OA", "+wu"],
    ["W", "Y0"],
    ["P1B"],
    ["f", "NB", "+NA", "+Y1A"],
    ["P2A", "MB", "Y2A", "+Y1A", "QA"],
    ["F1A"],
    ["f", "+Y0"],
    ["P3A", "QB", "Y3A"],
    ["F2A", "R2A"],
    ["F3A", "R3A", "OB"],
    ["P3B", "Y3B", "+R2A"],
    ["F0"],
    ["C2A"],
    ["C3A", "I3A"],
    ["P2B", "Y2B"],
    ["F3B", "R3B", "I2A"],
    ["D3A", "S3A", "Y1B", "+Y2B"],
    ["C3B", "X3B"],
    ["F2B", "R2B"],
    ["D2A", "+S3A", "+Y1B"],
    ["C2B", "R1A", "S3B", "I2B", "+Y1B"],
    ["F1B"],
    ["f", "R1B", "S2A", "+R1A", "+S3A", "+R2B"],
    ["D1A", "S1A"],
    ["D1B", "S1B", "+I2B"],
    ["D2B", "S2B", "R0", "+X3B"],
    ["fin"],
]


def lined(tokens, routes, route_weights, gate_weight, up_weight, down_weight):
    tok_rows, top_count = routes.shape
    width = tokens.shape[1]
    devices = lax.axis_size("expert")
    experts = devices // 2
    capacity = tok_rows * top_count // experts
    half = gate_weight.shape[1]
    index = lax.axis_index("expert")
    core, side, line = index % 2, index // 2 % 2, index // 4
    inner = ((line == 1) | (line == 2)).astype(jnp.int32)
    idx = jnp.stack(
        [core, 2 * line + side, 2 * line + 1 - side, inner, core * down_weight.shape[1], 1 - side]
    ).astype(jnp.int32)
    rows = tok_rows // 2
    total = width + LANES
    bf16 = jnp.bfloat16

    def like(*shape):
        return jax.ShapeDtypeStruct(shape, bf16)

    gate, up = gate_weight.T, up_weight.T

    val = {}
    for name, w in (("wg", gate), ("wu", up), ("wd", down_weight)):
        with jax.named_scope("move_" + name):
            val[name] = swapped(w, "expert", 0)
    steps = {name for name, *_ in ORDER}
    slots = {name[1:] for name in steps if name[0] == "P"}

    def kernel_of(name):
        kind, q = name[:-1], name[-1]
        if name == "prep":
            return (
                functools.partial(prepare_kernel, experts),
                [like(rows, total), like(rows, total), like(tok_rows, tok_rows)],
                [routes.T, route_weights.T],
                [pltpu.VMEM(tokens.shape, bf16), pltpu.SemaphoreType.DMA],
            )
        if name[0] == "P":
            slot = name[1:]
            if slot in ("0", "1"):
                blocks, mode = [["payA", "payB"], ["EA", "EB"]][int(slot)], "both"
                own, cross, size = capacity, capacity, tok_rows
            else:
                blocks = {"1": ["E" + q], "2": ["M" + q, "O" + q], "3": ["N" + q, "Q" + q]}[slot[0]]
                mode = "one" if len(blocks) == 1 else "either"
                own, cross, size = rows, CROSS_ROWS, rows
            return (
                functools.partial(pick_kernel, experts, mode),
                [like(own, total), like(cross, total), like(own + cross, size)],
                [val[b] for b in blocks],
                [],
            )
        if name[0] == "F":
            own, cross = val["own" + name[1:]], val["Y" + name[1:]]
            weights = [gate, val["vg"], up, val["vu"], down_weight, val["vd"]]
            weights = [pltpu.with_memory_space_constraint(w, pltpu.VMEM) for w in weights]
            args = [own, cross, *weights]
            return (
                functools.partial(expert_kernel, experts),
                [like(own.shape[0], width), like(cross.shape[0], width)],
                args,
                [pltpu.VMEM((2, own.shape[0] + cross.shape[0], half), bf16)],
            )
        if name == "W":
            outs = [pltpu.VMEM(w.shape, bf16) for w in (gate, up, down_weight)]
            return fetch_kernel, outs, [], [pltpu.SemaphoreType.DMA((3,))]
        if name == "fin":
            made = [val["order"], val["pick0"], val["made0"], val["R0"]]
            made += [val[s + q] for q in "AB" for s in ("S1", "S2", "X3") if s + q in val]
            counts = [sum(s + q in val for s in ("S1", "S2", "X3")) for q in "AB"]
            return functools.partial(finish_kernel, counts[0]), [like(tok_rows, width)], made, []
        slot = name[1:] if name[1:] in slots else name[1]
        made = [val[s + slot] for s in ("pick", "made", "R")]
        made += [val[x] for x in {"D2": ["I2" + q], "D3": ["I3" + q], "D1": ["S3" + q]}.get(kind, [])]
        first = rows if slot == name[1] and q == "B" else 0
        return functools.partial(combine_kernel, first), [like(rows, width)], made, []

    def keep(name, got):
        slot = name[1:]
        if name == "prep":
            val["payA"], val["payB"], val["order"] = got
        elif name[0] == "P":
            val["own" + slot], val["cross" + slot], val["pick" + slot] = got
        elif name == "W":
            val["vg"], val["vu"], val["vd"] = got
        elif name[0] == "F":
            val["made" + slot], val["back" + slot] = got
        else:
            val[name] = got[0]

    def move_of(name):
        kind, slot, q = name[0], name[1:], name[-1]
        if kind == "Y":
            return "cross" + slot, lambda x: swapped(x, "expert", 1)
        if kind == "R":
            return "back" + slot, lambda x: swapped(x, "expert", 1)
        source, pairs = {
            "E": ("pay" + q, OUTER),
            "M": ("pay" + q, MIDDLE),
            "O": ("M" + q, OUT),
            "N": ("E" + q, MIDDLE),
            "Q": ("N" + q, OUT),
            "I2": ("C2" + q, IN),
            "S2": ("D2" + q, MIDDLE),
            "X3": ("C3" + q, ENDS),
            "I3": ("C3" + q, IN),
            "S3": (("D3" if "D3" + q in steps else "C3") + q, MIDDLE),
            "S1": ("D1" + q, OUTER),
        }[name[:-1]]
        return source, lambda x: along_line(x, pairs)

    token = jnp.zeros((8, LANES), jnp.float32)
    for name, *moves in ORDER:
        done = [m[1:] for m in moves if m[0] == "+"]
        moves = [m for m in moves if m[0] != "+"]
        sources = {m: move_of(m)[0] for m in moves}
        passed = sorted({s for s in [*sources.values(), *done] if s in val})
        if name == "f":
            _, token, through = call("fence", fence_kernel, [], idx, token, [], passes=[val[s] for s in passed])
        else:
            kernel, outs, args, scratch = kernel_of(name)
            cost = sum(x.size * x.dtype.itemsize for x in [*args, *outs]) if name[0] == "F" else 1
            through = [val[s] for s in passed]
            left = {"prep": [tokens], "W": [val["wg"], val["wu"], val["wd"]]}.get(name, [])
            got, token, through = call(name, kernel, outs, idx, token, args, through, scratch, cost, left)
            keep(name, got)
        val.update(zip(passed, through))
        for m in moves:
            with jax.named_scope("move_" + m):
                val[m] = move_of(m)[1](val[sources[m]])
    return val["fin"]


def solution(mesh):
    body = lined if mesh.shape["expert"] == 16 else dispatched
    return jax.shard_map(
        body,
        mesh=mesh,
        in_specs=(
            P(("groups", "expert"), None),
            P(("groups", "expert"), None),
            P(("groups", "expert"), None),
            P(None, "expert"),
            P(None, "expert"),
            P(None, "expert"),
        ),
        out_specs=P(("groups", "expert"), None),
        check_vma=False,
    )
```

```python
import functools

import jax
import jax.experimental.pallas as pl
import jax.experimental.pallas.tpu as pltpu
import jax.numpy as jnp
from jax import lax
from jax.sharding import PartitionSpec as P

CROSS_ROWS = 40
LANES = 128
STEP = 1024
LIMIT = 12 << 20


def swapped(x, axis, apart):
    return lax.ppermute(x, axis, [(i, i ^ 1 << apart) for i in range(lax.axis_size(axis))])


def dot32(a, b):
    return jnp.dot(a, b, preferred_element_type=jnp.float32)


def expert_hidden(rows, gate_part, up_part, parity):
    gate = dot32(rows, gate_part)
    upval = dot32(rows, up_part)
    hidden = (jax.nn.silu(gate) * upval).astype(jnp.bfloat16)
    partner = swapped(hidden, "expert", 0)
    return jnp.where(
        parity == 0, jnp.concatenate([hidden, partner], 1), jnp.concatenate([partner, hidden], 1)
    )


def dispatched(tokens, routes, route_weights, gate_weight, up_weight, down_weight):
    tok_rows, top_count = routes.shape
    width = tokens.shape[1]
    half_width = down_weight.shape[1]
    devices = lax.axis_size("expert")
    experts = devices // 2
    capacity = tok_rows * top_count // experts
    parity = lax.axis_index("expert") % 2
    flat = routes.reshape(-1)
    onehot = (flat[:, None] == jnp.arange(experts, dtype=jnp.int32)[None, :]).astype(jnp.int32)
    before = jnp.cumsum(onehot, axis=0) - onehot
    slot_of = jnp.sum(before * onehot, axis=1)
    position = flat * capacity + slot_of
    assign_ids = jnp.arange(flat.shape[0], dtype=jnp.int32) // top_count
    owner = jnp.zeros((experts * capacity,), jnp.int32).at[position].set(assign_ids)
    gathered = tokens[owner]
    outgoing = jnp.broadcast_to(
        gathered.reshape(experts, 1, capacity, width), (experts, 2, capacity, width)
    )
    outgoing = outgoing.reshape(devices, capacity, width)
    received = lax.all_to_all(outgoing, "expert", split_axis=0, concat_axis=0, tiled=True)
    count, items, _ = received.shape
    hidden = expert_hidden(received.reshape(count * items, width), gate_weight, up_weight, parity)
    produced = dot32(hidden, down_weight).astype(jnp.bfloat16)
    returned = lax.all_to_all(
        produced.reshape(count, items, half_width),
        "expert",
        split_axis=0,
        concat_axis=0,
        tiled=True,
    )
    returned = returned.reshape(experts, 2, capacity, half_width).transpose(0, 2, 1, 3)
    expert_rows = returned.reshape(experts * capacity, width)
    picked = expert_rows[position].reshape(tok_rows, top_count, width)
    mixed = jnp.einsum("tk,tkd->td", route_weights, picked.astype(jnp.float32))
    return mixed.astype(jnp.bfloat16)


def along_line(x, pairs):
    moves = [((a * 2 + s) * 2 + c, (b * 2 + s) * 2 + c) for a, b in pairs for s in (0, 1) for c in (0, 1)]
    return lax.ppermute(x, "expert", moves)


OUTER = [(0, 1), (1, 0), (2, 3), (3, 2)]
MIDDLE = [(1, 2), (2, 1)]
OUT = [(1, 0), (2, 3)]
IN = [(0, 1), (3, 2)]
ENDS = [(0, 3), (3, 0)]


def contract(a, b, da, db):
    return lax.dot_general(a, b, (((da,), (db,)), ((), ())), preferred_element_type=jnp.float32)


def iota(shape, dim):
    return lax.broadcasted_iota(jnp.int32, shape, dim)


def eye(n):
    return (iota((n, n), 0) == iota((n, n), 1)).astype(jnp.bfloat16)


def scale_of(ext, expert, experts):
    lane = iota(ext.shape, 1)
    mine = (lane % experts == expert) & (lane < 3 * experts)
    return jnp.sum(jnp.where(mine, ext.astype(jnp.float32), 0.0), axis=1, keepdims=True)


def prepare_kernel(experts, idx, routes, weights, tokens, *refs):
    *chunks, order_out, held, sem = refs
    fetch = pltpu.make_async_copy(tokens, held, sem)
    fetch.start()
    rows, width = tokens.shape
    size = rows // len(chunks)
    f32, bf16 = jnp.float32, jnp.bfloat16
    full = jnp.zeros((experts, rows), f32)
    for k in range(routes.shape[0]):
        full += jnp.where(iota((experts, rows), 0) == routes[k : k + 1], weights[k : k + 1], 0.0)
    high = full.astype(bf16).astype(f32)
    mid = (full - high).astype(bf16).astype(f32)
    parts = jnp.concatenate([high, mid, full - high - mid], 0).astype(bf16)
    spread = (iota((3 * experts, LANES), 0) == iota((3 * experts, LANES), 1)).astype(bf16)
    ext = contract(parts, spread, 0, 0).astype(bf16)
    gray = jnp.zeros((1, rows), jnp.int32)
    bit = jnp.zeros((1, rows), jnp.int32)
    for z in range(experts // 2):
        named = jnp.zeros((1, rows), jnp.int32)
        for k in range(routes.shape[0]):
            named += (routes[k : k + 1] == idx[5] + 2 * z).astype(jnp.int32)
        bit = bit ^ named
        gray = gray * 2 + bit
    across = jnp.broadcast_to(gray.astype(f32), (rows, rows))
    first, second = iota((rows, rows), 0), iota((rows, rows), 1)
    top = jnp.where(first[:8] == 0, across[:8], 0.0).astype(bf16)
    down = contract(top, jnp.ones((8, rows), bf16), 0, 0)
    ahead = (down < across) | ((down == across) & (first < second))
    rank = jnp.sum(ahead.astype(f32), axis=0, keepdims=True).astype(jnp.int32)
    target = rank % len(chunks) * size + rank // len(chunks)
    order = (first == target).astype(bf16)
    order_out[...] = order
    ext = dot32(order, ext).astype(bf16)
    for q, chunk in enumerate(chunks):
        chunk[:, width:] = ext[q * size : (q + 1) * size]
    fetch.wait()
    @pl.loop(0, width // STEP)
    def _(n):
        cols = pl.ds(pl.multiple_of(n * STEP, STEP), STEP)
        moved = dot32(order, held[:, cols]).astype(bf16)
        for q, chunk in enumerate(chunks):
            chunk[:, cols] = moved[q * size : (q + 1) * size]


def pick_kernel(experts, mode, idx, *refs):
    *blocks, own_out, cross_out, pick_out = refs
    total = blocks[0].shape[1]
    rows = blocks[0].shape[0] * (len(blocks) if mode == "both" else 1)
    own_rows, cross_rows = own_out.shape[0], cross_out.shape[0]
    inner = idx[3] == 1

    def load(cols):
        if mode == "both":
            return jnp.concatenate([b[:, cols] for b in blocks], 0)
        if mode == "either":
            return jnp.where(inner, blocks[0][:, cols], blocks[1][:, cols])
        return blocks[0][:, cols]

    ext = load(pl.ds(total - LANES, LANES))

    def picks(expert, count):
        mask = jnp.broadcast_to(scale_of(ext, expert, experts) > 0, (rows, LANES)).astype(jnp.bfloat16)
        upto = (iota((rows, rows), 0) <= iota((rows, rows), 1)).astype(jnp.bfloat16)
        place = contract(mask, upto, 0, 0)[:count]
        named = contract(mask, eye(rows), 0, 0)[:count]
        slot = iota((count, rows), 0).astype(jnp.float32)
        return ((named > 0.5) & (place - 1.0 == slot)).astype(jnp.float32)

    own = picks(idx[1], own_rows) if mode == "both" else eye(rows).astype(jnp.float32)
    pick = jnp.concatenate([own, picks(idx[2], cross_rows)], 0).astype(jnp.bfloat16)
    pick_out[...] = pick
    step = total // 3

    @pl.loop(0, 3)
    def _(n):
        cols = pl.ds(pl.multiple_of(n * step, LANES), step)
        got = dot32(pick, load(cols))
        own_out[:, cols] = got[:own_rows].astype(jnp.bfloat16)
        cross_out[:, cols] = got[own_rows:].astype(jnp.bfloat16)


def expert_kernel(experts, idx, own, cross, ga, gb, ua, ub, da, db, own_out, cross_out, hidden):
    own_rows, total = own.shape
    width = total - LANES
    core, expert = idx[0], idx[1]
    half = ga.shape[0]
    x = jnp.concatenate([own[:, :width], cross[:, :width]], 0)
    ext = jnp.concatenate([own[:, width:], cross[:, width:]], 0)
    scale = scale_of(ext, expert, experts)
    for place, g, u in ((core, ga, ua), (1 - core, gb, ub)):
        gate = contract(x, g[...], 1, 1)
        upval = contract(x, u[...], 1, 1)
        hidden[place] = (gate / (1.0 + jnp.exp(-gate)) * upval * scale).astype(jnp.bfloat16)
    for base, d in ((0, da), (da.shape[1], db)):

        @pl.loop(0, d.shape[1] // STEP)
        def _(n, base=base, d=d):
            cols = pl.ds(pl.multiple_of(n * STEP, STEP), STEP)
            made = dot32(hidden[0], d[:half, cols]) + dot32(hidden[1], d[half:, cols])
            to = pl.ds(pl.multiple_of(base + n * STEP, STEP), STEP)
            own_out[:, to] = made[:own_rows].astype(jnp.bfloat16)
            cross_out[:, to] = made[own_rows:].astype(jnp.bfloat16)


def combine_kernel(first, idx, pick, own, cross, *refs):
    *more, out = refs
    width = own.shape[1]
    rows = slice(first, first + out.shape[0])

    @pl.loop(0, width // STEP)
    def _(n):
        cols = pl.ds(pl.multiple_of(n * STEP, STEP), STEP)
        got = contract(pick[...], jnp.concatenate([own[:, cols], cross[:, cols]], 0), 0, 0)[rows]
        for ref in more:
            got += ref[:, cols].astype(jnp.float32)
        out[:, cols] = got.astype(jnp.bfloat16)


def finish_kernel(half, idx, order, pick, own, cross, *refs):
    *more, out = refs
    width = own.shape[1]

    @pl.loop(0, width // STEP)
    def _(n):
        cols = pl.ds(pl.multiple_of(n * STEP, STEP), STEP)
        got = contract(pick[...], jnp.concatenate([own[:, cols], cross[:, cols]], 0), 0, 0)
        sums = [sum(r[:, cols].astype(jnp.float32) for r in part) for part in (more[:half], more[half:])]
        got = (got + jnp.concatenate(sums, 0)).astype(jnp.bfloat16)
        got = contract(order[...], got, 0, 0).astype(jnp.bfloat16)
        out[:, pl.ds(pl.multiple_of((idx[4] + n * STEP) % width, STEP), STEP)] = got


def fence_kernel(idx):
    pass


def run_copies(sems, pairs):
    copies = [pltpu.make_async_copy(s, d, sems.at[i]) for i, (s, d) in enumerate(pairs)]
    for c in copies:
        c.start()
    for c in copies:
        c.wait()


def fetch_kernel(idx, *refs):
    count = len(refs) // 2
    run_copies(refs[-1], zip(refs[:count], refs[count:-1]))


def call(name, kernel, outs, idx, token, args, passes=(), scratch=(), cost=1, left=()):
    vmem, anywhere = pl.BlockSpec(memory_space=pltpu.VMEM), pl.BlockSpec(memory_space=pl.ANY)
    through = [token, *passes]
    first = 1 + len(args) + len(left)

    def body(*refs):
        ins, rest = refs[:first], refs[first + len(through) :]
        kernel(*ins, *rest[: len(outs)], *rest[len(outs) + len(through) :])

    got = pl.pallas_call(
        body,
        out_shape=[*outs, *(jax.ShapeDtypeStruct(x.shape, x.dtype) for x in through)],
        in_specs=[pl.BlockSpec(memory_space=pltpu.SMEM)]
        + [vmem] * len(args)
        + [anywhere] * len(left)
        + [anywhere] * len(through),
        out_specs=[vmem] * len(outs) + [anywhere] * len(through),
        input_output_aliases={first + i: len(outs) + i for i in range(len(through))},
        scratch_shapes=list(scratch),
        name=name,
        compiler_params=pltpu.CompilerParams(vmem_limit_bytes=LIMIT),
        cost_estimate=pl.CostEstimate(flops=1, bytes_accessed=cost, transcendentals=0),
    )(idx, *args, *left, *through)
    return got[: len(outs)], got[len(outs)], got[len(outs) + 1 :]


ORDER = [
    ["prep", "EB", "EA", "MA"],
    ["P0", "NA", "+MA"],
    ["P1A", "Y1A", "OA", "+wu", "+MA"],
    ["W", "Y0"],
    ["P1B"],
    ["f", "NB", "+NA", "+Y1A"],
    ["P2A", "MB", "Y2A", "+Y1A", "QA"],
    ["F1A", "+Y0"],
    ["P3A", "QB", "Y3A", "+NB"],
    ["F2A", "R2A"],
    ["F3A", "R3A", "OB"],
    ["P3B", "+Y2A"],
    ["f", "Y3B", "+R2A"],
    ["F0"],
    ["C2A"],
    ["C3A", "I3A"],
    ["P2B", "Y2B"],
    ["F3B", "R3B", "I2A"],
    ["D3A", "S3A", "Y1B", "+Y2B"],
    ["C3B", "X3B"],
    ["F2B", "R2B"],
    ["D2A", "+S3A", "+Y1B"],
    ["C2B", "R1A", "S3B", "I2B", "+Y1B"],
    ["F1B"],
    ["f", "R1B", "S2A", "+R1A", "+S3A", "+R2B"],
    ["D1A", "S1A"],
    ["D1B", "S1B", "R0"],
    ["D2B", "S2B", "+X3B"],
    ["fin"],
]


def lined(tokens, routes, route_weights, gate_weight, up_weight, down_weight):
    tok_rows, top_count = routes.shape
    width = tokens.shape[1]
    devices = lax.axis_size("expert")
    experts = devices // 2
    capacity = tok_rows * top_count // experts
    half = gate_weight.shape[1]
    index = lax.axis_index("expert")
    core, side, line = index % 2, index // 2 % 2, index // 4
    inner = ((line == 1) | (line == 2)).astype(jnp.int32)
    idx = jnp.stack(
        [core, 2 * line + side, 2 * line + 1 - side, inner, core * down_weight.shape[1], 1 - side]
    ).astype(jnp.int32)
    rows = tok_rows // 2
    total = width + LANES
    bf16 = jnp.bfloat16

    def in_hbm(x):
        return pltpu.with_memory_space_constraint(x, pltpu.HBM)

    def like(*shape):
        return jax.ShapeDtypeStruct(shape, bf16)

    gate, up = gate_weight.T, up_weight.T

    val = {}
    for name, w in (("wg", gate), ("wu", up), ("wd", down_weight)):
        with jax.named_scope("move_" + name):
            val[name] = swapped(w, "expert", 0)
    steps = {name for name, *_ in ORDER}
    slots = {name[1:] for name in steps if name[0] == "P"}

    def kernel_of(name):
        kind, q = name[:-1], name[-1]
        if name == "prep":
            return (
                functools.partial(prepare_kernel, experts),
                [like(rows, total), like(rows, total), like(tok_rows, tok_rows)],
                [in_hbm(routes.T), in_hbm(route_weights.T)],
                [pltpu.VMEM(tokens.shape, bf16), pltpu.SemaphoreType.DMA],
            )
        if name[0] == "P":
            slot = name[1:]
            if slot in ("0", "1"):
                blocks, mode = [["payA", "payB"], ["EA", "EB"]][int(slot)], "both"
                own, cross, size = capacity, capacity, tok_rows
            else:
                blocks = {"1": ["E" + q], "2": ["M" + q, "O" + q], "3": ["N" + q, "Q" + q]}[slot[0]]
                mode = "one" if len(blocks) == 1 else "either"
                own, cross, size = rows, CROSS_ROWS, rows
            return (
                functools.partial(pick_kernel, experts, mode),
                [like(own, total), like(cross, total), like(own + cross, size)],
                [val[b] for b in blocks],
                [],
            )
        if name[0] == "F":
            own, cross = val["own" + name[1:]], val["Y" + name[1:]]
            weights = [gate, val["vg"], up, val["vu"], down_weight, val["vd"]]
            weights = [pltpu.with_memory_space_constraint(w, pltpu.VMEM) for w in weights]
            args = [own, cross, *weights]
            return (
                functools.partial(expert_kernel, experts),
                [like(own.shape[0], width), like(cross.shape[0], width)],
                args,
                [pltpu.VMEM((2, own.shape[0] + cross.shape[0], half), bf16)],
            )
        if name == "W":
            outs = [pltpu.VMEM(w.shape, bf16) for w in (gate, up, down_weight)]
            return fetch_kernel, outs, [], [pltpu.SemaphoreType.DMA((3,))]
        if name == "fin":
            made = [val["order"], val["pick0"], val["made0"], val["R0"]]
            made += [val[s + q] for q in "AB" for s in ("S1", "S2", "X3") if s + q in val]
            counts = [sum(s + q in val for s in ("S1", "S2", "X3")) for q in "AB"]
            return functools.partial(finish_kernel, counts[0]), [like(tok_rows, width)], made, []
        slot = name[1:] if name[1:] in slots else name[1]
        made = [val[s + slot] for s in ("pick", "made", "R")]
        made += [val[x] for x in {"D2": ["I2" + q], "D3": ["I3" + q], "D1": ["S3" + q]}.get(kind, [])]
        first = rows if slot == name[1] and q == "B" else 0
        return functools.partial(combine_kernel, first), [like(rows, width)], made, []

    def keep(name, got):
        slot = name[1:]
        if name == "prep":
            val["payA"], val["payB"], val["order"] = got
        elif name[0] == "P":
            val["own" + slot], val["cross" + slot], val["pick" + slot] = got
        elif name == "W":
            val["vg"], val["vu"], val["vd"] = got
        elif name[0] == "F":
            val["made" + slot], val["back" + slot] = got
        else:
            val[name] = got[0]

    def move_of(name):
        kind, slot, q = name[0], name[1:], name[-1]
        if kind == "Y":
            return "cross" + slot, lambda x: swapped(x, "expert", 1)
        if kind == "R":
            return "back" + slot, lambda x: swapped(x, "expert", 1)
        source, pairs = {
            "E": ("pay" + q, OUTER),
            "M": ("pay" + q, MIDDLE),
            "O": ("M" + q, OUT),
            "N": ("E" + q, MIDDLE),
            "Q": ("N" + q, OUT),
            "I2": ("C2" + q, IN),
            "S2": ("D2" + q, MIDDLE),
            "X3": ("C3" + q, ENDS),
            "I3": ("C3" + q, IN),
            "S3": (("D3" if "D3" + q in steps else "C3") + q, MIDDLE),
            "S1": ("D1" + q, OUTER),
        }[name[:-1]]
        return source, lambda x: along_line(x, pairs)

    token = jnp.zeros((8, LANES), jnp.float32)
    for name, *moves in ORDER:
        done = [m[1:] for m in moves if m[0] == "+"]
        moves = [m for m in moves if m[0] != "+"]
        sources = {m: move_of(m)[0] for m in moves}
        passed = sorted({s for s in [*sources.values(), *done] if s in val})
        if name == "f":
            _, token, through = call("fence", fence_kernel, [], idx, token, [], passes=[val[s] for s in passed])
        else:
            kernel, outs, args, scratch = kernel_of(name)
            cost = sum(x.size * x.dtype.itemsize for x in [*args, *outs]) if name[0] == "F" else 1
            through = [val[s] for s in passed]
            left = {"prep": [in_hbm(tokens)], "W": [val["wg"], val["wu"], val["wd"]]}.get(name, [])
            got, token, through = call(name, kernel, outs, idx, token, args, through, scratch, cost, left)
            keep(name, got)
        val.update(zip(passed, through))
        for m in moves:
            with jax.named_scope("move_" + m):
                val[m] = move_of(m)[1](val[sources[m]])
    return val["fin"]


def solution(mesh):
    body = lined if mesh.shape["expert"] == 16 else dispatched
    return jax.shard_map(
        body,
        mesh=mesh,
        in_specs=(
            P(("groups", "expert"), None),
            P(("groups", "expert"), None),
            P(("groups", "expert"), None),
            P(None, "expert"),
            P(None, "expert"),
            P(None, "expert"),
        ),
        out_specs=P(("groups", "expert"), None),
        check_vma=False,
    )
```

```python
import functools

import jax
import jax.experimental.pallas as pl
import jax.experimental.pallas.tpu as pltpu
import jax.numpy as jnp
from jax import lax
from jax.sharding import PartitionSpec as P

CROSS_ROWS = 40
LANES = 128
LIMIT = 12 << 20


def swapped(x, axis, apart):
    return lax.ppermute(x, axis, [(i, i ^ 1 << apart) for i in range(lax.axis_size(axis))])


def dot32(a, b):
    return jnp.dot(a, b, preferred_element_type=jnp.float32)


def expert_hidden(rows, gate_part, up_part, parity):
    gate = dot32(rows, gate_part)
    upval = dot32(rows, up_part)
    hidden = (jax.nn.silu(gate) * upval).astype(jnp.bfloat16)
    partner = swapped(hidden, "expert", 0)
    return jnp.where(
        parity == 0, jnp.concatenate([hidden, partner], 1), jnp.concatenate([partner, hidden], 1)
    )


def dispatched(tokens, routes, route_weights, gate_weight, up_weight, down_weight):
    tok_rows, top_count = routes.shape
    width = tokens.shape[1]
    half_width = down_weight.shape[1]
    devices = lax.axis_size("expert")
    experts = devices // 2
    capacity = tok_rows * top_count // experts
    parity = lax.axis_index("expert") % 2
    flat = routes.reshape(-1)
    onehot = (flat[:, None] == jnp.arange(experts, dtype=jnp.int32)[None, :]).astype(jnp.int32)
    before = jnp.cumsum(onehot, axis=0) - onehot
    slot_of = jnp.sum(before * onehot, axis=1)
    position = flat * capacity + slot_of
    assign_ids = jnp.arange(flat.shape[0], dtype=jnp.int32) // top_count
    owner = jnp.zeros((experts * capacity,), jnp.int32).at[position].set(assign_ids)
    gathered = tokens[owner]
    outgoing = jnp.broadcast_to(
        gathered.reshape(experts, 1, capacity, width), (experts, 2, capacity, width)
    )
    outgoing = outgoing.reshape(devices, capacity, width)
    received = lax.all_to_all(outgoing, "expert", split_axis=0, concat_axis=0, tiled=True)
    count, items, _ = received.shape
    hidden = expert_hidden(received.reshape(count * items, width), gate_weight, up_weight, parity)
    produced = dot32(hidden, down_weight).astype(jnp.bfloat16)
    returned = lax.all_to_all(
        produced.reshape(count, items, half_width),
        "expert",
        split_axis=0,
        concat_axis=0,
        tiled=True,
    )
    returned = returned.reshape(experts, 2, capacity, half_width).transpose(0, 2, 1, 3)
    expert_rows = returned.reshape(experts * capacity, width)
    picked = expert_rows[position].reshape(tok_rows, top_count, width)
    mixed = jnp.einsum("tk,tkd->td", route_weights, picked.astype(jnp.float32))
    return mixed.astype(jnp.bfloat16)


def along_line(x, pairs):
    moves = [((a * 2 + s) * 2 + c, (b * 2 + s) * 2 + c) for a, b in pairs for s in (0, 1) for c in (0, 1)]
    return lax.ppermute(x, "expert", moves)


OUTER = [(0, 1), (1, 0), (2, 3), (3, 2)]
MIDDLE = [(1, 2), (2, 1)]
OUT = [(1, 0), (2, 3)]
IN = [(0, 1), (3, 2)]
ENDS = [(0, 3), (3, 0)]


def contract(a, b, da, db):
    return lax.dot_general(a, b, (((da,), (db,)), ((), ())), preferred_element_type=jnp.float32)


def iota(shape, dim):
    return lax.broadcasted_iota(jnp.int32, shape, dim)


def eye(n):
    return (iota((n, n), 0) == iota((n, n), 1)).astype(jnp.bfloat16)


def scale_of(ext, expert, experts):
    lane = iota(ext.shape, 1)
    mine = (lane % experts == expert) & (lane < 3 * experts)
    return jnp.sum(jnp.where(mine, ext.astype(jnp.float32), 0.0), axis=1, keepdims=True)


def prepare_kernel(experts, idx, routes, weights, tokens, *refs):
    *chunks, order_out, held, sem = refs
    fetch = pltpu.make_async_copy(tokens, held, sem)
    fetch.start()
    rows, width = tokens.shape
    size = rows // len(chunks)
    f32, bf16 = jnp.float32, jnp.bfloat16
    full = jnp.zeros((experts, rows), f32)
    for k in range(routes.shape[0]):
        full += jnp.where(iota((experts, rows), 0) == routes[k : k + 1], weights[k : k + 1], 0.0)
    high = full.astype(bf16).astype(f32)
    mid = (full - high).astype(bf16).astype(f32)
    parts = jnp.concatenate([high, mid, full - high - mid], 0).astype(bf16)
    spread = (iota((3 * experts, LANES), 0) == iota((3 * experts, LANES), 1)).astype(bf16)
    ext = contract(parts, spread, 0, 0).astype(bf16)
    gray = jnp.zeros((1, rows), jnp.int32)
    bit = jnp.zeros((1, rows), jnp.int32)
    for z in range(experts // 2):
        named = jnp.zeros((1, rows), jnp.int32)
        for k in range(routes.shape[0]):
            named += (routes[k : k + 1] == idx[5] + 2 * z).astype(jnp.int32)
        bit = bit ^ named
        gray = gray * 2 + bit
    across = jnp.broadcast_to(gray.astype(f32), (rows, rows))
    first, second = iota((rows, rows), 0), iota((rows, rows), 1)
    top = jnp.where(first[:8] == 0, across[:8], 0.0).astype(bf16)
    down = contract(top, jnp.ones((8, rows), bf16), 0, 0)
    ahead = (down < across) | ((down == across) & (first < second))
    rank = jnp.sum(ahead.astype(f32), axis=0, keepdims=True).astype(jnp.int32)
    target = rank % len(chunks) * size + rank // len(chunks)
    order = (first == target).astype(bf16)
    order_out[...] = order
    ext = dot32(order, ext).astype(bf16)
    for q, chunk in enumerate(chunks):
        chunk[:, width:] = ext[q * size : (q + 1) * size]
    fetch.wait()
    step = 1024
    for n in range(0, width, step):
        moved = dot32(order, held[:, n : n + step]).astype(bf16)
        for q, chunk in enumerate(chunks):
            chunk[:, n : n + step] = moved[q * size : (q + 1) * size]


def pick_kernel(experts, mode, idx, *refs):
    *blocks, own_out, cross_out, pick_out = refs
    total = blocks[0].shape[1]
    rows = blocks[0].shape[0] * (len(blocks) if mode == "both" else 1)
    own_rows, cross_rows = own_out.shape[0], cross_out.shape[0]
    inner = idx[3] == 1

    def load(cols):
        if mode == "both":
            return jnp.concatenate([b[:, cols] for b in blocks], 0)
        if mode == "either":
            return jnp.where(inner, blocks[0][:, cols], blocks[1][:, cols])
        return blocks[0][:, cols]

    ext = load(slice(total - LANES, total))

    def picks(expert, count):
        mask = jnp.broadcast_to(scale_of(ext, expert, experts) > 0, (rows, LANES)).astype(jnp.bfloat16)
        upto = (iota((rows, rows), 0) <= iota((rows, rows), 1)).astype(jnp.bfloat16)
        place = contract(mask, upto, 0, 0)[:count]
        named = contract(mask, eye(rows), 0, 0)[:count]
        slot = iota((count, rows), 0).astype(jnp.float32)
        return ((named > 0.5) & (place - 1.0 == slot)).astype(jnp.float32)

    own = picks(idx[1], own_rows) if mode == "both" else eye(rows).astype(jnp.float32)
    pick = jnp.concatenate([own, picks(idx[2], cross_rows)], 0).astype(jnp.bfloat16)
    pick_out[...] = pick
    step = total // 3
    for n in range(0, total, step):
        got = dot32(pick, load(slice(n, n + step)))
        own_out[:, n : n + step] = got[:own_rows].astype(jnp.bfloat16)
        cross_out[:, n : n + step] = got[own_rows:].astype(jnp.bfloat16)


def expert_kernel(experts, idx, own, cross, ga, gb, ua, ub, da, db, own_out, cross_out, hidden):
    own_rows, total = own.shape
    width = total - LANES
    core, expert = idx[0], idx[1]
    half = ga.shape[0]
    x = jnp.concatenate([own[:, :width], cross[:, :width]], 0)
    ext = jnp.concatenate([own[:, width:], cross[:, width:]], 0)
    scale = scale_of(ext, expert, experts)
    for place, g, u in ((core, ga, ua), (1 - core, gb, ub)):
        gate = contract(x, g[...], 1, 1)
        upval = contract(x, u[...], 1, 1)
        hidden[place] = (gate / (1.0 + jnp.exp(-gate)) * upval * scale).astype(jnp.bfloat16)
    step = 512
    cols = da.shape[1]
    for n in range(0, 2 * cols, step):
        d, m = (da, n) if n < cols else (db, n - cols)
        made = dot32(hidden[0], d[:half, m : m + step]) + dot32(hidden[1], d[half:, m : m + step])
        own_out[:, n : n + step] = made[:own_rows].astype(jnp.bfloat16)
        cross_out[:, n : n + step] = made[own_rows:].astype(jnp.bfloat16)


def combine_kernel(first, idx, pick, own, cross, *refs):
    *more, out = refs
    width = own.shape[1]
    rows = slice(first, first + out.shape[0])
    step = 1024
    for n in range(0, width, step):
        cols = slice(n, n + step)
        got = contract(pick[...], jnp.concatenate([own[:, cols], cross[:, cols]], 0), 0, 0)[rows]
        for ref in more:
            got += ref[:, cols].astype(jnp.float32)
        out[:, cols] = got.astype(jnp.bfloat16)


def finish_kernel(half, idx, order, pick, own, cross, *refs):
    *more, out, held, sems = refs
    width = own.shape[1]
    step = 1024
    copies = []
    for i, n in enumerate(range(0, width, step)):
        cols = slice(n, n + step)
        got = contract(pick[...], jnp.concatenate([own[:, cols], cross[:, cols]], 0), 0, 0)
        sums = [sum(r[:, cols].astype(jnp.float32) for r in part) for part in (more[:half], more[half:])]
        got = (got + jnp.concatenate(sums, 0)).astype(jnp.bfloat16)
        held[i] = contract(order[...], got, 0, 0).astype(jnp.bfloat16)
        to = pl.ds(pl.multiple_of((idx[4] + n) % width, step), step)
        copies.append(pltpu.make_async_copy(held.at[i], out.at[:, to], sems.at[i]))
        copies[-1].start()
    for c in copies:
        c.wait()


def fence_kernel(idx):
    pass


def run_copies(sems, pairs):
    copies = [pltpu.make_async_copy(s, d, sems.at[i]) for i, (s, d) in enumerate(pairs)]
    for c in copies:
        c.start()
    for c in copies:
        c.wait()


def fetch_kernel(idx, *refs):
    count = len(refs) // 2
    run_copies(refs[-1], zip(refs[:count], refs[count:-1]))


def call(name, kernel, outs, idx, token, args, passes=(), scratch=(), cost=1, left=(), away=False):
    vmem, anywhere = pl.BlockSpec(memory_space=pltpu.VMEM), pl.BlockSpec(memory_space=pl.ANY)
    through = [token, *passes]
    first = 1 + len(args) + len(left)

    def body(*refs):
        ins, rest = refs[:first], refs[first + len(through) :]
        kernel(*ins, *rest[: len(outs)], *rest[len(outs) + len(through) :])

    got = pl.pallas_call(
        body,
        out_shape=[*outs, *(jax.ShapeDtypeStruct(x.shape, x.dtype) for x in through)],
        in_specs=[pl.BlockSpec(memory_space=pltpu.SMEM)]
        + [vmem] * len(args)
        + [anywhere] * len(left)
        + [anywhere] * len(through),
        out_specs=[anywhere if away else vmem] * len(outs) + [anywhere] * len(through),
        input_output_aliases={first + i: len(outs) + i for i in range(len(through))},
        scratch_shapes=list(scratch),
        name=name,
        compiler_params=pltpu.CompilerParams(vmem_limit_bytes=LIMIT),
        cost_estimate=pl.CostEstimate(flops=1, bytes_accessed=cost, transcendentals=0),
    )(idx, *args, *left, *through)
    return got[: len(outs)], got[len(outs)], got[len(outs) + 1 :]


ORDER = [
    ["prep", "EA", "MB", "EB"],
    ["P0", "NA", "Y0"],
    ["f", "OB", "+wg", "+wu"],
    ["W"],
    ["f", "MA"],
    ["P1", "Y1", "QA"],
    ["P2B", "Y2B", "NB"],
    ["F0", "OA"],
    ["P3A", "Y3A", "+Y1"],
    ["F2B", "R2B"],
    ["f", "QB", "+Y3A"],
    ["P2A"],
    ["f", "Y2A"],
    ["F3A"],
    ["C2B", "I2B"],
    ["P3B", "Y3B", "+Y2A"],
    ["F1", "R3A"],
    ["F3B", "+I2B"],
    ["D2B", "R3B"],
    ["C3A", "I3A", "S2B"],
    ["F2A"],
    ["C3B", "I3B", "R2A", "+R3A"],
    ["D3A", "S3A"],
    ["C2A", "R1", "I2A", "+S2B"],
    ["D3B", "S3B", "+R2A"],
    ["D1A", "S1A", "R0"],
    ["D2A", "+R1"],
    ["D1B", "S2A", "S1B", "+I2A"],
    ["fin"],
]


def lined(tokens, routes, route_weights, gate_weight, up_weight, down_weight):
    tok_rows, top_count = routes.shape
    width = tokens.shape[1]
    devices = lax.axis_size("expert")
    experts = devices // 2
    capacity = tok_rows * top_count // experts
    half = gate_weight.shape[1]
    index = lax.axis_index("expert")
    core, side, line = index % 2, index // 2 % 2, index // 4
    inner = ((line == 1) | (line == 2)).astype(jnp.int32)
    idx = jnp.stack(
        [core, 2 * line + side, 2 * line + 1 - side, inner, core * down_weight.shape[1], 1 - side]
    ).astype(jnp.int32)
    rows = tok_rows // 2
    total = width + LANES
    bf16 = jnp.bfloat16

    def in_hbm(x):
        return pltpu.with_memory_space_constraint(x, pltpu.HBM)

    def like(*shape):
        return jax.ShapeDtypeStruct(shape, bf16)

    gate, up = gate_weight.T, up_weight.T

    val = {}
    for name, w in (("wg", gate), ("wu", up), ("wd", down_weight)):
        with jax.named_scope("move_" + name):
            val[name] = swapped(w, "expert", 0)
    steps = {name for name, *_ in ORDER}
    slots = {name[1:] for name in steps if name[0] == "P"}

    def kernel_of(name):
        kind, q = name[:-1], name[-1]
        if name == "prep":
            return (
                functools.partial(prepare_kernel, experts),
                [like(rows, total), like(rows, total), like(tok_rows, tok_rows)],
                [in_hbm(routes.T), in_hbm(route_weights.T)],
                [pltpu.VMEM(tokens.shape, bf16), pltpu.SemaphoreType.DMA],
            )
        if name[0] == "P":
            slot = name[1:]
            if slot in ("0", "1"):
                blocks, mode = [["payA", "payB"], ["EA", "EB"]][int(slot)], "both"
                own, cross, size = capacity, capacity, tok_rows
            else:
                blocks = {"1": ["E" + q], "2": ["M" + q, "O" + q], "3": ["N" + q, "Q" + q]}[slot[0]]
                mode = "one" if len(blocks) == 1 else "either"
                own, cross, size = rows, CROSS_ROWS, rows
            return (
                functools.partial(pick_kernel, experts, mode),
                [like(own, total), like(cross, total), like(own + cross, size)],
                [val[b] for b in blocks],
                [],
            )
        if name[0] == "F":
            own, cross = val["own" + name[1:]], val["Y" + name[1:]]
            weights = [gate, val["vg"], up, val["vu"], down_weight, val["vd"]]
            weights = [pltpu.with_memory_space_constraint(w, pltpu.VMEM) for w in weights]
            args = [own, cross, *weights]
            return (
                functools.partial(expert_kernel, experts),
                [like(own.shape[0], width), like(cross.shape[0], width)],
                args,
                [pltpu.VMEM((2, own.shape[0] + cross.shape[0], half), bf16)],
            )
        if name == "W":
            outs = [pltpu.VMEM(w.shape, bf16) for w in (gate, up, down_weight)]
            return fetch_kernel, outs, [], [pltpu.SemaphoreType.DMA((3,))]
        if name == "fin":
            made = [val["order"], val["pick0"], val["made0"], val["R0"]]
            made += [val[s + q] for q in "AB" for s in ("S1", "S2", "X3") if s + q in val]
            counts = [sum(s + q in val for s in ("S1", "S2", "X3")) for q in "AB"]
            parts = width // 1024
            scratch = [pltpu.VMEM((parts, tok_rows, 1024), bf16), pltpu.SemaphoreType.DMA((parts,))]
            return functools.partial(finish_kernel, counts[0]), [like(tok_rows, width)], made, scratch
        slot = name[1:] if name[1:] in slots else name[1]
        made = [val[s + slot] for s in ("pick", "made", "R")]
        made += [val[x] for x in {"D2": ["I2" + q], "D3": ["I3" + q], "D1": ["S3" + q]}.get(kind, [])]
        first = rows if slot == name[1] and q == "B" else 0
        return functools.partial(combine_kernel, first), [like(rows, width)], made, []

    def keep(name, got):
        slot = name[1:]
        if name == "prep":
            val["payA"], val["payB"], val["order"] = got
        elif name[0] == "P":
            val["own" + slot], val["cross" + slot], val["pick" + slot] = got
        elif name == "W":
            val["vg"], val["vu"], val["vd"] = got
        elif name[0] == "F":
            val["made" + slot], val["back" + slot] = got
        else:
            val[name] = got[0]

    def move_of(name):
        kind, slot, q = name[0], name[1:], name[-1]
        if kind == "Y":
            return "cross" + slot, lambda x: swapped(x, "expert", 1)
        if kind == "R":
            return "back" + slot, lambda x: swapped(x, "expert", 1)
        source, pairs = {
            "E": ("pay" + q, OUTER),
            "M": ("pay" + q, MIDDLE),
            "O": ("M" + q, OUT),
            "N": ("E" + q, MIDDLE),
            "Q": ("N" + q, OUT),
            "I2": ("C2" + q, IN),
            "S2": ("D2" + q, MIDDLE),
            "X3": ("C3" + q, ENDS),
            "I3": ("C3" + q, IN),
            "S3": (("D3" if "D3" + q in steps else "C3") + q, MIDDLE),
            "S1": ("D1" + q, OUTER),
        }[name[:-1]]
        return source, lambda x: along_line(x, pairs)

    token = jnp.zeros((8, LANES), jnp.float32)
    for name, *moves in ORDER:
        done = [m[1:] for m in moves if m[0] == "+"]
        moves = [m for m in moves if m[0] != "+"]
        sources = {m: move_of(m)[0] for m in moves}
        passed = sorted({s for s in [*sources.values(), *done] if s in val})
        if name == "f":
            _, token, through = call("fence", fence_kernel, [], idx, token, [], passes=[val[s] for s in passed])
        else:
            kernel, outs, args, scratch = kernel_of(name)
            cost = sum(x.size * x.dtype.itemsize for x in [*args, *outs]) if name[0] == "F" else 1
            through = [val[s] for s in passed]
            left = {"prep": [in_hbm(tokens)], "W": [val["wg"], val["wu"], val["wd"]]}.get(name, [])
            got, token, through = call(name, kernel, outs, idx, token, args, through, scratch, cost, left, name == "fin")
            keep(name, got)
        val.update(zip(passed, through))
        for m in moves:
            with jax.named_scope("move_" + m):
                val[m] = move_of(m)[1](val[sources[m]])
    return val["fin"]


def solution(mesh):
    body = lined if mesh.shape["expert"] == 16 else dispatched
    return jax.shard_map(
        body,
        mesh=mesh,
        in_specs=(
            P(("groups", "expert"), None),
            P(("groups", "expert"), None),
            P(("groups", "expert"), None),
            P(None, "expert"),
            P(None, "expert"),
            P(None, "expert"),
        ),
        out_specs=P(("groups", "expert"), None),
        check_vma=False,
    )
```

```python
import functools

import jax
import jax.experimental.pallas as pl
import jax.experimental.pallas.tpu as pltpu
import jax.numpy as jnp
from jax import lax
from jax.sharding import PartitionSpec as P

CROSS_ROWS = 40
LANES = 128
LIMIT = 12 << 20


def swapped(x, axis, apart):
    return lax.ppermute(x, axis, [(i, i ^ 1 << apart) for i in range(lax.axis_size(axis))])


def dot32(a, b):
    return jnp.dot(a, b, preferred_element_type=jnp.float32)


def expert_hidden(rows, gate_part, up_part, parity):
    gate = dot32(rows, gate_part)
    upval = dot32(rows, up_part)
    hidden = (jax.nn.silu(gate) * upval).astype(jnp.bfloat16)
    partner = swapped(hidden, "expert", 0)
    return jnp.where(
        parity == 0, jnp.concatenate([hidden, partner], 1), jnp.concatenate([partner, hidden], 1)
    )


def dispatched(tokens, routes, route_weights, gate_weight, up_weight, down_weight):
    tok_rows, top_count = routes.shape
    width = tokens.shape[1]
    half_width = down_weight.shape[1]
    devices = lax.axis_size("expert")
    experts = devices // 2
    capacity = tok_rows * top_count // experts
    parity = lax.axis_index("expert") % 2
    flat = routes.reshape(-1)
    onehot = (flat[:, None] == jnp.arange(experts, dtype=jnp.int32)[None, :]).astype(jnp.int32)
    before = jnp.cumsum(onehot, axis=0) - onehot
    slot_of = jnp.sum(before * onehot, axis=1)
    position = flat * capacity + slot_of
    assign_ids = jnp.arange(flat.shape[0], dtype=jnp.int32) // top_count
    owner = jnp.zeros((experts * capacity,), jnp.int32).at[position].set(assign_ids)
    gathered = tokens[owner]
    outgoing = jnp.broadcast_to(
        gathered.reshape(experts, 1, capacity, width), (experts, 2, capacity, width)
    )
    outgoing = outgoing.reshape(devices, capacity, width)
    received = lax.all_to_all(outgoing, "expert", split_axis=0, concat_axis=0, tiled=True)
    count, items, _ = received.shape
    hidden = expert_hidden(received.reshape(count * items, width), gate_weight, up_weight, parity)
    produced = dot32(hidden, down_weight).astype(jnp.bfloat16)
    returned = lax.all_to_all(
        produced.reshape(count, items, half_width),
        "expert",
        split_axis=0,
        concat_axis=0,
        tiled=True,
    )
    returned = returned.reshape(experts, 2, capacity, half_width).transpose(0, 2, 1, 3)
    expert_rows = returned.reshape(experts * capacity, width)
    picked = expert_rows[position].reshape(tok_rows, top_count, width)
    mixed = jnp.einsum("tk,tkd->td", route_weights, picked.astype(jnp.float32))
    return mixed.astype(jnp.bfloat16)


def along_line(x, pairs):
    moves = [((a * 2 + s) * 2 + c, (b * 2 + s) * 2 + c) for a, b in pairs for s in (0, 1) for c in (0, 1)]
    return lax.ppermute(x, "expert", moves)


OUTER = [(0, 1), (1, 0), (2, 3), (3, 2)]
MIDDLE = [(1, 2), (2, 1)]
OUT = [(1, 0), (2, 3)]
IN = [(0, 1), (3, 2)]
ENDS = [(0, 3), (3, 0)]


def contract(a, b, da, db):
    return lax.dot_general(a, b, (((da,), (db,)), ((), ())), preferred_element_type=jnp.float32)


def iota(shape, dim):
    return lax.broadcasted_iota(jnp.int32, shape, dim)


def eye(n):
    return (iota((n, n), 0) == iota((n, n), 1)).astype(jnp.bfloat16)


def scale_of(ext, expert, experts):
    lane = iota(ext.shape, 1)
    mine = (lane % experts == expert) & (lane < 3 * experts)
    return jnp.sum(jnp.where(mine, ext.astype(jnp.float32), 0.0), axis=1, keepdims=True)


def prepare_kernel(experts, idx, routes, weights, tokens, *refs):
    *chunks, order_out, held, sem = refs
    fetch = pltpu.make_async_copy(tokens, held, sem)
    fetch.start()
    rows, width = tokens.shape
    size = rows // len(chunks)
    f32, bf16 = jnp.float32, jnp.bfloat16
    full = jnp.zeros((experts, rows), f32)
    for k in range(routes.shape[0]):
        full += jnp.where(iota((experts, rows), 0) == routes[k : k + 1], weights[k : k + 1], 0.0)
    high = full.astype(bf16).astype(f32)
    mid = (full - high).astype(bf16).astype(f32)
    parts = jnp.concatenate([high, mid, full - high - mid], 0).astype(bf16)
    spread = (iota((3 * experts, LANES), 0) == iota((3 * experts, LANES), 1)).astype(bf16)
    ext = contract(parts, spread, 0, 0).astype(bf16)
    gray = jnp.zeros((1, rows), jnp.int32)
    bit = jnp.zeros((1, rows), jnp.int32)
    for z in range(experts // 2):
        named = jnp.zeros((1, rows), jnp.int32)
        for k in range(routes.shape[0]):
            named += (routes[k : k + 1] == idx[5] + 2 * z).astype(jnp.int32)
        bit = bit ^ named
        gray = gray * 2 + bit
    across = jnp.broadcast_to(gray.astype(f32), (rows, rows))
    first, second = iota((rows, rows), 0), iota((rows, rows), 1)
    top = jnp.where(first[:8] == 0, across[:8], 0.0).astype(bf16)
    down = contract(top, jnp.ones((8, rows), bf16), 0, 0)
    ahead = (down < across) | ((down == across) & (first < second))
    rank = jnp.sum(ahead.astype(f32), axis=0, keepdims=True).astype(jnp.int32)
    target = rank % len(chunks) * size + rank // len(chunks)
    order = (first == target).astype(bf16)
    order_out[...] = order
    ext = dot32(order, ext).astype(bf16)
    for q, chunk in enumerate(chunks):
        chunk[:, width:] = ext[q * size : (q + 1) * size]
    fetch.wait()
    step = 1024
    for n in range(0, width, step):
        moved = dot32(order, held[:, n : n + step]).astype(bf16)
        for q, chunk in enumerate(chunks):
            chunk[:, n : n + step] = moved[q * size : (q + 1) * size]


def pick_kernel(experts, mode, idx, *refs):
    *blocks, own_out, cross_out, pick_out = refs
    total = blocks[0].shape[1]
    rows = blocks[0].shape[0] * (len(blocks) if mode == "both" else 1)
    own_rows, cross_rows = own_out.shape[0], cross_out.shape[0]
    inner = idx[3] == 1

    def load(cols):
        if mode == "both":
            return jnp.concatenate([b[:, cols] for b in blocks], 0)
        if mode == "either":
            return jnp.where(inner, blocks[0][:, cols], blocks[1][:, cols])
        return blocks[0][:, cols]

    ext = load(slice(total - LANES, total))

    def picks(expert, count):
        mask = jnp.broadcast_to(scale_of(ext, expert, experts) > 0, (rows, LANES)).astype(jnp.bfloat16)
        upto = (iota((rows, rows), 0) <= iota((rows, rows), 1)).astype(jnp.bfloat16)
        place = contract(mask, upto, 0, 0)[:count]
        named = contract(mask, eye(rows), 0, 0)[:count]
        slot = iota((count, rows), 0).astype(jnp.float32)
        return ((named > 0.5) & (place - 1.0 == slot)).astype(jnp.float32)

    own = picks(idx[1], own_rows) if mode == "both" else eye(rows).astype(jnp.float32)
    pick = jnp.concatenate([own, picks(idx[2], cross_rows)], 0).astype(jnp.bfloat16)
    pick_out[...] = pick
    step = total // 3
    for n in range(0, total, step):
        got = dot32(pick, load(slice(n, n + step)))
        own_out[:, n : n + step] = got[:own_rows].astype(jnp.bfloat16)
        cross_out[:, n : n + step] = got[own_rows:].astype(jnp.bfloat16)


def expert_kernel(experts, idx, own, cross, ga, gb, ua, ub, da, db, own_out, cross_out, hidden):
    own_rows, total = own.shape
    width = total - LANES
    core, expert = idx[0], idx[1]
    half = ga.shape[0]
    x = jnp.concatenate([own[:, :width], cross[:, :width]], 0)
    ext = jnp.concatenate([own[:, width:], cross[:, width:]], 0)
    lane = iota((8, LANES), 1)
    mine = ((lane % experts == expert) & (lane < 3 * experts)).astype(jnp.bfloat16)
    scale = contract(mine, ext, 1, 1)[:1]
    for place, g, u in ((core, ga, ua), (1 - core, gb, ub)):
        gate = contract(g[...], x, 1, 1)
        upval = contract(u[...], x, 1, 1)
        made = gate / (1.0 + jnp.exp(-gate)) * upval * scale
        hidden[place] = made.T.astype(jnp.bfloat16)
    step = 512
    cols = da.shape[1]
    for n in range(0, 2 * cols, step):
        d, m = (da, n) if n < cols else (db, n - cols)
        made = dot32(hidden[0], d[:half, m : m + step]) + dot32(hidden[1], d[half:, m : m + step])
        own_out[:, n : n + step] = made[:own_rows].astype(jnp.bfloat16)
        cross_out[:, n : n + step] = made[own_rows:].astype(jnp.bfloat16)


def combine_kernel(first, idx, pick, own, cross, *refs):
    *more, out = refs
    width = own.shape[1]
    rows = slice(first, first + out.shape[0])
    step = 1024
    for n in range(0, width, step):
        cols = slice(n, n + step)
        got = contract(pick[...], jnp.concatenate([own[:, cols], cross[:, cols]], 0), 0, 0)[rows]
        for ref in more:
            got += ref[:, cols].astype(jnp.float32)
        out[:, cols] = got.astype(jnp.bfloat16)


def finish_kernel(half, idx, order, pick, own, cross, *refs):
    *more, out, held, sems = refs
    width = own.shape[1]
    step = 1024
    copies = []
    for i, n in enumerate(range(0, width, step)):
        cols = slice(n, n + step)
        got = contract(pick[...], jnp.concatenate([own[:, cols], cross[:, cols]], 0), 0, 0)
        sums = [sum(r[:, cols].astype(jnp.float32) for r in part) for part in (more[:half], more[half:])]
        got = (got + jnp.concatenate(sums, 0)).astype(jnp.bfloat16)
        held[i] = contract(order[...], got, 0, 0).astype(jnp.bfloat16)
        to = pl.ds(pl.multiple_of((idx[4] + n) % width, step), step)
        copies.append(pltpu.make_async_copy(held.at[i], out.at[:, to], sems.at[i]))
        copies[-1].start()
    for c in copies:
        c.wait()


def fence_kernel(idx):
    pass


def run_copies(sems, pairs):
    copies = [pltpu.make_async_copy(s, d, sems.at[i]) for i, (s, d) in enumerate(pairs)]
    for c in copies:
        c.start()
    for c in copies:
        c.wait()


def fetch_kernel(idx, *refs):
    count = len(refs) // 2
    run_copies(refs[-1], zip(refs[:count], refs[count:-1]))


def call(name, kernel, outs, idx, token, args, passes=(), scratch=(), cost=1, left=(), away=False):
    vmem, anywhere = pl.BlockSpec(memory_space=pltpu.VMEM), pl.BlockSpec(memory_space=pl.ANY)
    through = [token, *passes]
    first = 1 + len(args) + len(left)

    def body(*refs):
        ins, rest = refs[:first], refs[first + len(through) :]
        kernel(*ins, *rest[: len(outs)], *rest[len(outs) + len(through) :])

    got = pl.pallas_call(
        body,
        out_shape=[*outs, *(jax.ShapeDtypeStruct(x.shape, x.dtype) for x in through)],
        in_specs=[pl.BlockSpec(memory_space=pltpu.SMEM)]
        + [vmem] * len(args)
        + [anywhere] * len(left)
        + [anywhere] * len(through),
        out_specs=[anywhere if away else vmem] * len(outs) + [anywhere] * len(through),
        input_output_aliases={first + i: len(outs) + i for i in range(len(through))},
        scratch_shapes=list(scratch),
        name=name,
        compiler_params=pltpu.CompilerParams(vmem_limit_bytes=LIMIT),
        cost_estimate=pl.CostEstimate(flops=1, bytes_accessed=cost, transcendentals=0),
    )(idx, *args, *left, *through)
    return got[: len(outs)], got[len(outs)], got[len(outs) + 1 :]


ORDER = [
    ["prep", "EA", "MB", "EB"],
    ["P0", "NA", "Y0"],
    ["f", "OB", "+wg", "+wu"],
    ["W"],
    ["f", "MA"],
    ["P1", "Y1"],
    ["P2B", "QA", "Y2B", "NB"],
    ["F0", "OA"],
    ["P3A", "Y3A", "+Y1"],
    ["F2B", "R2B"],
    ["f", "QB", "+Y3A"],
    ["P2A"],
    ["f", "Y2A"],
    ["F3A"],
    ["C2B", "I2B"],
    ["P3B", "Y3B", "+Y2A"],
    ["F1", "R3A"],
    ["F3B", "+I2B"],
    ["D2B", "R3B"],
    ["C3A", "I3A", "S2B"],
    ["F2A"],
    ["C3B", "I3B", "R2A", "+R3A"],
    ["D3A", "S3A"],
    ["C2A", "R1", "I2A", "+S2B"],
    ["D3B", "S3B", "+R2A"],
    ["D1A", "S1A", "R0"],
    ["D2A", "+R1"],
    ["D1B", "S2A", "S1B", "+I2A"],
    ["fin"],
]


def lined(tokens, routes, route_weights, gate_weight, up_weight, down_weight):
    tok_rows, top_count = routes.shape
    width = tokens.shape[1]
    devices = lax.axis_size("expert")
    experts = devices // 2
    capacity = tok_rows * top_count // experts
    half = gate_weight.shape[1]
    index = lax.axis_index("expert")
    core, side, line = index % 2, index // 2 % 2, index // 4
    inner = ((line == 1) | (line == 2)).astype(jnp.int32)
    idx = jnp.stack(
        [core, 2 * line + side, 2 * line + 1 - side, inner, core * down_weight.shape[1], 1 - side]
    ).astype(jnp.int32)
    rows = tok_rows // 2
    total = width + LANES
    bf16 = jnp.bfloat16

    def in_hbm(x):
        return pltpu.with_memory_space_constraint(x, pltpu.HBM)

    def like(*shape):
        return jax.ShapeDtypeStruct(shape, bf16)

    gate, up = gate_weight.T, up_weight.T

    val = {}
    for name, w in (("wg", gate), ("wu", up), ("wd", down_weight)):
        with jax.named_scope("move_" + name):
            val[name] = swapped(w, "expert", 0)
    steps = {name for name, *_ in ORDER}
    slots = {name[1:] for name in steps if name[0] == "P"}

    def kernel_of(name):
        kind, q = name[:-1], name[-1]
        if name == "prep":
            return (
                functools.partial(prepare_kernel, experts),
                [like(rows, total), like(rows, total), like(tok_rows, tok_rows)],
                [in_hbm(routes.T), in_hbm(route_weights.T)],
                [pltpu.VMEM(tokens.shape, bf16), pltpu.SemaphoreType.DMA],
            )
        if name[0] == "P":
            slot = name[1:]
            if slot in ("0", "1"):
                blocks, mode = [["payA", "payB"], ["EA", "EB"]][int(slot)], "both"
                own, cross, size = capacity, capacity, tok_rows
            else:
                blocks = {"1": ["E" + q], "2": ["M" + q, "O" + q], "3": ["N" + q, "Q" + q]}[slot[0]]
                mode = "one" if len(blocks) == 1 else "either"
                own, cross, size = rows, CROSS_ROWS, rows
            return (
                functools.partial(pick_kernel, experts, mode),
                [like(own, total), like(cross, total), like(own + cross, size)],
                [val[b] for b in blocks],
                [],
            )
        if name[0] == "F":
            own, cross = val["own" + name[1:]], val["Y" + name[1:]]
            weights = [gate, val["vg"], up, val["vu"], down_weight, val["vd"]]
            weights = [pltpu.with_memory_space_constraint(w, pltpu.VMEM) for w in weights]
            args = [own, cross, *weights]
            return (
                functools.partial(expert_kernel, experts),
                [like(own.shape[0], width), like(cross.shape[0], width)],
                args,
                [pltpu.VMEM((2, own.shape[0] + cross.shape[0], half), bf16)],
            )
        if name == "W":
            outs = [pltpu.VMEM(w.shape, bf16) for w in (gate, up, down_weight)]
            return fetch_kernel, outs, [], [pltpu.SemaphoreType.DMA((3,))]
        if name == "fin":
            made = [val["order"], val["pick0"], val["made0"], val["R0"]]
            made += [val[s + q] for q in "AB" for s in ("S1", "S2", "X3") if s + q in val]
            counts = [sum(s + q in val for s in ("S1", "S2", "X3")) for q in "AB"]
            parts = width // 1024
            scratch = [pltpu.VMEM((parts, tok_rows, 1024), bf16), pltpu.SemaphoreType.DMA((parts,))]
            return functools.partial(finish_kernel, counts[0]), [like(tok_rows, width)], made, scratch
        slot = name[1:] if name[1:] in slots else name[1]
        made = [val[s + slot] for s in ("pick", "made", "R")]
        made += [val[x] for x in {"D2": ["I2" + q], "D3": ["I3" + q], "D1": ["S3" + q]}.get(kind, [])]
        first = rows if slot == name[1] and q == "B" else 0
        return functools.partial(combine_kernel, first), [like(rows, width)], made, []

    def keep(name, got):
        slot = name[1:]
        if name == "prep":
            val["payA"], val["payB"], val["order"] = got
        elif name[0] == "P":
            val["own" + slot], val["cross" + slot], val["pick" + slot] = got
        elif name == "W":
            val["vg"], val["vu"], val["vd"] = got
        elif name[0] == "F":
            val["made" + slot], val["back" + slot] = got
        else:
            val[name] = got[0]

    def move_of(name):
        kind, slot, q = name[0], name[1:], name[-1]
        if kind == "Y":
            return "cross" + slot, lambda x: swapped(x, "expert", 1)
        if kind == "R":
            return "back" + slot, lambda x: swapped(x, "expert", 1)
        source, pairs = {
            "E": ("pay" + q, OUTER),
            "M": ("pay" + q, MIDDLE),
            "O": ("M" + q, OUT),
            "N": ("E" + q, MIDDLE),
            "Q": ("N" + q, OUT),
            "I2": ("C2" + q, IN),
            "S2": ("D2" + q, MIDDLE),
            "X3": ("C3" + q, ENDS),
            "I3": ("C3" + q, IN),
            "S3": (("D3" if "D3" + q in steps else "C3") + q, MIDDLE),
            "S1": ("D1" + q, OUTER),
        }[name[:-1]]
        return source, lambda x: along_line(x, pairs)

    token = jnp.zeros((8, LANES), jnp.float32)
    for name, *moves in ORDER:
        done = [m[1:] for m in moves if m[0] == "+"]
        moves = [m for m in moves if m[0] != "+"]
        sources = {m: move_of(m)[0] for m in moves}
        passed = sorted({s for s in [*sources.values(), *done] if s in val})
        if name == "f":
            _, token, through = call("fence", fence_kernel, [], idx, token, [], passes=[val[s] for s in passed])
        else:
            kernel, outs, args, scratch = kernel_of(name)
            cost = sum(x.size * x.dtype.itemsize for x in [*args, *outs]) if name[0] == "F" else 1
            through = [val[s] for s in passed]
            left = {"prep": [in_hbm(tokens)], "W": [val["wg"], val["wu"], val["wd"]]}.get(name, [])
            got, token, through = call(name, kernel, outs, idx, token, args, through, scratch, cost, left, name == "fin")
            keep(name, got)
        val.update(zip(passed, through))
        for m in moves:
            with jax.named_scope("move_" + m):
                val[m] = move_of(m)[1](val[sources[m]])
    return val["fin"]


def solution(mesh):
    body = lined if mesh.shape["expert"] == 16 else dispatched
    return jax.shard_map(
        body,
        mesh=mesh,
        in_specs=(
            P(("groups", "expert"), None),
            P(("groups", "expert"), None),
            P(("groups", "expert"), None),
            P(None, "expert"),
            P(None, "expert"),
            P(None, "expert"),
        ),
        out_specs=P(("groups", "expert"), None),
        check_vma=False,
    )
```

```python
import functools

import jax
import jax.experimental.pallas as pl
import jax.experimental.pallas.tpu as pltpu
import jax.numpy as jnp
from jax import lax
from jax.sharding import PartitionSpec as P

CROSS_ROWS = 40
LANES = 128
LIMIT = 12 << 20


def swapped(x, axis, apart):
    return lax.ppermute(x, axis, [(i, i ^ 1 << apart) for i in range(lax.axis_size(axis))])


def dot32(a, b):
    return jnp.dot(a, b, preferred_element_type=jnp.float32)


def expert_hidden(rows, gate_part, up_part, parity):
    gate = dot32(rows, gate_part)
    upval = dot32(rows, up_part)
    hidden = (jax.nn.silu(gate) * upval).astype(jnp.bfloat16)
    partner = swapped(hidden, "expert", 0)
    return jnp.where(
        parity == 0, jnp.concatenate([hidden, partner], 1), jnp.concatenate([partner, hidden], 1)
    )


def dispatched(tokens, routes, route_weights, gate_weight, up_weight, down_weight):
    tok_rows, top_count = routes.shape
    width = tokens.shape[1]
    half_width = down_weight.shape[1]
    devices = lax.axis_size("expert")
    experts = devices // 2
    capacity = tok_rows * top_count // experts
    parity = lax.axis_index("expert") % 2
    flat = routes.reshape(-1)
    onehot = (flat[:, None] == jnp.arange(experts, dtype=jnp.int32)[None, :]).astype(jnp.int32)
    before = jnp.cumsum(onehot, axis=0) - onehot
    slot_of = jnp.sum(before * onehot, axis=1)
    position = flat * capacity + slot_of
    assign_ids = jnp.arange(flat.shape[0], dtype=jnp.int32) // top_count
    owner = jnp.zeros((experts * capacity,), jnp.int32).at[position].set(assign_ids)
    gathered = tokens[owner]
    outgoing = jnp.broadcast_to(
        gathered.reshape(experts, 1, capacity, width), (experts, 2, capacity, width)
    )
    outgoing = outgoing.reshape(devices, capacity, width)
    received = lax.all_to_all(outgoing, "expert", split_axis=0, concat_axis=0, tiled=True)
    count, items, _ = received.shape
    hidden = expert_hidden(received.reshape(count * items, width), gate_weight, up_weight, parity)
    produced = dot32(hidden, down_weight).astype(jnp.bfloat16)
    returned = lax.all_to_all(
        produced.reshape(count, items, half_width),
        "expert",
        split_axis=0,
        concat_axis=0,
        tiled=True,
    )
    returned = returned.reshape(experts, 2, capacity, half_width).transpose(0, 2, 1, 3)
    expert_rows = returned.reshape(experts * capacity, width)
    picked = expert_rows[position].reshape(tok_rows, top_count, width)
    mixed = jnp.einsum("tk,tkd->td", route_weights, picked.astype(jnp.float32))
    return mixed.astype(jnp.bfloat16)


def along_line(x, pairs):
    moves = [((a * 2 + s) * 2 + c, (b * 2 + s) * 2 + c) for a, b in pairs for s in (0, 1) for c in (0, 1)]
    return lax.ppermute(x, "expert", moves)


OUTER = [(0, 1), (1, 0), (2, 3), (3, 2)]
MIDDLE = [(1, 2), (2, 1)]
OUT = [(1, 0), (2, 3)]
IN = [(0, 1), (3, 2)]
ENDS = [(0, 3), (3, 0)]


def contract(a, b, da, db):
    return lax.dot_general(a, b, (((da,), (db,)), ((), ())), preferred_element_type=jnp.float32)


def iota(shape, dim):
    return lax.broadcasted_iota(jnp.int32, shape, dim)


def eye(n):
    return (iota((n, n), 0) == iota((n, n), 1)).astype(jnp.bfloat16)


def scale_of(ext, expert, experts):
    lane = iota(ext.shape, 1)
    mine = (lane % experts == expert) & (lane < 3 * experts)
    return jnp.sum(jnp.where(mine, ext.astype(jnp.float32), 0.0), axis=1, keepdims=True)


def prepare_kernel(experts, idx, routes, weights, tokens, *refs):
    *chunks, order_out, held, sem = refs
    fetch = pltpu.make_async_copy(tokens, held, sem)
    fetch.start()
    rows, width = tokens.shape
    size = rows // len(chunks)
    f32, bf16 = jnp.float32, jnp.bfloat16
    full = jnp.zeros((experts, rows), f32)
    for k in range(routes.shape[0]):
        full += jnp.where(iota((experts, rows), 0) == routes[k : k + 1], weights[k : k + 1], 0.0)
    high = full.astype(bf16).astype(f32)
    mid = (full - high).astype(bf16).astype(f32)
    parts = jnp.concatenate([high, mid, full - high - mid], 0).astype(bf16)
    spread = (iota((3 * experts, LANES), 0) == iota((3 * experts, LANES), 1)).astype(bf16)
    ext = contract(parts, spread, 0, 0).astype(bf16)
    gray = jnp.zeros((1, rows), jnp.int32)
    bit = jnp.zeros((1, rows), jnp.int32)
    for z in range(experts // 2):
        named = jnp.zeros((1, rows), jnp.int32)
        for k in range(routes.shape[0]):
            named += (routes[k : k + 1] == idx[5] + 2 * z).astype(jnp.int32)
        bit = bit ^ named
        gray = gray * 2 + bit
    across = jnp.broadcast_to(gray.astype(f32), (rows, rows))
    first, second = iota((rows, rows), 0), iota((rows, rows), 1)
    top = jnp.where(first[:8] == 0, across[:8], 0.0).astype(bf16)
    down = contract(top, jnp.ones((8, rows), bf16), 0, 0)
    ahead = (down < across) | ((down == across) & (first < second))
    rank = jnp.sum(ahead.astype(f32), axis=0, keepdims=True).astype(jnp.int32)
    target = rank % len(chunks) * size + rank // len(chunks)
    order = (first == target).astype(bf16)
    order_out[...] = order
    ext = dot32(order, ext).astype(bf16)
    for q, chunk in enumerate(chunks):
        chunk[:, width:] = ext[q * size : (q + 1) * size]
    fetch.wait()
    step = 1024
    for n in range(0, width, step):
        moved = dot32(order, held[:, n : n + step]).astype(bf16)
        for q, chunk in enumerate(chunks):
            chunk[:, n : n + step] = moved[q * size : (q + 1) * size]


def pick_kernel(experts, mode, idx, *refs):
    *blocks, own_out, cross_out, pick_out = refs
    total = blocks[0].shape[1]
    rows = blocks[0].shape[0] * (len(blocks) if mode == "both" else 1)
    own_rows, cross_rows = own_out.shape[0], cross_out.shape[0]
    inner = idx[3] == 1

    def load(cols):
        if mode == "both":
            return jnp.concatenate([b[:, cols] for b in blocks], 0)
        if mode == "either":
            return jnp.where(inner, blocks[0][:, cols], blocks[1][:, cols])
        return blocks[0][:, cols]

    ext = load(slice(total - LANES, total))

    def picks(expert, count):
        mask = jnp.broadcast_to(scale_of(ext, expert, experts) > 0, (rows, LANES)).astype(jnp.bfloat16)
        upto = (iota((rows, rows), 0) <= iota((rows, rows), 1)).astype(jnp.bfloat16)
        place = contract(mask, upto, 0, 0)[:count]
        named = contract(mask, eye(rows), 0, 0)[:count]
        slot = iota((count, rows), 0).astype(jnp.float32)
        return ((named > 0.5) & (place - 1.0 == slot)).astype(jnp.float32)

    own = picks(idx[1], own_rows) if mode == "both" else eye(rows).astype(jnp.float32)
    pick = jnp.concatenate([own, picks(idx[2], cross_rows)], 0).astype(jnp.bfloat16)
    pick_out[...] = pick
    step = total // 3
    for n in range(0, total, step):
        got = dot32(pick, load(slice(n, n + step)))
        own_out[:, n : n + step] = got[:own_rows].astype(jnp.bfloat16)
        cross_out[:, n : n + step] = got[own_rows:].astype(jnp.bfloat16)


def expert_kernel(experts, idx, own, cross, ga, gb, ua, ub, da, db, own_out, cross_out, hidden):
    own_rows, total = own.shape
    width = total - LANES
    core, expert = idx[0], idx[1]
    half = ga.shape[0]
    x = jnp.concatenate([own[:, :width], cross[:, :width]], 0)
    ext = jnp.concatenate([own[:, width:], cross[:, width:]], 0)
    lane = iota((8, LANES), 1)
    mine = ((lane % experts == expert) & (lane < 3 * experts)).astype(jnp.bfloat16)
    scale = contract(mine, ext, 1, 1)[:1]
    for place, g, u in ((core, ga, ua), (1 - core, gb, ub)):
        gate = contract(g[...], x, 1, 1)
        upval = contract(u[...], x, 1, 1)
        made = gate / (1.0 + jnp.exp(-gate)) * upval * scale
        hidden[place] = made.T.astype(jnp.bfloat16)
    step = 512
    cols = da.shape[1]
    for n in range(0, 2 * cols, step):
        d, m = (da, n) if n < cols else (db, n - cols)
        made = dot32(hidden[0], d[:half, m : m + step]) + dot32(hidden[1], d[half:, m : m + step])
        own_out[:, n : n + step] = made[:own_rows].astype(jnp.bfloat16)
        cross_out[:, n : n + step] = made[own_rows:].astype(jnp.bfloat16)


def combine_kernel(first, idx, pick, own, cross, *refs):
    *more, out = refs
    width = own.shape[1]
    rows = slice(first, first + out.shape[0])
    step = 1024
    for n in range(0, width, step):
        cols = slice(n, n + step)
        got = contract(pick[...], jnp.concatenate([own[:, cols], cross[:, cols]], 0), 0, 0)[rows]
        for ref in more:
            got += ref[:, cols].astype(jnp.float32)
        out[:, cols] = got.astype(jnp.bfloat16)


def finish_kernel(half, idx, order, pick, own, cross, *refs):
    *more, out, held, sems = refs
    width = own.shape[1]
    step = 1024
    copies = []
    for i, n in enumerate(range(0, width, step)):
        cols = slice(n, n + step)
        got = contract(pick[...], jnp.concatenate([own[:, cols], cross[:, cols]], 0), 0, 0)
        sums = [sum(r[:, cols].astype(jnp.float32) for r in part) for part in (more[:half], more[half:])]
        got = (got + jnp.concatenate(sums, 0)).astype(jnp.bfloat16)
        held[i] = contract(order[...], got, 0, 0).astype(jnp.bfloat16)
        to = pl.ds(pl.multiple_of((idx[4] + n) % width, step), step)
        copies.append(pltpu.make_async_copy(held.at[i], out.at[:, to], sems.at[i]))
        copies[-1].start()
    for c in copies:
        c.wait()


def fence_kernel(idx):
    pass


def run_copies(sems, pairs):
    copies = [pltpu.make_async_copy(s, d, sems.at[i]) for i, (s, d) in enumerate(pairs)]
    for c in copies:
        c.start()
    for c in copies:
        c.wait()


def fetch_kernel(idx, *refs):
    count = len(refs) // 2
    run_copies(refs[-1], zip(refs[:count], refs[count:-1]))


def call(name, kernel, outs, idx, token, args, passes=(), scratch=(), cost=1, left=(), away=False):
    vmem, anywhere = pl.BlockSpec(memory_space=pltpu.VMEM), pl.BlockSpec(memory_space=pl.ANY)
    through = [token, *passes]
    first = 1 + len(args) + len(left)

    def body(*refs):
        ins, rest = refs[:first], refs[first + len(through) :]
        kernel(*ins, *rest[: len(outs)], *rest[len(outs) + len(through) :])

    got = pl.pallas_call(
        body,
        out_shape=[*outs, *(jax.ShapeDtypeStruct(x.shape, x.dtype) for x in through)],
        in_specs=[pl.BlockSpec(memory_space=pltpu.SMEM)]
        + [vmem] * len(args)
        + [anywhere] * len(left)
        + [anywhere] * len(through),
        out_specs=[anywhere if away else vmem] * len(outs) + [anywhere] * len(through),
        input_output_aliases={first + i: len(outs) + i for i in range(len(through))},
        scratch_shapes=list(scratch),
        name=name,
        compiler_params=pltpu.CompilerParams(vmem_limit_bytes=LIMIT),
        cost_estimate=pl.CostEstimate(flops=1, bytes_accessed=cost, transcendentals=0),
    )(idx, *args, *left, *through)
    return got[: len(outs)], got[len(outs)], got[len(outs) + 1 :]


ORDER = [
    ["prep", "EA", "MB", "EB"],
    ["P0", "NA", "Y0"],
    ["f", "OB", "+wg", "+wu"],
    ["W"],
    ["f", "MA"],
    ["P1", "Y1", "QA"],
    ["P2B", "Y2B", "NB"],
    ["F0", "OA"],
    ["P3A", "Y3A", "+Y1"],
    ["F2B", "R2B"],
    ["f", "QB", "+Y3A"],
    ["P2A"],
    ["f", "Y2A"],
    ["F3A"],
    ["C2B", "I2B"],
    ["P3B", "Y3B", "+Y2A"],
    ["F1", "R3A"],
    ["F3B", "+I2B"],
    ["D2B", "R3B"],
    ["C3A", "I3A", "S2B"],
    ["F2A"],
    ["C3B", "I3B", "R2A", "+R3A"],
    ["D3A", "S3A"],
    ["C2A", "R1", "I2A", "+S2B"],
    ["D3B", "S3B", "+R2A"],
    ["D1A", "S1A", "R0"],
    ["D2A", "+R1"],
    ["D1B", "S2A", "S1B", "+I2A"],
    ["fin"],
]


def lined(tokens, routes, route_weights, gate_weight, up_weight, down_weight):
    tok_rows, top_count = routes.shape
    width = tokens.shape[1]
    devices = lax.axis_size("expert")
    experts = devices // 2
    capacity = tok_rows * top_count // experts
    half = gate_weight.shape[1]
    index = lax.axis_index("expert")
    core, side, line = index % 2, index // 2 % 2, index // 4
    inner = ((line == 1) | (line == 2)).astype(jnp.int32)
    idx = jnp.stack(
        [core, 2 * line + side, 2 * line + 1 - side, inner, core * down_weight.shape[1], 1 - side]
    ).astype(jnp.int32)
    rows = tok_rows // 2
    total = width + LANES
    bf16 = jnp.bfloat16

    def in_hbm(x):
        return pltpu.with_memory_space_constraint(x, pltpu.HBM)

    def like(*shape):
        return jax.ShapeDtypeStruct(shape, bf16)

    gate, up = gate_weight.T, up_weight.T

    val = {}
    for name, w in (("wg", gate), ("wu", up), ("wd", down_weight)):
        with jax.named_scope("move_" + name):
            val[name] = swapped(w, "expert", 0)
    steps = {name for name, *_ in ORDER}
    slots = {name[1:] for name in steps if name[0] == "P"}

    def kernel_of(name):
        kind, q = name[:-1], name[-1]
        if name == "prep":
            return (
                functools.partial(prepare_kernel, experts),
                [like(rows, total), like(rows, total), like(tok_rows, tok_rows)],
                [in_hbm(routes.T), in_hbm(route_weights.T)],
                [pltpu.VMEM(tokens.shape, bf16), pltpu.SemaphoreType.DMA],
            )
        if name[0] == "P":
            slot = name[1:]
            if slot in ("0", "1"):
                blocks, mode = [["payA", "payB"], ["EA", "EB"]][int(slot)], "both"
                own, cross, size = capacity, capacity, tok_rows
            else:
                blocks = {"1": ["E" + q], "2": ["M" + q, "O" + q], "3": ["N" + q, "Q" + q]}[slot[0]]
                mode = "one" if len(blocks) == 1 else "either"
                own, cross, size = rows, CROSS_ROWS, rows
            return (
                functools.partial(pick_kernel, experts, mode),
                [like(own, total), like(cross, total), like(own + cross, size)],
                [val[b] for b in blocks],
                [],
            )
        if name[0] == "F":
            own, cross = val["own" + name[1:]], val["Y" + name[1:]]
            weights = [gate, val["vg"], up, val["vu"], down_weight, val["vd"]]
            weights = [pltpu.with_memory_space_constraint(w, pltpu.VMEM) for w in weights]
            args = [own, cross, *weights]
            return (
                functools.partial(expert_kernel, experts),
                [like(own.shape[0], width), like(cross.shape[0], width)],
                args,
                [pltpu.VMEM((2, own.shape[0] + cross.shape[0], half), bf16)],
            )
        if name == "W":
            outs = [pltpu.VMEM(w.shape, bf16) for w in (gate, up, down_weight)]
            return fetch_kernel, outs, [], [pltpu.SemaphoreType.DMA((3,))]
        if name == "fin":
            made = [val["order"], val["pick0"], val["made0"], val["R0"]]
            made += [val[s + q] for q in "AB" for s in ("S1", "S2", "X3") if s + q in val]
            counts = [sum(s + q in val for s in ("S1", "S2", "X3")) for q in "AB"]
            parts = width // 1024
            scratch = [pltpu.VMEM((parts, tok_rows, 1024), bf16), pltpu.SemaphoreType.DMA((parts,))]
            return functools.partial(finish_kernel, counts[0]), [like(tok_rows, width)], made, scratch
        slot = name[1:] if name[1:] in slots else name[1]
        made = [val[s + slot] for s in ("pick", "made", "R")]
        made += [val[x] for x in {"D2": ["I2" + q], "D3": ["I3" + q], "D1": ["S3" + q]}.get(kind, [])]
        first = rows if slot == name[1] and q == "B" else 0
        return functools.partial(combine_kernel, first), [like(rows, width)], made, []

    def keep(name, got):
        slot = name[1:]
        if name == "prep":
            val["payA"], val["payB"], val["order"] = got
        elif name[0] == "P":
            val["own" + slot], val["cross" + slot], val["pick" + slot] = got
        elif name == "W":
            val["vg"], val["vu"], val["vd"] = got
        elif name[0] == "F":
            val["made" + slot], val["back" + slot] = got
        else:
            val[name] = got[0]

    def move_of(name):
        kind, slot, q = name[0], name[1:], name[-1]
        if kind == "Y":
            return "cross" + slot, lambda x: swapped(x, "expert", 1)
        if kind == "R":
            return "back" + slot, lambda x: swapped(x, "expert", 1)
        source, pairs = {
            "E": ("pay" + q, OUTER),
            "M": ("pay" + q, MIDDLE),
            "O": ("M" + q, OUT),
            "N": ("E" + q, MIDDLE),
            "Q": ("N" + q, OUT),
            "I2": ("C2" + q, IN),
            "S2": ("D2" + q, MIDDLE),
            "X3": ("C3" + q, ENDS),
            "I3": ("C3" + q, IN),
            "S3": (("D3" if "D3" + q in steps else "C3") + q, MIDDLE),
            "S1": ("D1" + q, OUTER),
        }[name[:-1]]
        return source, lambda x: along_line(x, pairs)

    token = jnp.zeros((8, LANES), jnp.float32)
    for name, *moves in ORDER:
        done = [m[1:] for m in moves if m[0] == "+"]
        moves = [m for m in moves if m[0] != "+"]
        sources = {m: move_of(m)[0] for m in moves}
        passed = sorted({s for s in [*sources.values(), *done] if s in val})
        if name == "f":
            _, token, through = call("fence", fence_kernel, [], idx, token, [], passes=[val[s] for s in passed])
        else:
            kernel, outs, args, scratch = kernel_of(name)
            cost = sum(x.size * x.dtype.itemsize for x in [*args, *outs]) if name[0] == "F" else 1
            through = [val[s] for s in passed]
            left = {"prep": [in_hbm(tokens)], "W": [val["wg"], val["wu"], val["wd"]]}.get(name, [])
            got, token, through = call(name, kernel, outs, idx, token, args, through, scratch, cost, left, name == "fin")
            keep(name, got)
        val.update(zip(passed, through))
        for m in moves:
            with jax.named_scope("move_" + m):
                val[m] = move_of(m)[1](val[sources[m]])
    return val["fin"]


def solution(mesh):
    body = lined if mesh.shape["expert"] == 16 else dispatched
    return jax.shard_map(
        body,
        mesh=mesh,
        in_specs=(
            P(("groups", "expert"), None),
            P(("groups", "expert"), None),
            P(("groups", "expert"), None),
            P(None, "expert"),
            P(None, "expert"),
            P(None, "expert"),
        ),
        out_specs=P(("groups", "expert"), None),
        check_vma=False,
    )
```

```python
import functools

import jax
import jax.experimental.pallas as pl
import jax.experimental.pallas.tpu as pltpu
import jax.numpy as jnp
from jax import lax
from jax.sharding import PartitionSpec as P

CROSS_ROWS = 40
LANES = 128
LIMIT = 12 << 20


def swapped(x, axis, apart):
    return lax.ppermute(x, axis, [(i, i ^ 1 << apart) for i in range(lax.axis_size(axis))])


def dot32(a, b):
    return jnp.dot(a, b, preferred_element_type=jnp.float32)


def expert_hidden(rows, gate_part, up_part, parity):
    gate = dot32(rows, gate_part)
    upval = dot32(rows, up_part)
    hidden = (jax.nn.silu(gate) * upval).astype(jnp.bfloat16)
    partner = swapped(hidden, "expert", 0)
    return jnp.where(
        parity == 0, jnp.concatenate([hidden, partner], 1), jnp.concatenate([partner, hidden], 1)
    )


def dispatched(tokens, routes, route_weights, gate_weight, up_weight, down_weight):
    tok_rows, top_count = routes.shape
    width = tokens.shape[1]
    half_width = down_weight.shape[1]
    devices = lax.axis_size("expert")
    experts = devices // 2
    capacity = tok_rows * top_count // experts
    parity = lax.axis_index("expert") % 2
    flat = routes.reshape(-1)
    onehot = (flat[:, None] == jnp.arange(experts, dtype=jnp.int32)[None, :]).astype(jnp.int32)
    before = jnp.cumsum(onehot, axis=0) - onehot
    slot_of = jnp.sum(before * onehot, axis=1)
    position = flat * capacity + slot_of
    assign_ids = jnp.arange(flat.shape[0], dtype=jnp.int32) // top_count
    owner = jnp.zeros((experts * capacity,), jnp.int32).at[position].set(assign_ids)
    gathered = tokens[owner]
    outgoing = jnp.broadcast_to(
        gathered.reshape(experts, 1, capacity, width), (experts, 2, capacity, width)
    )
    outgoing = outgoing.reshape(devices, capacity, width)
    received = lax.all_to_all(outgoing, "expert", split_axis=0, concat_axis=0, tiled=True)
    count, items, _ = received.shape
    hidden = expert_hidden(received.reshape(count * items, width), gate_weight, up_weight, parity)
    produced = dot32(hidden, down_weight).astype(jnp.bfloat16)
    returned = lax.all_to_all(
        produced.reshape(count, items, half_width),
        "expert",
        split_axis=0,
        concat_axis=0,
        tiled=True,
    )
    returned = returned.reshape(experts, 2, capacity, half_width).transpose(0, 2, 1, 3)
    expert_rows = returned.reshape(experts * capacity, width)
    picked = expert_rows[position].reshape(tok_rows, top_count, width)
    mixed = jnp.einsum("tk,tkd->td", route_weights, picked.astype(jnp.float32))
    return mixed.astype(jnp.bfloat16)


def along_line(x, pairs):
    moves = [((a * 2 + s) * 2 + c, (b * 2 + s) * 2 + c) for a, b in pairs for s in (0, 1) for c in (0, 1)]
    return lax.ppermute(x, "expert", moves)


OUTER = [(0, 1), (1, 0), (2, 3), (3, 2)]
MIDDLE = [(1, 2), (2, 1)]
OUT = [(1, 0), (2, 3)]
IN = [(0, 1), (3, 2)]
ENDS = [(0, 3), (3, 0)]


def contract(a, b, da, db):
    return lax.dot_general(a, b, (((da,), (db,)), ((), ())), preferred_element_type=jnp.float32)


def iota(shape, dim):
    return lax.broadcasted_iota(jnp.int32, shape, dim)


def eye(n):
    return (iota((n, n), 0) == iota((n, n), 1)).astype(jnp.bfloat16)


def scale_of(ext, expert, experts):
    lane = iota(ext.shape, 1)
    mine = (lane % experts == expert) & (lane < 3 * experts)
    return jnp.sum(jnp.where(mine, ext.astype(jnp.float32), 0.0), axis=1, keepdims=True)


def prepare_kernel(experts, idx, routes, weights, tokens, *refs):
    *chunks, order_out, held, sem = refs
    fetch = pltpu.make_async_copy(tokens, held, sem)
    fetch.start()
    rows, width = tokens.shape
    size = rows // len(chunks)
    f32, bf16 = jnp.float32, jnp.bfloat16
    full = jnp.zeros((experts, rows), f32)
    for k in range(routes.shape[0]):
        full += jnp.where(iota((experts, rows), 0) == routes[k : k + 1], weights[k : k + 1], 0.0)
    high = full.astype(bf16).astype(f32)
    mid = (full - high).astype(bf16).astype(f32)
    parts = jnp.concatenate([high, mid, full - high - mid], 0).astype(bf16)
    spread = (iota((3 * experts, LANES), 0) == iota((3 * experts, LANES), 1)).astype(bf16)
    ext = contract(parts, spread, 0, 0).astype(bf16)
    gray = jnp.zeros((1, rows), jnp.int32)
    bit = jnp.zeros((1, rows), jnp.int32)
    for z in range(experts // 2):
        named = jnp.zeros((1, rows), jnp.int32)
        for k in range(routes.shape[0]):
            named += (routes[k : k + 1] == idx[5] + 2 * z).astype(jnp.int32)
        bit = bit ^ named
        gray = gray * 2 + bit
    across = jnp.broadcast_to(gray.astype(f32), (rows, rows))
    first, second = iota((rows, rows), 0), iota((rows, rows), 1)
    top = jnp.where(first[:8] == 0, across[:8], 0.0).astype(bf16)
    down = contract(top, jnp.ones((8, rows), bf16), 0, 0)
    ahead = (down < across) | ((down == across) & (first < second))
    rank = jnp.sum(ahead.astype(f32), axis=0, keepdims=True).astype(jnp.int32)
    target = rank % len(chunks) * size + rank // len(chunks)
    order = (first == target).astype(bf16)
    order_out[...] = order
    ext = dot32(order, ext).astype(bf16)
    for q, chunk in enumerate(chunks):
        chunk[:, width:] = ext[q * size : (q + 1) * size]
    fetch.wait()
    step = 1024
    for n in range(0, width, step):
        moved = dot32(order, held[:, n : n + step]).astype(bf16)
        for q, chunk in enumerate(chunks):
            chunk[:, n : n + step] = moved[q * size : (q + 1) * size]


def pick_kernel(experts, mode, idx, *refs):
    *blocks, own_out, cross_out, pick_out = refs
    total = blocks[0].shape[1]
    rows = blocks[0].shape[0] * (len(blocks) if mode == "both" else 1)
    own_rows, cross_rows = own_out.shape[0], cross_out.shape[0]
    inner = idx[3] == 1

    def load(cols):
        if mode == "both":
            return jnp.concatenate([b[:, cols] for b in blocks], 0)
        if mode == "either":
            return jnp.where(inner, blocks[0][:, cols], blocks[1][:, cols])
        return blocks[0][:, cols]

    ext = load(slice(total - LANES, total))

    def picks(expert, count):
        mask = jnp.broadcast_to(scale_of(ext, expert, experts) > 0, (rows, LANES)).astype(jnp.bfloat16)
        upto = (iota((rows, rows), 0) <= iota((rows, rows), 1)).astype(jnp.bfloat16)
        place = contract(mask, upto, 0, 0)[:count]
        named = contract(mask, eye(rows), 0, 0)[:count]
        slot = iota((count, rows), 0).astype(jnp.float32)
        return ((named > 0.5) & (place - 1.0 == slot)).astype(jnp.float32)

    own = picks(idx[1], own_rows) if mode == "both" else eye(rows).astype(jnp.float32)
    pick = jnp.concatenate([own, picks(idx[2], cross_rows)], 0).astype(jnp.bfloat16)
    pick_out[...] = pick
    step = total // 3
    for n in range(0, total, step):
        got = dot32(pick, load(slice(n, n + step)))
        own_out[:, n : n + step] = got[:own_rows].astype(jnp.bfloat16)
        cross_out[:, n : n + step] = got[own_rows:].astype(jnp.bfloat16)


def expert_kernel(experts, idx, own, cross, ga, gb, ua, ub, da, db, own_out, cross_out, hidden):
    own_rows, total = own.shape
    width = total - LANES
    core, expert = idx[0], idx[1]
    half = ga.shape[0]
    x = jnp.concatenate([own[:, :width], cross[:, :width]], 0)
    ext = jnp.concatenate([own[:, width:], cross[:, width:]], 0)
    lane = iota((8, LANES), 1)
    mine = ((lane % experts == expert) & (lane < 3 * experts)).astype(jnp.bfloat16)
    scale = contract(mine, ext, 1, 1)[:1]
    for place, g, u in ((core, ga, ua), (1 - core, gb, ub)):
        gate = contract(g[...], x, 1, 1)
        upval = contract(u[...], x, 1, 1)
        made = gate / (1.0 + jnp.exp(-gate)) * upval * scale
        hidden[place] = made.T.astype(jnp.bfloat16)
    step = 512
    cols = da.shape[1]
    for n in range(0, 2 * cols, step):
        d, m = (da, n) if n < cols else (db, n - cols)
        made = dot32(hidden[0], d[:half, m : m + step]) + dot32(hidden[1], d[half:, m : m + step])
        own_out[:, n : n + step] = made[:own_rows].astype(jnp.bfloat16)
        cross_out[:, n : n + step] = made[own_rows:].astype(jnp.bfloat16)


def combine_kernel(first, idx, pick, own, cross, *refs):
    *more, out = refs
    width = own.shape[1]
    rows = slice(first, first + out.shape[0])
    step = 1024
    for n in range(0, width, step):
        cols = slice(n, n + step)
        got = contract(pick[...], jnp.concatenate([own[:, cols], cross[:, cols]], 0), 0, 0)[rows]
        for ref in more:
            got += ref[:, cols].astype(jnp.float32)
        out[:, cols] = got.astype(jnp.bfloat16)


def finish_kernel(half, idx, order, pick, own, cross, *refs):
    *more, out, held, sems = refs
    width = own.shape[1]
    step = 1024
    copies = []
    for i, n in enumerate(range(0, width, step)):
        cols = slice(n, n + step)
        got = contract(pick[...], jnp.concatenate([own[:, cols], cross[:, cols]], 0), 0, 0)
        sums = [sum(r[:, cols].astype(jnp.float32) for r in part) for part in (more[:half], more[half:])]
        got = (got + jnp.concatenate(sums, 0)).astype(jnp.bfloat16)
        held[i] = contract(order[...], got, 0, 0).astype(jnp.bfloat16)
        to = pl.ds(pl.multiple_of((idx[4] + n) % width, step), step)
        copies.append(pltpu.make_async_copy(held.at[i], out.at[:, to], sems.at[i]))
        copies[-1].start()
    for c in copies:
        c.wait()


def fence_kernel(idx):
    pass


def run_copies(sems, pairs):
    copies = [pltpu.make_async_copy(s, d, sems.at[i]) for i, (s, d) in enumerate(pairs)]
    for c in copies:
        c.start()
    for c in copies:
        c.wait()


def copy_kernel(idx, source, to, sem):
    copy = pltpu.make_async_copy(source, to, sem)
    copy.start()
    copy.wait()


def fetch_kernel(idx, *refs):
    count = len(refs) // 2
    run_copies(refs[-1], zip(refs[:count], refs[count:-1]))


def call(name, kernel, outs, idx, token, args, passes=(), scratch=(), cost=1, left=(), away=False):
    vmem, anywhere = pl.BlockSpec(memory_space=pltpu.VMEM), pl.BlockSpec(memory_space=pl.ANY)
    through = [token, *passes]
    first = 1 + len(args) + len(left)

    def body(*refs):
        ins, rest = refs[:first], refs[first + len(through) :]
        kernel(*ins, *rest[: len(outs)], *rest[len(outs) + len(through) :])

    got = pl.pallas_call(
        body,
        out_shape=[*outs, *(jax.ShapeDtypeStruct(x.shape, x.dtype) for x in through)],
        in_specs=[pl.BlockSpec(memory_space=pltpu.SMEM)]
        + [vmem] * len(args)
        + [anywhere] * len(left)
        + [anywhere] * len(through),
        out_specs=[anywhere if away else vmem] * len(outs) + [anywhere] * len(through),
        input_output_aliases={first + i: len(outs) + i for i in range(len(through))},
        scratch_shapes=list(scratch),
        name=name,
        compiler_params=pltpu.CompilerParams(vmem_limit_bytes=LIMIT),
        cost_estimate=pl.CostEstimate(flops=1, bytes_accessed=cost, transcendentals=0),
    )(idx, *args, *left, *through)
    return got[: len(outs)], got[len(outs)], got[len(outs) + 1 :]


ORDER = [
    ["prep", "EA", "MB", "EB"],
    ["V"],
    ["P0"],
    ["f", "NA", "Y0", "OB", "wd", "+wu"],
    ["W"],
    ["f", "MA"],
    ["P1", "Y1", "QA"],
    ["P2B", "Y2B", "NB"],
    ["F0", "OA", "+OB"],
    ["P3A", "Y3A", "+Y1"],
    ["F2B", "QB", "R2B"],
    ["f", "+Y3A"],
    ["P2A", "+Y2B"],
    ["f", "Y2A"],
    ["F3A"],
    ["C2B", "I2B"],
    ["P3B"],
    ["f", "Y3B", "+Y2A"],
    ["F1", "R3A"],
    ["F3B"],
    ["D2B", "R3B"],
    ["C3A", "I3A", "S2B"],
    ["F2A"],
    ["C3B", "I3B", "R2A", "+R3A"],
    ["D3A", "S3A"],
    ["C2A", "R1", "I2A", "+S2B"],
    ["D3B", "S3B", "+R2A"],
    ["D1A", "S1A", "R0"],
    ["D2A", "+R1", "S2A"],
    ["D1B", "S1B"],
    ["fin"],
]


def lined(tokens, routes, route_weights, gate_weight, up_weight, down_weight):
    tok_rows, top_count = routes.shape
    width = tokens.shape[1]
    devices = lax.axis_size("expert")
    experts = devices // 2
    capacity = tok_rows * top_count // experts
    half = gate_weight.shape[1]
    index = lax.axis_index("expert")
    core, side, line = index % 2, index // 2 % 2, index // 4
    inner = ((line == 1) | (line == 2)).astype(jnp.int32)
    idx = jnp.stack(
        [core, 2 * line + side, 2 * line + 1 - side, inner, core * down_weight.shape[1], 1 - side]
    ).astype(jnp.int32)
    rows = tok_rows // 2
    total = width + LANES
    bf16 = jnp.bfloat16

    def in_hbm(x):
        return pltpu.with_memory_space_constraint(x, pltpu.HBM)

    def like(*shape):
        return jax.ShapeDtypeStruct(shape, bf16)

    gate, up = gate_weight.T, up_weight.T

    val = {}
    for name, w in (("wg", gate), ("wu", up)):
        with jax.named_scope("move_" + name):
            val[name] = swapped(w, "expert", 0)
    steps = {name for name, *_ in ORDER}
    slots = {name[1:] for name in steps if name[0] == "P"}

    def kernel_of(name):
        kind, q = name[:-1], name[-1]
        if name == "prep":
            return (
                functools.partial(prepare_kernel, experts),
                [like(rows, total), like(rows, total), like(tok_rows, tok_rows)],
                [in_hbm(routes.T), in_hbm(route_weights.T)],
                [pltpu.VMEM(tokens.shape, bf16), pltpu.SemaphoreType.DMA],
            )
        if name[0] == "P":
            slot = name[1:]
            if slot in ("0", "1"):
                blocks, mode = [["payA", "payB"], ["EA", "EB"]][int(slot)], "both"
                own, cross, size = capacity, capacity, tok_rows
            else:
                blocks = {"1": ["E" + q], "2": ["M" + q, "O" + q], "3": ["N" + q, "Q" + q]}[slot[0]]
                mode = "one" if len(blocks) == 1 else "either"
                own, cross, size = rows, CROSS_ROWS, rows
            return (
                functools.partial(pick_kernel, experts, mode),
                [like(own, total), like(cross, total), like(own + cross, size)],
                [val[b] for b in blocks],
                [],
            )
        if name[0] == "F":
            own, cross = val["own" + name[1:]], val["Y" + name[1:]]
            weights = [gate, val["vg"], up, val["vu"], down_weight, val["vd"]]
            weights = [pltpu.with_memory_space_constraint(w, pltpu.VMEM) for w in weights]
            args = [own, cross, *weights]
            return (
                functools.partial(expert_kernel, experts),
                [like(own.shape[0], width), like(cross.shape[0], width)],
                args,
                [pltpu.VMEM((2, own.shape[0] + cross.shape[0], half), bf16)],
            )
        if name == "V":
            return copy_kernel, [like(*down_weight.shape)], [], [pltpu.SemaphoreType.DMA]
        if name == "W":
            outs = [pltpu.VMEM(w.shape, bf16) for w in (gate, up, down_weight)]
            return fetch_kernel, outs, [], [pltpu.SemaphoreType.DMA((3,))]
        if name == "fin":
            made = [val["order"], val["pick0"], val["made0"], val["R0"]]
            made += [val[s + q] for q in "AB" for s in ("S1", "S2", "X3") if s + q in val]
            counts = [sum(s + q in val for s in ("S1", "S2", "X3")) for q in "AB"]
            parts = width // 1024
            scratch = [pltpu.VMEM((parts, tok_rows, 1024), bf16), pltpu.SemaphoreType.DMA((parts,))]
            return functools.partial(finish_kernel, counts[0]), [like(tok_rows, width)], made, scratch
        slot = name[1:] if name[1:] in slots else name[1]
        made = [val[s + slot] for s in ("pick", "made", "R")]
        made += [val[x] for x in {"D2": ["I2" + q], "D3": ["I3" + q], "D1": ["S3" + q]}.get(kind, [])]
        first = rows if slot == name[1] and q == "B" else 0
        return functools.partial(combine_kernel, first), [like(rows, width)], made, []

    def keep(name, got):
        slot = name[1:]
        if name == "prep":
            val["payA"], val["payB"], val["order"] = got
        elif name[0] == "P":
            val["own" + slot], val["cross" + slot], val["pick" + slot] = got
        elif name == "V":
            val["down"] = got[0]
        elif name == "W":
            val["vg"], val["vu"], val["vd"] = got
        elif name[0] == "F":
            val["made" + slot], val["back" + slot] = got
        else:
            val[name] = got[0]

    def move_of(name):
        kind, slot, q = name[0], name[1:], name[-1]
        if name == "wd":
            return "down", lambda x: swapped(x, "expert", 0)
        if kind == "Y":
            return "cross" + slot, lambda x: swapped(x, "expert", 1)
        if kind == "R":
            return "back" + slot, lambda x: swapped(x, "expert", 1)
        source, pairs = {
            "E": ("pay" + q, OUTER),
            "M": ("pay" + q, MIDDLE),
            "O": ("M" + q, OUT),
            "N": ("E" + q, MIDDLE),
            "Q": ("N" + q, OUT),
            "I2": ("C2" + q, IN),
            "S2": ("D2" + q, MIDDLE),
            "X3": ("C3" + q, ENDS),
            "I3": ("C3" + q, IN),
            "S3": (("D3" if "D3" + q in steps else "C3") + q, MIDDLE),
            "S1": ("D1" + q, OUTER),
        }[name[:-1]]
        return source, lambda x: along_line(x, pairs)

    token = jnp.zeros((8, LANES), jnp.float32)
    for name, *moves in ORDER:
        done = [m[1:] for m in moves if m[0] == "+"]
        moves = [m for m in moves if m[0] != "+"]
        sources = {m: move_of(m)[0] for m in moves}
        passed = sorted({s for s in [*sources.values(), *done] if s in val})
        if name == "f":
            _, token, through = call("fence", fence_kernel, [], idx, token, [], passes=[val[s] for s in passed])
        else:
            kernel, outs, args, scratch = kernel_of(name)
            cost = sum(x.size * x.dtype.itemsize for x in [*args, *outs]) if name[0] == "F" else 1
            through = [val[s] for s in passed]
            left = {"prep": [in_hbm(tokens)], "V": [in_hbm(down_weight)]}.get(name, [])
            if name == "W":
                left = [val["wg"], val["wu"], val["wd"]]
            got, token, through = call(name, kernel, outs, idx, token, args, through, scratch, cost, left, name in ("V", "fin"))
            keep(name, got)
        val.update(zip(passed, through))
        for m in moves:
            with jax.named_scope("move_" + m):
                val[m] = move_of(m)[1](val[sources[m]])
    return val["fin"]


def solution(mesh):
    body = lined if mesh.shape["expert"] == 16 else dispatched
    return jax.shard_map(
        body,
        mesh=mesh,
        in_specs=(
            P(("groups", "expert"), None),
            P(("groups", "expert"), None),
            P(("groups", "expert"), None),
            P(None, "expert"),
            P(None, "expert"),
            P(None, "expert"),
        ),
        out_specs=P(("groups", "expert"), None),
        check_vma=False,
    )
```

```python
import functools

import jax
import jax.experimental.pallas as pl
import jax.experimental.pallas.tpu as pltpu
import jax.numpy as jnp
from jax import lax
from jax.sharding import PartitionSpec as P

CROSS_ROWS = 40
LANES = 128
LIMIT = 12 << 20


def swapped(x, axis, apart):
    return lax.ppermute(x, axis, [(i, i ^ 1 << apart) for i in range(lax.axis_size(axis))])


def dot32(a, b):
    return jnp.dot(a, b, preferred_element_type=jnp.float32)


def expert_hidden(rows, gate_part, up_part, parity):
    gate = dot32(rows, gate_part)
    upval = dot32(rows, up_part)
    hidden = (jax.nn.silu(gate) * upval).astype(jnp.bfloat16)
    partner = swapped(hidden, "expert", 0)
    return jnp.where(
        parity == 0, jnp.concatenate([hidden, partner], 1), jnp.concatenate([partner, hidden], 1)
    )


def dispatched(tokens, routes, route_weights, gate_weight, up_weight, down_weight):
    tok_rows, top_count = routes.shape
    width = tokens.shape[1]
    half_width = down_weight.shape[1]
    devices = lax.axis_size("expert")
    experts = devices // 2
    capacity = tok_rows * top_count // experts
    parity = lax.axis_index("expert") % 2
    flat = routes.reshape(-1)
    onehot = (flat[:, None] == jnp.arange(experts, dtype=jnp.int32)[None, :]).astype(jnp.int32)
    before = jnp.cumsum(onehot, axis=0) - onehot
    slot_of = jnp.sum(before * onehot, axis=1)
    position = flat * capacity + slot_of
    assign_ids = jnp.arange(flat.shape[0], dtype=jnp.int32) // top_count
    owner = jnp.zeros((experts * capacity,), jnp.int32).at[position].set(assign_ids)
    gathered = tokens[owner]
    outgoing = jnp.broadcast_to(
        gathered.reshape(experts, 1, capacity, width), (experts, 2, capacity, width)
    )
    outgoing = outgoing.reshape(devices, capacity, width)
    received = lax.all_to_all(outgoing, "expert", split_axis=0, concat_axis=0, tiled=True)
    count, items, _ = received.shape
    hidden = expert_hidden(received.reshape(count * items, width), gate_weight, up_weight, parity)
    produced = dot32(hidden, down_weight).astype(jnp.bfloat16)
    returned = lax.all_to_all(
        produced.reshape(count, items, half_width),
        "expert",
        split_axis=0,
        concat_axis=0,
        tiled=True,
    )
    returned = returned.reshape(experts, 2, capacity, half_width).transpose(0, 2, 1, 3)
    expert_rows = returned.reshape(experts * capacity, width)
    picked = expert_rows[position].reshape(tok_rows, top_count, width)
    mixed = jnp.einsum("tk,tkd->td", route_weights, picked.astype(jnp.float32))
    return mixed.astype(jnp.bfloat16)


def along_line(x, pairs):
    moves = [((a * 2 + s) * 2 + c, (b * 2 + s) * 2 + c) for a, b in pairs for s in (0, 1) for c in (0, 1)]
    return lax.ppermute(x, "expert", moves)


OUTER = [(0, 1), (1, 0), (2, 3), (3, 2)]
MIDDLE = [(1, 2), (2, 1)]
OUT = [(1, 0), (2, 3)]
IN = [(0, 1), (3, 2)]
ENDS = [(0, 3), (3, 0)]


def contract(a, b, da, db):
    return lax.dot_general(a, b, (((da,), (db,)), ((), ())), preferred_element_type=jnp.float32)


def iota(shape, dim):
    return lax.broadcasted_iota(jnp.int32, shape, dim)


def eye(n):
    return (iota((n, n), 0) == iota((n, n), 1)).astype(jnp.bfloat16)


def scale_of(ext, expert, experts):
    lane = iota(ext.shape, 1)
    mine = (lane % experts == expert) & (lane < 3 * experts)
    return jnp.sum(jnp.where(mine, ext.astype(jnp.float32), 0.0), axis=1, keepdims=True)


def prepare_kernel(experts, idx, routes, weights, tokens, *refs):
    *chunks, order_out, held, sem = refs
    fetch = pltpu.make_async_copy(tokens, held, sem)
    fetch.start()
    rows, width = tokens.shape
    size = rows // len(chunks)
    f32, bf16 = jnp.float32, jnp.bfloat16
    full = jnp.zeros((experts, rows), f32)
    for k in range(routes.shape[0]):
        full += jnp.where(iota((experts, rows), 0) == routes[k : k + 1], weights[k : k + 1], 0.0)
    high = full.astype(bf16).astype(f32)
    mid = (full - high).astype(bf16).astype(f32)
    parts = jnp.concatenate([high, mid, full - high - mid], 0).astype(bf16)
    spread = (iota((3 * experts, LANES), 0) == iota((3 * experts, LANES), 1)).astype(bf16)
    ext = contract(parts, spread, 0, 0).astype(bf16)
    gray = jnp.zeros((1, rows), jnp.int32)
    bit = jnp.zeros((1, rows), jnp.int32)
    for z in range(experts // 2):
        named = jnp.zeros((1, rows), jnp.int32)
        for k in range(routes.shape[0]):
            named += (routes[k : k + 1] == idx[5] + 2 * z).astype(jnp.int32)
        bit = bit ^ named
        gray = gray * 2 + bit
    across = jnp.broadcast_to(gray.astype(f32), (rows, rows))
    first, second = iota((rows, rows), 0), iota((rows, rows), 1)
    top = jnp.where(first[:8] == 0, across[:8], 0.0).astype(bf16)
    down = contract(top, jnp.ones((8, rows), bf16), 0, 0)
    ahead = (down < across) | ((down == across) & (first < second))
    rank = jnp.sum(ahead.astype(f32), axis=0, keepdims=True).astype(jnp.int32)
    target = rank % len(chunks) * size + rank // len(chunks)
    order = (first == target).astype(bf16)
    order_out[...] = order
    ext = dot32(order, ext).astype(bf16)
    for q, chunk in enumerate(chunks):
        chunk[:, width:] = ext[q * size : (q + 1) * size]
    fetch.wait()
    step = 1024
    for n in range(0, width, step):
        moved = dot32(order, held[:, n : n + step]).astype(bf16)
        for q, chunk in enumerate(chunks):
            chunk[:, n : n + step] = moved[q * size : (q + 1) * size]


def pick_kernel(experts, mode, idx, *refs):
    *blocks, own_out, cross_out, pick_out = refs
    total = blocks[0].shape[1]
    rows = blocks[0].shape[0] * (len(blocks) if mode == "both" else 1)
    own_rows, cross_rows = own_out.shape[0], cross_out.shape[0]
    inner = idx[3] == 1

    def load(cols):
        if mode == "both":
            return jnp.concatenate([b[:, cols] for b in blocks], 0)
        if mode == "either":
            return jnp.where(inner, blocks[0][:, cols], blocks[1][:, cols])
        return blocks[0][:, cols]

    ext = load(slice(total - LANES, total))

    def picks(expert, count):
        mask = jnp.broadcast_to(scale_of(ext, expert, experts) > 0, (rows, LANES)).astype(jnp.bfloat16)
        upto = (iota((rows, rows), 0) <= iota((rows, rows), 1)).astype(jnp.bfloat16)
        place = contract(mask, upto, 0, 0)[:count]
        named = contract(mask, eye(rows), 0, 0)[:count]
        slot = iota((count, rows), 0).astype(jnp.float32)
        return ((named > 0.5) & (place - 1.0 == slot)).astype(jnp.float32)

    own = picks(idx[1], own_rows) if mode == "both" else eye(rows).astype(jnp.float32)
    pick = jnp.concatenate([own, picks(idx[2], cross_rows)], 0).astype(jnp.bfloat16)
    pick_out[...] = pick
    step = total // 3
    for n in range(0, total, step):
        got = dot32(pick, load(slice(n, n + step)))
        own_out[:, n : n + step] = got[:own_rows].astype(jnp.bfloat16)
        cross_out[:, n : n + step] = got[own_rows:].astype(jnp.bfloat16)


def expert_kernel(experts, idx, own, cross, ga, gb, ua, ub, da, db, own_out, cross_out, hidden):
    own_rows, total = own.shape
    width = total - LANES
    core, expert = idx[0], idx[1]
    half = ga.shape[0]
    x = jnp.concatenate([own[:, :width], cross[:, :width]], 0)
    ext = jnp.concatenate([own[:, width:], cross[:, width:]], 0)
    lane = iota((8, LANES), 1)
    mine = ((lane % experts == expert) & (lane < 3 * experts)).astype(jnp.bfloat16)
    scale = contract(mine, ext, 1, 1)[:1]
    for place, g, u in ((core, ga, ua), (1 - core, gb, ub)):
        gate = contract(g[...], x, 1, 1)
        upval = contract(u[...], x, 1, 1)
        made = gate / (1.0 + jnp.exp(-gate)) * upval * scale
        hidden[place] = made.T.astype(jnp.bfloat16)
    step = 512
    cols = da.shape[1]
    for n in range(0, 2 * cols, step):
        d, m = (da, n) if n < cols else (db, n - cols)
        made = dot32(hidden[0], d[:half, m : m + step]) + dot32(hidden[1], d[half:, m : m + step])
        own_out[:, n : n + step] = made[:own_rows].astype(jnp.bfloat16)
        cross_out[:, n : n + step] = made[own_rows:].astype(jnp.bfloat16)


def combine_kernel(first, idx, pick, own, cross, *refs):
    *more, out = refs
    width = own.shape[1]
    rows = slice(first, first + out.shape[0])
    step = 1024
    for n in range(0, width, step):
        cols = slice(n, n + step)
        got = contract(pick[...], jnp.concatenate([own[:, cols], cross[:, cols]], 0), 0, 0)[rows]
        for ref in more:
            got += ref[:, cols].astype(jnp.float32)
        out[:, cols] = got.astype(jnp.bfloat16)


def finish_kernel(half, idx, order, pick, own, cross, *refs):
    *more, out, held, sems = refs
    width = own.shape[1]
    step = 1024
    copies = []
    for i, n in enumerate(range(0, width, step)):
        cols = slice(n, n + step)
        got = contract(pick[...], jnp.concatenate([own[:, cols], cross[:, cols]], 0), 0, 0)
        sums = [sum(r[:, cols].astype(jnp.float32) for r in part) for part in (more[:half], more[half:])]
        got = (got + jnp.concatenate(sums, 0)).astype(jnp.bfloat16)
        held[i] = contract(order[...], got, 0, 0).astype(jnp.bfloat16)
        to = pl.ds(pl.multiple_of((idx[4] + n) % width, step), step)
        copies.append(pltpu.make_async_copy(held.at[i], out.at[:, to], sems.at[i]))
        copies[-1].start()
    for c in copies:
        c.wait()


def fence_kernel(idx):
    pass


def run_copies(sems, pairs):
    copies = [pltpu.make_async_copy(s, d, sems.at[i]) for i, (s, d) in enumerate(pairs)]
    for c in copies:
        c.start()
    for c in copies:
        c.wait()


def fetch_kernel(idx, *refs):
    count = len(refs) // 2
    run_copies(refs[-1], zip(refs[:count], refs[count:-1]))


def call(name, kernel, outs, idx, token, args, passes=(), scratch=(), cost=1, left=(), away=False):
    vmem, anywhere = pl.BlockSpec(memory_space=pltpu.VMEM), pl.BlockSpec(memory_space=pl.ANY)
    through = [token, *passes]
    first = 1 + len(args) + len(left)

    def body(*refs):
        ins, rest = refs[:first], refs[first + len(through) :]
        kernel(*ins, *rest[: len(outs)], *rest[len(outs) + len(through) :])

    got = pl.pallas_call(
        body,
        out_shape=[*outs, *(jax.ShapeDtypeStruct(x.shape, x.dtype) for x in through)],
        in_specs=[pl.BlockSpec(memory_space=pltpu.SMEM)]
        + [vmem] * len(args)
        + [anywhere] * len(left)
        + [anywhere] * len(through),
        out_specs=[anywhere if away else vmem] * len(outs) + [anywhere] * len(through),
        input_output_aliases={first + i: len(outs) + i for i in range(len(through))},
        scratch_shapes=list(scratch),
        name=name,
        compiler_params=pltpu.CompilerParams(vmem_limit_bytes=LIMIT),
        cost_estimate=pl.CostEstimate(flops=1, bytes_accessed=cost, transcendentals=0),
    )(idx, *args, *left, *through)
    return got[: len(outs)], got[len(outs)], got[len(outs) + 1 :]


ORDER = [
    ["prep", "EA", "MB", "EB"],
    ["P0", "NA", "Y0"],
    ["f", "OB", "+wg", "+wu"],
    ["W"],
    ["f", "MA"],
    ["P1", "Y1", "QA"],
    ["P2B", "Y2B", "NB"],
    ["F0", "OA"],
    ["P3A", "Y3A", "+Y1"],
    ["F2B", "R2B"],
    ["f", "QB", "+Y3A"],
    ["P2A"],
    ["f", "Y2A"],
    ["F3A"],
    ["C2B", "I2B"],
    ["P3B", "Y3B", "+Y2A"],
    ["F1", "R3A"],
    ["F3B", "+I2B"],
    ["D2B", "R3B"],
    ["C3A", "I3A", "S2B", "R1"],
    ["F2A"],
    ["C3B", "I3B", "R2A", "+R3A"],
    ["D3A", "S3A"],
    ["C2A", "I2A", "+S2B", "+R1"],
    ["D3B", "S3B", "+R2A"],
    ["D1A", "S1A", "R0"],
    ["D2A"],
    ["D1B", "S2A", "S1B", "+I2A"],
    ["fin"],
]


def lined(tokens, routes, route_weights, gate_weight, up_weight, down_weight):
    tok_rows, top_count = routes.shape
    width = tokens.shape[1]
    devices = lax.axis_size("expert")
    experts = devices // 2
    capacity = tok_rows * top_count // experts
    half = gate_weight.shape[1]
    index = lax.axis_index("expert")
    core, side, line = index % 2, index // 2 % 2, index // 4
    inner = ((line == 1) | (line == 2)).astype(jnp.int32)
    idx = jnp.stack(
        [core, 2 * line + side, 2 * line + 1 - side, inner, core * down_weight.shape[1], 1 - side]
    ).astype(jnp.int32)
    rows = tok_rows // 2
    total = width + LANES
    bf16 = jnp.bfloat16

    def in_hbm(x):
        return pltpu.with_memory_space_constraint(x, pltpu.HBM)

    def like(*shape):
        return jax.ShapeDtypeStruct(shape, bf16)

    gate, up = gate_weight.T, up_weight.T

    val = {}
    for name, w in (("wg", gate), ("wu", up), ("wd", down_weight)):
        with jax.named_scope("move_" + name):
            val[name] = swapped(w, "expert", 0)
    steps = {name for name, *_ in ORDER}
    slots = {name[1:] for name in steps if name[0] == "P"}

    def kernel_of(name):
        kind, q = name[:-1], name[-1]
        if name == "prep":
            return (
                functools.partial(prepare_kernel, experts),
                [like(rows, total), like(rows, total), like(tok_rows, tok_rows)],
                [in_hbm(routes.T), in_hbm(route_weights.T)],
                [pltpu.VMEM(tokens.shape, bf16), pltpu.SemaphoreType.DMA],
            )
        if name[0] == "P":
            slot = name[1:]
            if slot in ("0", "1"):
                blocks, mode = [["payA", "payB"], ["EA", "EB"]][int(slot)], "both"
                own, cross, size = capacity, capacity, tok_rows
            else:
                blocks = {"1": ["E" + q], "2": ["M" + q, "O" + q], "3": ["N" + q, "Q" + q]}[slot[0]]
                mode = "one" if len(blocks) == 1 else "either"
                own, cross, size = rows, CROSS_ROWS, rows
            return (
                functools.partial(pick_kernel, experts, mode),
                [like(own, total), like(cross, total), like(own + cross, size)],
                [val[b] for b in blocks],
                [],
            )
        if name[0] == "F":
            own, cross = val["own" + name[1:]], val["Y" + name[1:]]
            weights = [gate, val["vg"], up, val["vu"], down_weight, val["vd"]]
            weights = [pltpu.with_memory_space_constraint(w, pltpu.VMEM) for w in weights]
            args = [own, cross, *weights]
            return (
                functools.partial(expert_kernel, experts),
                [like(own.shape[0], width), like(cross.shape[0], width)],
                args,
                [pltpu.VMEM((2, own.shape[0] + cross.shape[0], half), bf16)],
            )
        if name == "W":
            outs = [pltpu.VMEM(w.shape, bf16) for w in (gate, up, down_weight)]
            return fetch_kernel, outs, [], [pltpu.SemaphoreType.DMA((3,))]
        if name == "fin":
            made = [val["order"], val["pick0"], val["made0"], val["R0"]]
            made += [val[s + q] for q in "AB" for s in ("S1", "S2", "X3") if s + q in val]
            counts = [sum(s + q in val for s in ("S1", "S2", "X3")) for q in "AB"]
            parts = width // 1024
            scratch = [pltpu.VMEM((parts, tok_rows, 1024), bf16), pltpu.SemaphoreType.DMA((parts,))]
            return functools.partial(finish_kernel, counts[0]), [like(tok_rows, width)], made, scratch
        slot = name[1:] if name[1:] in slots else name[1]
        made = [val[s + slot] for s in ("pick", "made", "R")]
        made += [val[x] for x in {"D2": ["I2" + q], "D3": ["I3" + q], "D1": ["S3" + q]}.get(kind, [])]
        first = rows if slot == name[1] and q == "B" else 0
        return functools.partial(combine_kernel, first), [like(rows, width)], made, []

    def keep(name, got):
        slot = name[1:]
        if name == "prep":
            val["payA"], val["payB"], val["order"] = got
        elif name[0] == "P":
            val["own" + slot], val["cross" + slot], val["pick" + slot] = got
        elif name == "W":
            val["vg"], val["vu"], val["vd"] = got
        elif name[0] == "F":
            val["made" + slot], val["back" + slot] = got
        else:
            val[name] = got[0]

    def move_of(name):
        kind, slot, q = name[0], name[1:], name[-1]
        if kind == "Y":
            return "cross" + slot, lambda x: swapped(x, "expert", 1)
        if kind == "R":
            return "back" + slot, lambda x: swapped(x, "expert", 1)
        source, pairs = {
            "E": ("pay" + q, OUTER),
            "M": ("pay" + q, MIDDLE),
            "O": ("M" + q, OUT),
            "N": ("E" + q, MIDDLE),
            "Q": ("N" + q, OUT),
            "I2": ("C2" + q, IN),
            "S2": ("D2" + q, MIDDLE),
            "X3": ("C3" + q, ENDS),
            "I3": ("C3" + q, IN),
            "S3": (("D3" if "D3" + q in steps else "C3") + q, MIDDLE),
            "S1": ("D1" + q, OUTER),
        }[name[:-1]]
        return source, lambda x: along_line(x, pairs)

    token = jnp.zeros((8, LANES), jnp.float32)
    for name, *moves in ORDER:
        done = [m[1:] for m in moves if m[0] == "+"]
        moves = [m for m in moves if m[0] != "+"]
        sources = {m: move_of(m)[0] for m in moves}
        passed = sorted({s for s in [*sources.values(), *done] if s in val})
        if name == "f":
            _, token, through = call("fence", fence_kernel, [], idx, token, [], passes=[val[s] for s in passed])
        else:
            kernel, outs, args, scratch = kernel_of(name)
            cost = sum(x.size * x.dtype.itemsize for x in [*args, *outs]) if name[0] == "F" else 1
            through = [val[s] for s in passed]
            left = {"prep": [in_hbm(tokens)], "W": [val["wg"], val["wu"], val["wd"]]}.get(name, [])
            got, token, through = call(name, kernel, outs, idx, token, args, through, scratch, cost, left, name == "fin")
            keep(name, got)
        val.update(zip(passed, through))
        for m in moves:
            with jax.named_scope("move_" + m):
                val[m] = move_of(m)[1](val[sources[m]])
    return val["fin"]


def solution(mesh):
    body = lined if mesh.shape["expert"] == 16 else dispatched
    return jax.shard_map(
        body,
        mesh=mesh,
        in_specs=(
            P(("groups", "expert"), None),
            P(("groups", "expert"), None),
            P(("groups", "expert"), None),
            P(None, "expert"),
            P(None, "expert"),
            P(None, "expert"),
        ),
        out_specs=P(("groups", "expert"), None),
        check_vma=False,
    )
```

```python
import functools

import jax
import jax.experimental.pallas as pl
import jax.experimental.pallas.tpu as pltpu
import jax.numpy as jnp
from jax import lax
from jax.sharding import PartitionSpec as P

CROSS_ROWS = 40
LANES = 128
LIMIT = 12 << 20


def swapped(x, axis, apart):
    return lax.ppermute(x, axis, [(i, i ^ 1 << apart) for i in range(lax.axis_size(axis))])


def dot32(a, b):
    return jnp.dot(a, b, preferred_element_type=jnp.float32)


def expert_hidden(rows, gate_part, up_part, parity):
    gate = dot32(rows, gate_part)
    upval = dot32(rows, up_part)
    hidden = (jax.nn.silu(gate) * upval).astype(jnp.bfloat16)
    partner = swapped(hidden, "expert", 0)
    return jnp.where(
        parity == 0, jnp.concatenate([hidden, partner], 1), jnp.concatenate([partner, hidden], 1)
    )


def dispatched(tokens, routes, route_weights, gate_weight, up_weight, down_weight):
    tok_rows, top_count = routes.shape
    width = tokens.shape[1]
    half_width = down_weight.shape[1]
    devices = lax.axis_size("expert")
    experts = devices // 2
    capacity = tok_rows * top_count // experts
    parity = lax.axis_index("expert") % 2
    flat = routes.reshape(-1)
    onehot = (flat[:, None] == jnp.arange(experts, dtype=jnp.int32)[None, :]).astype(jnp.int32)
    before = jnp.cumsum(onehot, axis=0) - onehot
    slot_of = jnp.sum(before * onehot, axis=1)
    position = flat * capacity + slot_of
    assign_ids = jnp.arange(flat.shape[0], dtype=jnp.int32) // top_count
    owner = jnp.zeros((experts * capacity,), jnp.int32).at[position].set(assign_ids)
    gathered = tokens[owner]
    outgoing = jnp.broadcast_to(
        gathered.reshape(experts, 1, capacity, width), (experts, 2, capacity, width)
    )
    outgoing = outgoing.reshape(devices, capacity, width)
    received = lax.all_to_all(outgoing, "expert", split_axis=0, concat_axis=0, tiled=True)
    count, items, _ = received.shape
    hidden = expert_hidden(received.reshape(count * items, width), gate_weight, up_weight, parity)
    produced = dot32(hidden, down_weight).astype(jnp.bfloat16)
    returned = lax.all_to_all(
        produced.reshape(count, items, half_width),
        "expert",
        split_axis=0,
        concat_axis=0,
        tiled=True,
    )
    returned = returned.reshape(experts, 2, capacity, half_width).transpose(0, 2, 1, 3)
    expert_rows = returned.reshape(experts * capacity, width)
    picked = expert_rows[position].reshape(tok_rows, top_count, width)
    mixed = jnp.einsum("tk,tkd->td", route_weights, picked.astype(jnp.float32))
    return mixed.astype(jnp.bfloat16)


def along_line(x, pairs):
    moves = [((a * 2 + s) * 2 + c, (b * 2 + s) * 2 + c) for a, b in pairs for s in (0, 1) for c in (0, 1)]
    return lax.ppermute(x, "expert", moves)


OUTER = [(0, 1), (1, 0), (2, 3), (3, 2)]
MIDDLE = [(1, 2), (2, 1)]
OUT = [(1, 0), (2, 3)]
IN = [(0, 1), (3, 2)]
ENDS = [(0, 3), (3, 0)]


def contract(a, b, da, db):
    return lax.dot_general(a, b, (((da,), (db,)), ((), ())), preferred_element_type=jnp.float32)


def iota(shape, dim):
    return lax.broadcasted_iota(jnp.int32, shape, dim)


def eye(n):
    return (iota((n, n), 0) == iota((n, n), 1)).astype(jnp.bfloat16)


def scale_of(ext, expert, experts):
    lane = iota(ext.shape, 1)
    mine = (lane % experts == expert) & (lane < 3 * experts)
    return jnp.sum(jnp.where(mine, ext.astype(jnp.float32), 0.0), axis=1, keepdims=True)


def prepare_kernel(experts, idx, routes, weights, tokens, *refs):
    *chunks, order_out, held, sem = refs
    fetch = pltpu.make_async_copy(tokens, held, sem)
    fetch.start()
    rows, width = tokens.shape
    size = rows // len(chunks)
    f32, bf16 = jnp.float32, jnp.bfloat16
    full = jnp.zeros((experts, rows), f32)
    for k in range(routes.shape[0]):
        full += jnp.where(iota((experts, rows), 0) == routes[k : k + 1], weights[k : k + 1], 0.0)
    high = full.astype(bf16).astype(f32)
    mid = (full - high).astype(bf16).astype(f32)
    parts = jnp.concatenate([high, mid, full - high - mid], 0).astype(bf16)
    spread = (iota((3 * experts, LANES), 0) == iota((3 * experts, LANES), 1)).astype(bf16)
    ext = contract(parts, spread, 0, 0).astype(bf16)
    gray = jnp.zeros((1, rows), jnp.int32)
    bit = jnp.zeros((1, rows), jnp.int32)
    for z in range(experts // 2):
        named = jnp.zeros((1, rows), jnp.int32)
        for k in range(routes.shape[0]):
            named += (routes[k : k + 1] == idx[5] + 2 * z).astype(jnp.int32)
        bit = bit ^ named
        gray = gray * 2 + bit
    across = jnp.broadcast_to(gray.astype(f32), (rows, rows))
    first, second = iota((rows, rows), 0), iota((rows, rows), 1)
    top = jnp.where(first[:8] == 0, across[:8], 0.0).astype(bf16)
    down = contract(top, jnp.ones((8, rows), bf16), 0, 0)
    ahead = (down < across) | ((down == across) & (first < second))
    rank = jnp.sum(ahead.astype(f32), axis=0, keepdims=True).astype(jnp.int32)
    target = rank % len(chunks) * size + rank // len(chunks)
    order = (first == target).astype(bf16)
    order_out[...] = order
    ext = dot32(order, ext).astype(bf16)
    for q, chunk in enumerate(chunks):
        chunk[:, width:] = ext[q * size : (q + 1) * size]
    fetch.wait()
    step = 1024
    for n in range(0, width, step):
        moved = dot32(order, held[:, n : n + step]).astype(bf16)
        for q, chunk in enumerate(chunks):
            chunk[:, n : n + step] = moved[q * size : (q + 1) * size]


def pick_kernel(experts, mode, idx, *refs):
    *blocks, own_out, cross_out, pick_out = refs
    total = blocks[0].shape[1]
    rows = blocks[0].shape[0] * (len(blocks) if mode == "both" else 1)
    own_rows, cross_rows = own_out.shape[0], cross_out.shape[0]
    inner = idx[3] == 1

    def load(cols):
        if mode == "both":
            return jnp.concatenate([b[:, cols] for b in blocks], 0)
        if mode == "either":
            return jnp.where(inner, blocks[0][:, cols], blocks[1][:, cols])
        return blocks[0][:, cols]

    ext = load(slice(total - LANES, total))

    def picks(expert, count):
        mask = jnp.broadcast_to(scale_of(ext, expert, experts) > 0, (rows, LANES)).astype(jnp.bfloat16)
        upto = (iota((rows, rows), 0) <= iota((rows, rows), 1)).astype(jnp.bfloat16)
        place = contract(mask, upto, 0, 0)[:count]
        named = contract(mask, eye(rows), 0, 0)[:count]
        slot = iota((count, rows), 0).astype(jnp.float32)
        return ((named > 0.5) & (place - 1.0 == slot)).astype(jnp.float32)

    own = picks(idx[1], own_rows) if mode == "both" else eye(rows).astype(jnp.float32)
    pick = jnp.concatenate([own, picks(idx[2], cross_rows)], 0).astype(jnp.bfloat16)
    pick_out[...] = pick
    step = total // 3
    for n in range(0, total, step):
        got = dot32(pick, load(slice(n, n + step)))
        own_out[:, n : n + step] = got[:own_rows].astype(jnp.bfloat16)
        cross_out[:, n : n + step] = got[own_rows:].astype(jnp.bfloat16)


def expert_kernel(experts, idx, own, cross, ga, gb, ua, ub, da, db, own_out, cross_out, hidden):
    own_rows, total = own.shape
    width = total - LANES
    core, expert = idx[0], idx[1]
    half = ga.shape[0]
    x = jnp.concatenate([own[:, :width], cross[:, :width]], 0)
    ext = jnp.concatenate([own[:, width:], cross[:, width:]], 0)
    lane = iota((8, LANES), 1)
    mine = ((lane % experts == expert) & (lane < 3 * experts)).astype(jnp.bfloat16)
    scale = contract(mine, ext, 1, 1)[:1]
    for place, g, u in ((core, ga, ua), (1 - core, gb, ub)):
        gate = contract(g[...], x, 1, 1)
        upval = contract(u[...], x, 1, 1)
        made = gate / (1.0 + jnp.exp(-gate)) * upval * scale
        hidden[place] = made.T.astype(jnp.bfloat16)
    step = 512
    cols = da.shape[1]
    for n in range(0, 2 * cols, step):
        d, m = (da, n) if n < cols else (db, n - cols)
        made = dot32(hidden[0], d[:half, m : m + step]) + dot32(hidden[1], d[half:, m : m + step])
        own_out[:, n : n + step] = made[:own_rows].astype(jnp.bfloat16)
        cross_out[:, n : n + step] = made[own_rows:].astype(jnp.bfloat16)


def combine_kernel(first, idx, pick, own, cross, *refs):
    *more, out = refs
    width = own.shape[1]
    rows = slice(first, first + out.shape[0])
    step = 1024
    for n in range(0, width, step):
        cols = slice(n, n + step)
        got = contract(pick[...], jnp.concatenate([own[:, cols], cross[:, cols]], 0), 0, 0)[rows]
        for ref in more:
            got += ref[:, cols].astype(jnp.float32)
        out[:, cols] = got.astype(jnp.bfloat16)


def finish_kernel(idx, order, pick, own, cross, *refs):
    *more, out, held, sems = refs
    width = own.shape[1]
    step = 1024
    copies = []
    for i, n in enumerate(range(0, width, step)):
        cols = slice(n, n + step)
        got = contract(pick[...], jnp.concatenate([own[:, cols], cross[:, cols]], 0), 0, 0)
        sums = [sum(r[:, cols].astype(jnp.float32) for r in part) for part in (more[::2], more[1::2])]
        got = (got + jnp.concatenate(sums, 0)).astype(jnp.bfloat16)
        held[i] = contract(order[...], got, 0, 0).astype(jnp.bfloat16)
        to = pl.ds(pl.multiple_of((idx[4] + n) % width, step), step)
        copies.append(pltpu.make_async_copy(held.at[i], out.at[:, to], sems.at[i]))
        copies[-1].start()
    for c in copies:
        c.wait()


def fence_kernel(idx):
    pass


def run_copies(sems, pairs):
    copies = [pltpu.make_async_copy(s, d, sems.at[i]) for i, (s, d) in enumerate(pairs)]
    for c in copies:
        c.start()
    for c in copies:
        c.wait()


def fetch_kernel(idx, *refs):
    count = len(refs) // 2
    run_copies(refs[-1], zip(refs[:count], refs[count:-1]))


def call(name, kernel, outs, idx, token, args, passes=(), scratch=(), cost=1, left=(), away=False):
    vmem, anywhere = pl.BlockSpec(memory_space=pltpu.VMEM), pl.BlockSpec(memory_space=pl.ANY)
    through = [token, *passes]
    first = 1 + len(args) + len(left)

    def body(*refs):
        ins, rest = refs[:first], refs[first + len(through) :]
        kernel(*ins, *rest[: len(outs)], *rest[len(outs) + len(through) :])

    got = pl.pallas_call(
        body,
        out_shape=[*outs, *(jax.ShapeDtypeStruct(x.shape, x.dtype) for x in through)],
        in_specs=[pl.BlockSpec(memory_space=pltpu.SMEM)]
        + [vmem] * len(args)
        + [anywhere] * len(left)
        + [anywhere] * len(through),
        out_specs=[anywhere if away else vmem] * len(outs) + [anywhere] * len(through),
        input_output_aliases={first + i: len(outs) + i for i in range(len(through))},
        scratch_shapes=list(scratch),
        name=name,
        compiler_params=pltpu.CompilerParams(vmem_limit_bytes=LIMIT),
        cost_estimate=pl.CostEstimate(flops=1, bytes_accessed=cost, transcendentals=0),
    )(idx, *args, *left, *through)
    return got[: len(outs)], got[len(outs)], got[len(outs) + 1 :]


ORDER = [
    ["prep", "EA", "MB", "EB"],
    ["P0", "NA", "Y0"],
    ["f", "OB", "+wg", "+wu"],
    ["W"],
    ["f", "MA"],
    ["P1", "Y1", "QA"],
    ["P2B", "Y2B", "NB"],
    ["F0", "OA"],
    ["P3A", "Y3A", "+Y1"],
    ["F2B", "R2B"],
    ["f", "QB", "+Y3A"],
    ["P2A"],
    ["f", "Y2A"],
    ["F3A"],
    ["C2B", "I2B"],
    ["P3B", "Y3B", "+Y2A"],
    ["F1", "R3A"],
    ["F3B", "+I2B"],
    ["D2B", "R3B"],
    ["C3A", "I3A", "S2B", "R1"],
    ["F2A"],
    ["C3B", "I3B", "R2A", "+R3A"],
    ["D3A", "S3A"],
    ["C2A", "I2A", "+S2B", "+R1"],
    ["D3B", "S3B", "+R2A"],
    ["D1A", "S1A", "R0"],
    ["D2A"],
    ["D1B", "S2A", "S1B", "+I2A"],
    ["fin"],
]


def lined(tokens, routes, route_weights, gate_weight, up_weight, down_weight):
    tok_rows, top_count = routes.shape
    width = tokens.shape[1]
    devices = lax.axis_size("expert")
    experts = devices // 2
    capacity = tok_rows * top_count // experts
    half = gate_weight.shape[1]
    index = lax.axis_index("expert")
    core, side, line = index % 2, index // 2 % 2, index // 4
    inner = ((line == 1) | (line == 2)).astype(jnp.int32)
    idx = jnp.stack(
        [core, 2 * line + side, 2 * line + 1 - side, inner, core * down_weight.shape[1], 1 - side]
    ).astype(jnp.int32)
    rows = tok_rows // 2
    total = width + LANES
    bf16 = jnp.bfloat16

    def in_hbm(x):
        return pltpu.with_memory_space_constraint(x, pltpu.HBM)

    def like(*shape):
        return jax.ShapeDtypeStruct(shape, bf16)

    gate, up = gate_weight.T, up_weight.T

    val = {}
    for name, w in (("wg", gate), ("wu", up), ("wd", down_weight)):
        with jax.named_scope("move_" + name):
            val[name] = swapped(w, "expert", 0)
    steps = {name for name, *_ in ORDER}
    slots = {name[1:] for name in steps if name[0] == "P"}

    def kernel_of(name):
        kind, q = name[:-1], name[-1]
        if name == "prep":
            return (
                functools.partial(prepare_kernel, experts),
                [like(rows, total), like(rows, total), like(tok_rows, tok_rows)],
                [in_hbm(routes.T), in_hbm(route_weights.T)],
                [pltpu.VMEM(tokens.shape, bf16), pltpu.SemaphoreType.DMA],
            )
        if name[0] == "P":
            slot = name[1:]
            if slot in ("0", "1"):
                blocks, mode = [["payA", "payB"], ["EA", "EB"]][int(slot)], "both"
                own, cross, size = capacity, capacity, tok_rows
            else:
                blocks = {"1": ["E" + q], "2": ["M" + q, "O" + q], "3": ["N" + q, "Q" + q]}[slot[0]]
                mode = "one" if len(blocks) == 1 else "either"
                own, cross, size = rows, CROSS_ROWS, rows
            return (
                functools.partial(pick_kernel, experts, mode),
                [like(own, total), like(cross, total), like(own + cross, size)],
                [val[b] for b in blocks],
                [],
            )
        if name[0] == "F":
            own, cross = val["own" + name[1:]], val["Y" + name[1:]]
            weights = [gate, val["vg"], up, val["vu"], down_weight, val["vd"]]
            weights = [pltpu.with_memory_space_constraint(w, pltpu.VMEM) for w in weights]
            args = [own, cross, *weights]
            return (
                functools.partial(expert_kernel, experts),
                [like(own.shape[0], width), like(cross.shape[0], width)],
                args,
                [pltpu.VMEM((2, own.shape[0] + cross.shape[0], half), bf16)],
            )
        if name == "W":
            outs = [pltpu.VMEM(w.shape, bf16) for w in (gate, up, down_weight)]
            return fetch_kernel, outs, [], [pltpu.SemaphoreType.DMA((3,))]
        if name == "fin":
            made = [val["order"], val["pick0"], val["made0"], val["R0"]]
            made += [val[s + q] for s in ("S1", "S2") for q in "AB"]
            parts = width // 1024
            scratch = [pltpu.VMEM((parts, tok_rows, 1024), bf16), pltpu.SemaphoreType.DMA((parts,))]
            return finish_kernel, [like(tok_rows, width)], made, scratch
        slot = name[1:] if name[1:] in slots else name[1]
        made = [val[s + slot] for s in ("pick", "made", "R")]
        made += [val[x] for x in {"D2": ["I2" + q], "D3": ["I3" + q], "D1": ["S3" + q]}.get(kind, [])]
        first = rows if slot == name[1] and q == "B" else 0
        return functools.partial(combine_kernel, first), [like(rows, width)], made, []

    def keep(name, got):
        slot = name[1:]
        if name == "prep":
            val["payA"], val["payB"], val["order"] = got
        elif name[0] == "P":
            val["own" + slot], val["cross" + slot], val["pick" + slot] = got
        elif name == "W":
            val["vg"], val["vu"], val["vd"] = got
        elif name[0] == "F":
            val["made" + slot], val["back" + slot] = got
        else:
            val[name] = got[0]

    def move_of(name):
        kind, slot, q = name[0], name[1:], name[-1]
        if kind == "Y":
            return "cross" + slot, lambda x: swapped(x, "expert", 1)
        if kind == "R":
            return "back" + slot, lambda x: swapped(x, "expert", 1)
        source, pairs = {
            "E": ("pay" + q, OUTER),
            "M": ("pay" + q, MIDDLE),
            "O": ("M" + q, OUT),
            "N": ("E" + q, MIDDLE),
            "Q": ("N" + q, OUT),
            "I2": ("C2" + q, IN),
            "S2": ("D2" + q, MIDDLE),
            "X3": ("C3" + q, ENDS),
            "I3": ("C3" + q, IN),
            "S3": (("D3" if "D3" + q in steps else "C3") + q, MIDDLE),
            "S1": ("D1" + q, OUTER),
        }[name[:-1]]
        return source, lambda x: along_line(x, pairs)

    token = jnp.zeros((8, LANES), jnp.float32)
    for name, *moves in ORDER:
        done = [m[1:] for m in moves if m[0] == "+"]
        moves = [m for m in moves if m[0] != "+"]
        sources = {m: move_of(m)[0] for m in moves}
        passed = sorted({s for s in [*sources.values(), *done] if s in val})
        if name == "f":
            _, token, through = call("fence", fence_kernel, [], idx, token, [], passes=[val[s] for s in passed])
        else:
            kernel, outs, args, scratch = kernel_of(name)
            cost = sum(x.size * x.dtype.itemsize for x in [*args, *outs]) if name[0] == "F" else 1
            through = [val[s] for s in passed]
            left = {"prep": [in_hbm(tokens)], "W": [val["wg"], val["wu"], val["wd"]]}.get(name, [])
            got, token, through = call(name, kernel, outs, idx, token, args, through, scratch, cost, left, name == "fin")
            keep(name, got)
        val.update(zip(passed, through))
        for m in moves:
            with jax.named_scope("move_" + m):
                val[m] = move_of(m)[1](val[sources[m]])
    return val["fin"]


def solution(mesh):
    body = lined if mesh.shape["expert"] == 16 else dispatched
    return jax.shard_map(
        body,
        mesh=mesh,
        in_specs=(
            P(("groups", "expert"), None),
            P(("groups", "expert"), None),
            P(("groups", "expert"), None),
            P(None, "expert"),
            P(None, "expert"),
            P(None, "expert"),
        ),
        out_specs=P(("groups", "expert"), None),
        check_vma=False,
    )
```
